256 devices in a mesh: dp: 4 (over z_lo, core), space: 64 (over z_hi, y, x).
Axes of the slice: x: 4, y: 4, z: 8 (z_hi: 4, z_lo: 2; z = z_hi * 2 + z_lo), core: 2. Of those that a mesh axis runs over, the one named last changes fastest.
Arguments:
- field_in: bfloat16 [4, 64, 128, 128, 128], P('dp', None, 'space'), may hold values from -6 to 6
- cotangent: bfloat16 [4, 64, 128, 128, 128], P('dp', None, 'space'), may hold values from -6 to 6
- spectral_one: bfloat16 [2, 16, 256, 64, 64], P(None, None, 'space'), may hold values from -3 to 3
- spectral_two: bfloat16 [2, 16, 256, 64, 64], P(None, None, 'space'), may hold values from -3 to 3
- point_one: bfloat16 [64, 64], replicated, may hold values from -0.75 to 0.75
- point_two: bfloat16 [64, 64], replicated, may hold values from -0.75 to 0.75
- bias_one: float32 [64], replicated, may hold values from -3 to 3
- bias_two: float32 [64], replicated, may hold values from -3 to 3
Outputs:
- spectral_grad_one: bfloat16 [2, 16, 256, 64, 64], P(None, None, 'space')
- spectral_grad_two: bfloat16 [2, 16, 256, 64, 64], P(None, None, 'space')
- point_grad_one: float32 [64, 64], replicated
- point_grad_two: float32 [64, 64], replicated
- bias_grad_one: float32 [64], replicated
- bias_grad_two: float32 [64], replicated
The draws below stay inside these ranges and needn't reach their ends.
All inputs are finite; a program needn't handle non-finite values.
Results may differ from the reference program's by a relative error of at most 0.035.
Values may be sent and summed in bfloat16 or wider, within the bound.
No kernel may reach another device: no remote copies, remote signals or barrier semaphores. Data moves between devices by JAX's collectives and lax.ppermute only.
A program may use at most 128 MiB of HBM per device.

```python
import math
import jax
import jax.numpy as jnp
from jax import lax

C = 64
Y = 128
Z = 128
MX = 16
MY = 16
MZ = 16
X = 128
SAMPLES = 4
N_DP = 4


def level_of(stream_key, shape, cuts, low, high):
    def one(position, shards_of):
        heights = jax.random.uniform(jax.random.fold_in(jax.random.fold_in(stream_key, 6), position), (shards_of,), jnp.float32, low / len(cuts), high / len(cuts))
        return jnp.repeat(jnp.exp(heights), shape[position] // shards_of).reshape((-1,) + (1,) * (len(shape) - position - 1))

    level = one(*cuts[0])
    for cut in cuts[1:]:
        level = level * one(*cut)
    return level


def centred(rng, dims, spread, bound, split=(), kind=jnp.bfloat16):
    result = jax.random.normal(rng, dims, jnp.float32) * spread
    if len(split) > 0:
        result = level_of(rng, dims, split, -0.22, 0.18) * result
    return jnp.clip(result, min=-bound, max=bound).astype(kind)


def setup_inputs(seed: int = 0) -> dict:
    key_list = jax.random.split(jax.random.key(seed), 9)
    field_in = centred(key_list[0], (SAMPLES, C, X, Y, Z), 1.0, 6.0, ((0, 4), (2, 64)))
    cotangent = centred(key_list[1], (SAMPLES, C, X, Y, Z), 1.0, 6.0, ((0, 4), (2, 64)))
    spectral_one = centred(key_list[2], (2, MX, MY * MZ, C, C), 0.5, 3.0, ((2, 64),))
    spectral_two = centred(key_list[3], (2, MX, MY * MZ, C, C), 0.5, 3.0, ((2, 64),))
    point_one = centred(key_list[4], (C, C), C ** -0.5, 0.75)
    point_two = centred(key_list[5], (C, C), C ** -0.5, 0.75)
    bias_one = centred(key_list[6], (C,), 0.5, 3.0, (), jnp.float32)
    bias_two = centred(key_list[7], (C,), 0.5, 3.0, (), jnp.float32)
    return {"field_in": field_in, "cotangent": cotangent, "spectral_one": spectral_one, "spectral_two": spectral_two, "point_one": point_one, "point_two": point_two, "bias_one": bias_one, "bias_two": bias_two}


root_coef = math.sqrt(2.0 / math.pi)

def angles(length, modes, two_sided):
    places = jnp.arange(length, dtype=jnp.int32)[:, None]
    orders = jnp.arange(modes, dtype=jnp.int32)[None, :]
    if two_sided:
        orders = jnp.where(orders < modes // 2, orders, orders - modes + length)
    phases = places * orders % length
    return 2.0 * math.pi / length * phases.astype(jnp.float32)

def complex_tables(length, modes):
    radians = angles(length, modes, True)
    factor = 1.0 / math.sqrt(length)
    cosines = jnp.cos(radians) * factor
    sine_table = jnp.sin(radians) * factor
    forward = jnp.stack([jnp.stack([cosines, -sine_table], axis=1), jnp.stack([sine_table, cosines], axis=1)], axis=0)
    cosine_rows = cosines.T
    sine_rows = sine_table.T
    inverse = jnp.stack([jnp.stack([cosine_rows, sine_rows], axis=1), jnp.stack([-sine_rows, cosine_rows], axis=1)], axis=0)
    return (forward.astype(jnp.bfloat16), inverse.astype(jnp.bfloat16))

def real_tables(length, modes):
    radians = angles(length, modes, False)
    factor = 1.0 / math.sqrt(length)
    cosines = jnp.cos(radians) * factor
    sine_table = jnp.sin(radians) * factor
    forward = jnp.concatenate([cosines, -sine_table], axis=1)
    doubled = jnp.where(jnp.arange(modes, dtype=jnp.int32) == 0, jnp.float32(1.0), jnp.float32(2.0))[None, :]
    inverse = jnp.concatenate([(cosines * doubled).T, (-sine_table * doubled).T], axis=0)
    return (forward.astype(jnp.bfloat16), inverse.astype(jnp.bfloat16))

def flipped(table):
    return jnp.transpose(table, (2, 3, 0, 1))

def gelu_slope(preact):
    inner = root_coef * (preact + 0.044715 * preact * preact * preact)
    tangent = jnp.tanh(inner)
    return 0.5 * (1.0 + tangent) + 0.5 * preact * (1.0 - tangent * tangent) * root_coef * (1.0 + 3.0 * 0.044715 * preact * preact)

def product(form, left, right):
    return jnp.einsum(form, left.astype(jnp.float32), right.astype(jnp.float32), precision=lax.Precision.HIGHEST)

def partial_spectrum(values, table_third, table_second):
    channels, planes, grid_second = (values.shape[0], values.shape[1], values.shape[2])
    modes_third = table_third.shape[1] // 2
    modes_second = table_second.shape[3]
    third_done = product('cxyz,zj->cxjy', values, table_third).astype(jnp.bfloat16)
    third_done = third_done.reshape(channels, planes, 2, modes_third, grid_second)
    second_done = product('cxrky,rysm->cxskm', third_done, table_second).astype(jnp.bfloat16)
    return second_done.reshape(channels, planes, 2, modes_third * modes_second)

def partial_field(values, table_second, table_third):
    channels, planes = (values.shape[0], values.shape[1])
    modes_second = table_second.shape[1]
    modes_third = table_third.shape[0] // 2
    grid_second = table_second.shape[3]
    unfolded = values.reshape(channels, planes, 2, modes_third, modes_second)
    second_done = product('cxskm,smry->cxrky', unfolded, table_second).astype(jnp.bfloat16)
    second_done = second_done.reshape(channels, planes, 2 * modes_third, grid_second)
    return product('cxjy,jz->cxyz', second_done, table_third)

def first_spectrum(values, table_first):
    return product('cxrp,rxsm->smpc', values, table_first).astype(jnp.bfloat16)

def first_field(spectrum, table_first):
    return product('smpc,smrx->cxrp', spectrum, table_first).astype(jnp.bfloat16)

def mix_modes(spectrum, weights):
    products = product('smpc,tmpco->stmpo', spectrum, weights)
    return jnp.stack([products[0, 0] - products[1, 1], products[0, 1] + products[1, 0]]).astype(jnp.bfloat16)

def unmix_modes(gspectrum, weights):
    products = product('tmpco,smpo->tsmpc', weights, gspectrum)
    return jnp.stack([products[0, 0] + products[1, 1], products[0, 1] - products[1, 0]]).astype(jnp.bfloat16)

def weight_term(spectrum, gspectrum):
    products = product('smpc,tmpo->stmpco', spectrum, gspectrum)
    return jnp.stack([products[0, 0] + products[1, 1], products[0, 1] - products[1, 0]])

def reference(field_in, cotangent, spectral_one, spectral_two, point_one, point_two, bias_one, bias_two):
    forward_first, inverse_first = complex_tables(X, MX)
    forward_second, inverse_second = complex_tables(Y, MY)
    forward_third, inverse_third = real_tables(Z, MZ)

    def to_spectrum(values, table_third, table_second, table_first):
        return first_spectrum(partial_spectrum(values, table_third, table_second), table_first)

    def to_field(spectrum, table_first, table_second, table_third):
        return partial_field(first_field(spectrum, table_first), table_second, table_third)

    def layer_forward(values, weights, point, bias):
        spectrum = to_spectrum(values, forward_third, forward_second, forward_first)
        branch = to_field(mix_modes(spectrum, weights), inverse_first, inverse_second, inverse_third)
        preact = product('cxyz,co->oxyz', values, point) + bias[:, None, None, None] + branch
        return (spectrum, preact)

    def adjoint_spectrum(grads):
        return to_spectrum(grads, inverse_third.T, flipped(inverse_second), flipped(inverse_first))

    def adjoint_field(gspectrum):
        return to_field(gspectrum, flipped(forward_first), flipped(forward_second), forward_third.T)

    def per_sample(totals, inputs):
        values, grad_out = inputs
        spec_one, pre_one = layer_forward(values, spectral_one, point_one, bias_one)
        hidden = jax.nn.gelu(pre_one, approximate=True).astype(jnp.bfloat16)
        spec_two, pre_two = layer_forward(hidden, spectral_two, point_two, bias_two)
        grad_two = (grad_out.astype(jnp.float32) * gelu_slope(pre_two)).astype(jnp.bfloat16)
        gspec_two = adjoint_spectrum(grad_two)
        returned = adjoint_field(unmix_modes(gspec_two, spectral_two))
        grad_hidden = product('oxyz,co->cxyz', grad_two, point_two) + returned
        grad_one = (grad_hidden * gelu_slope(pre_one)).astype(jnp.bfloat16)
        gspec_one = adjoint_spectrum(grad_one)
        updated = (totals[0] + weight_term(spec_one, gspec_one), totals[1] + weight_term(spec_two, gspec_two), totals[2] + product('cxyz,oxyz->co', values, grad_one), totals[3] + product('cxyz,oxyz->co', hidden, grad_two), totals[4] + lax.optimization_barrier(jnp.sum(grad_one.astype(jnp.float32), axis=(1, 2, 3))), totals[5] + lax.optimization_barrier(jnp.sum(grad_two.astype(jnp.float32), axis=(1, 2, 3))))
        return (updated, None)
    spectral_zero = jnp.zeros(spectral_one.shape, jnp.float32)
    point_zero = jnp.zeros((C, C), jnp.float32)
    bias_zero = jnp.zeros((C,), jnp.float32)
    initial = (spectral_zero, spectral_zero, point_zero, point_zero, bias_zero, bias_zero)
    totals, _ = lax.scan(per_sample, initial, (field_in, cotangent))
    factor = 1.0 / math.sqrt(N_DP * X * Y * Z)
    return (totals[0].astype(jnp.bfloat16), totals[1].astype(jnp.bfloat16), totals[2] * factor, totals[3] * factor, totals[4] * factor, totals[5] * factor)
```

```python
import functools
import math

import jax
import jax.numpy as jnp
import numpy as np
from jax import lax
from jax.experimental import pallas as pl
from jax.experimental.pallas import tpu as pltpu
from jax.sharding import PartitionSpec as P

MY = 16
MZ = 16
CHANNELS = 64
LANES = 128
ROOT = math.sqrt(2.0 / math.pi)
CUBIC = 0.044715
F32 = jnp.float32
BF16 = jnp.bfloat16
VMEM_LIMIT = 44 * 1024 * 1024


def angles(length, modes, two_sided):
    places = np.arange(length, dtype=np.int64)[:, None]
    orders = np.arange(modes, dtype=np.int64)[None, :]
    if two_sided:
        orders = np.where(orders < modes // 2, orders, orders - modes + length)
    phases = places * orders % length
    return np.float32(2.0 * math.pi / length) * phases.astype(np.float32)


def complex_tables(length, modes):
    radians = angles(length, modes, True)
    factor = np.float32(1.0 / math.sqrt(length))
    cosines = np.cos(radians) * factor
    sines = np.sin(radians) * factor
    forward = np.stack(
        [np.stack([cosines, -sines], axis=1), np.stack([sines, cosines], axis=1)], axis=0
    )
    inverse = np.stack(
        [np.stack([cosines.T, sines.T], axis=1), np.stack([-sines.T, cosines.T], axis=1)], axis=0
    )
    return forward.astype(BF16), inverse.astype(BF16)


def real_tables(length, modes):
    radians = angles(length, modes, False)
    factor = np.float32(1.0 / math.sqrt(length))
    cosines = np.cos(radians) * factor
    sines = np.sin(radians) * factor
    forward = np.concatenate([cosines, -sines], axis=1)
    doubled = np.where(np.arange(modes) == 0, 1.0, 2.0).astype(np.float32)[None, :]
    inverse = np.concatenate([(cosines * doubled).T, (-sines * doubled).T], axis=0)
    return forward.astype(BF16), inverse.astype(BF16)


def flipped(table):
    return np.transpose(table, (2, 3, 0, 1))


def second_natural(table):
    length = table.shape[1]
    split = table.reshape(2, length, 2, MY // 4, 4)
    return split.transpose(3, 2, 4, 0, 1).reshape(2 * MY, 2 * length)


def second_paired(table):
    length = table.shape[1]
    split = table.reshape(2, length // 2, 2, 2, MY // 4, 4)
    return split.transpose(2, 4, 3, 5, 0, 1).reshape(4 * MY, length)


def second_inverse(table):
    length = table.shape[3]
    split = table.reshape(2, MY // 4, 4, 2, length // 2, 2)
    return split.transpose(3, 4, 5, 1, 0, 2).reshape(length, 4 * MY)


def first_forward(table):
    length, modes = table.shape[1], table.shape[3]
    split = table.reshape(2, length // 2, 2, 2, modes)
    return split.transpose(2, 3, 4, 0, 1).reshape(4 * modes, length)


def first_inverse(table):
    modes, length = table.shape[1], table.shape[3]
    split = table.reshape(2, modes, 2, length // 2, 2)
    return split.transpose(2, 3, 4, 0, 1).reshape(length, 4 * modes)


def twice_diagonal(table):
    zero = np.zeros_like(table)
    return np.block([[table, zero], [zero, table]])


def mm(left, right):
    return lax.dot_general(left, right, (((1,), (0,)), ((), ())), preferred_element_type=F32)


def nt(left, right):
    return lax.dot_general(left, right, (((1,), (1,)), ((), ())), preferred_element_type=F32)


def tn(left, right):
    return lax.dot_general(left, right, (((0,), (0,)), ((), ())), preferred_element_type=F32)


def side(rows):
    return lax.broadcasted_iota(jnp.int32, (rows, LANES), 1) < LANES // 2


def turned(values):
    return pltpu.roll(values, LANES // 2, 1)


def whole(shape):
    return pl.BlockSpec(shape, lambda *_: (0,) * len(shape))


VM = pl.BlockSpec(memory_space=pltpu.VMEM)


GROUPS = 8
ROWS = 2 * LANES * CHANNELS


def near(value):
    return pltpu.with_memory_space_constraint(value, pltpu.VMEM)


def call(
    kernel, outs, scratch, flops, moved, *operands, big=(), kinds=(), plain=(), token=None
):
    cut = ROWS // GROUPS
    counts = [
        len(operands),
        len(big),
        0 if token is None else 1,
        len(outs),
        len(kinds),
        len(plain),
        len(scratch),
        len(outs),
        len(big),
        len(kinds),
        3,
    ]

    def whole_kernel(*refs):
        parts = []
        at = 0
        for count in counts:
            parts.append(refs[at : at + count])
            at += count
        small, big_far, _, outs_far, kinds_far, plains, own, outs_near, big_near, kinds_near, sems = parts
        in_sem, out_sem, end_sem = sems

        def group_of(far, close, sem, index, group, out):
            rows = pl.ds(pl.multiple_of(group * cut, cut), cut)
            pair = (close.at[rows], far.at[rows]) if out else (far.at[rows], close.at[rows])
            return pltpu.make_async_copy(*pair, sem.at[index, group])

        def coming(index, group):
            return group_of(big_far[index], big_near[index], in_sem, index, group, False)

        def going(index, group):
            return group_of(kinds_far[index], kinds_near[index], out_sem, index, group, True)

        for group in range(GROUPS):
            for index in range(len(big)):
                coming(index, group).start()

        def loop(body, carry=0, unroll=4):
            per = PAIRS // GROUPS

            def some(i, carry):
                for j in range(unroll):
                    carry = body(i * unroll + j, carry)
                return carry

            def each(group, carry):
                for index in range(len(big)):
                    coming(index, group).wait()
                first = group * (per // unroll)
                carry = lax.fori_loop(first, first + per // unroll, some, carry)
                for index in range(len(kinds)):
                    going(index, group).start()
                return carry

            return lax.fori_loop(0, GROUPS, each, carry)

        kernel(small, big_near, outs_near, kinds_near, plains, own, loop)
        last = [
            pltpu.make_async_copy(close, far, end_sem.at[index])
            for index, (close, far) in enumerate(zip(outs_near, outs_far))
        ]
        for copy in last:
            copy.start()
        for index in range(len(kinds)):
            for group in range(GROUPS):
                going(index, group).wait()
        for copy in last:
            copy.wait()

    operands = [near(operand) for operand in operands]
    far = pl.BlockSpec(memory_space=pl.ANY)
    extra = [] if token is None else [token]
    shapes = [pltpu.HBM(shape, kind) for shape, kind in outs]
    shapes += [pltpu.HBM((ROWS, LANES), kind) for kind in kinds]
    return pl.pallas_call(
        whole_kernel,
        out_shape=shapes + list(plain),
        in_specs=[VM] * len(operands) + [far] * (len(big) + len(extra)),
        out_specs=[far] * len(shapes) + [VM] * len(plain),
        scratch_shapes=list(scratch)
        + [pltpu.VMEM(shape, kind) for shape, kind in outs]
        + [pltpu.VMEM((ROWS, LANES), array.dtype) for array in big]
        + [pltpu.VMEM((ROWS, LANES), kind) for kind in kinds]
        + [
            pltpu.SemaphoreType.DMA((max(len(big), 1), GROUPS)),
            pltpu.SemaphoreType.DMA((max(len(kinds), 1), GROUPS)),
            pltpu.SemaphoreType.DMA((max(len(outs), 1),)),
        ],
        cost_estimate=pl.CostEstimate(flops=flops, bytes_accessed=moved, transcendentals=0),
        compiler_params=pltpu.CompilerParams(vmem_limit_bytes=VMEM_LIMIT),
    )(*operands, *big, *extra)


C_STEP = 8


def spectrum_kernel(field, third_far, second_far, out_far, near_field, third_ref, second_ref, chunk, spec, sems, extra):
    def coming(step):
        cut = pl.ds(step * C_STEP, C_STEP)
        return pltpu.make_async_copy(field.at[0, cut], near_field.at[cut], sems.at[step])

    tables = [
        pltpu.make_async_copy(third_far, third_ref, extra.at[0]),
        pltpu.make_async_copy(second_far, second_ref, extra.at[1]),
    ]
    for copy in tables:
        copy.start()
    for step in range(CHANNELS // C_STEP):
        coming(step).start()
    for copy in tables:
        copy.wait()
    third = third_ref[...]

    def some(step, carry):
        coming(step).wait()
        for x in range(2):
            rows = near_field[pl.ds(step * C_STEP, C_STEP), x].reshape(C_STEP * LANES, LANES)
            done = nt(third, rows)
            for c in range(C_STEP):
                place = pl.multiple_of((x * CHANNELS + step * C_STEP + c) * 2 * MZ, 2 * MZ)
                spec[pl.ds(place, 2 * MZ), :] = done[:, c * LANES : (c + 1) * LANES]
        return carry

    lax.fori_loop(0, CHANNELS // C_STEP, some, 0)
    second = second_ref[...]
    for k in range(MZ):
        real = spec[pl.ds(k, LANES, stride=2 * MZ), :]
        imag = spec[pl.ds(MZ + k, LANES, stride=2 * MZ), :]
        both = jnp.concatenate([real, imag], axis=1).astype(BF16)
        chunk[k * 32 : (k + 1) * 32, :] = nt(second, both).astype(BF16)
    out = pltpu.make_async_copy(chunk, out_far, extra.at[2])
    out.start()
    out.wait()


def first_partial(field, third, second):
    far = pl.BlockSpec(memory_space=pl.ANY)
    return pl.pallas_call(
        spectrum_kernel,
        out_shape=pltpu.HBM((512, LANES), BF16),
        in_specs=[far] * 3,
        out_specs=far,
        scratch_shapes=[
            pltpu.VMEM(field.shape[1:], BF16),
            pltpu.VMEM(third.shape, BF16),
            pltpu.VMEM(second.shape, BF16),
            pltpu.VMEM((512, LANES), BF16),
            pltpu.VMEM((4096, LANES), F32),
            pltpu.SemaphoreType.DMA((CHANNELS // C_STEP,)),
            pltpu.SemaphoreType.DMA((3,)),
        ],
        cost_estimate=pl.CostEstimate(
            flops=600_000_000, bytes_accessed=6 << 20, transcendentals=0
        ),
        compiler_params=pltpu.CompilerParams(vmem_limit_bytes=VMEM_LIMIT),
    )(field, third, second)


Y_STEP = 16
Y_STEPS = LANES // Y_STEP
Y_ROWS = Y_STEP * CHANNELS


def relay_kernel(pointed, *refs):
    if pointed:
        point_ref, bias_ref = refs[:2]
        refs = refs[2:]
    outs = 2 if pointed else 1
    field = refs[0]
    out_far = refs[2 : 2 + outs]
    near_field = refs[2 + outs]
    out_near = refs[3 + outs : 3 + 2 * outs]
    rows_ref, in_sem, out_sem = refs[3 + 2 * outs :]

    def coming(step):
        x = step // Y_STEPS
        cut = pl.ds(pl.multiple_of((step % Y_STEPS) * Y_STEP, Y_STEP), Y_STEP)
        return pltpu.make_async_copy(
            field.at[0, :, x, cut], near_field.at[:, x, cut], in_sem.at[step]
        )

    def going(index, step):
        cut = pl.ds(pl.multiple_of(step * Y_ROWS, Y_ROWS), Y_ROWS)
        return pltpu.make_async_copy(
            out_near[index].at[cut], out_far[index].at[cut], out_sem.at[index, step]
        )

    for step in range(2 * Y_STEPS):
        coming(step).start()
    if pointed:
        point = point_ref[...]
        shift = jnp.concatenate([bias_ref[...], bias_ref[...]], axis=1)

    def some(step, carry):
        coming(step).wait()
        at = pl.multiple_of((step % Y_STEPS) * Y_STEP, Y_STEP)
        rows_ref[...] = (
            near_field[:, step // Y_STEPS, pl.ds(at, Y_STEP), :].astype(F32).reshape(Y_ROWS, LANES)
        )
        for y in range(0, Y_STEP, 2):
            pair = [rows_ref[pl.ds(y + e, CHANNELS, stride=Y_STEP), :] for e in range(2)]
            tile = step * (Y_STEP // 2) + y // 2
            out_near[0][tile_at(tile), :] = jnp.concatenate(pair, axis=0).astype(BF16)
            if pointed:
                wide = jnp.concatenate(pair, axis=1).astype(BF16)
                store_wide(out_near[1], tile, mm(point, wide) + shift)
        for index in range(outs):
            going(index, step).start()
        return carry

    lax.fori_loop(0, 2 * Y_STEPS, some, 0)
    for step in range(2 * Y_STEPS):
        for index in range(outs):
            going(index, step).wait()


def relay(field, *operands, token):
    far = pl.BlockSpec(memory_space=pl.ANY)
    pointed = bool(operands)
    outs = 2 if pointed else 1
    return pl.pallas_call(
        functools.partial(relay_kernel, pointed),
        out_shape=[pltpu.HBM((ROWS, LANES), BF16)] * outs,
        in_specs=[VM] * len(operands) + [far] * 2,
        out_specs=[far] * outs,
        scratch_shapes=[pltpu.VMEM(field.shape[1:], BF16)]
        + [pltpu.VMEM((ROWS, LANES), BF16)] * outs
        + [
            pltpu.VMEM((Y_ROWS, LANES), F32),
            pltpu.SemaphoreType.DMA((2 * Y_STEPS,)),
            pltpu.SemaphoreType.DMA((outs, 2 * Y_STEPS)),
        ],
        cost_estimate=pl.CostEstimate(
            flops=600_000_000, bytes_accessed=12 << 20, transcendentals=0
        ),
        compiler_params=pltpu.CompilerParams(vmem_limit_bytes=VMEM_LIMIT),
    )(*[near(operand) for operand in operands], field, token)


def own_spectrum(wide, table, place, block=8):
    real = wide[pl.ds(place, 64, stride=block), :]
    imag = wide[pl.ds(4 + place, 64, stride=block), :]
    both = mm(table, jnp.concatenate([real, imag], axis=0).astype(BF16))
    return both[:32, :CHANNELS] + both[32:, CHANNELS:]


def send_field(mixed, table, place, sent, block=8):
    twin = jnp.concatenate([mixed, mixed], axis=1)
    left = side(32)
    both = jnp.concatenate([jnp.where(left, twin, 0.0), jnp.where(left, 0.0, twin)], axis=0)
    out = mm(table, both.astype(BF16))
    sent[pl.ds(place, 64, stride=block), :] = out[:64]
    sent[pl.ds(4 + place, 64, stride=block), :] = out[64:]


def mode_lanes(modes):
    row = lax.broadcasted_iota(jnp.int32, (32, LANES), 0) % modes
    half = lax.broadcasted_iota(jnp.int32, (32, LANES), 1) // CHANNELS
    return row, half


def mix_kernel(small, _, outs, __, ___, scratch, loop):
    got_ref, weight_ref, forward_ref, inverse_ref = small
    out_ref, spec_ref = outs
    wide, sent = scratch
    wide[...] = got_ref[...].astype(F32)
    forward = forward_ref[...]
    inverse = inverse_ref[...]
    modes = weight_ref.shape[1]
    row, half = mode_lanes(modes)
    for p in range(4):
        spec = own_spectrum(wide, forward, p).astype(BF16)
        spec_ref[:, p * CHANNELS : (p + 1) * CHANNELS] = spec
        spec = spec.astype(F32)
        other = jnp.concatenate([-spec[modes:], spec[:modes]], axis=0)
        pieces = []
        for part in (spec, other):
            twin = jnp.concatenate([part, part], axis=1)
            for pair in range(modes // 2):
                pieces.append(jnp.where(row == 2 * pair + half, twin, 0.0).astype(BF16))
        spread = jnp.concatenate(pieces, axis=1)
        weights = weight_ref[:, :, p].reshape(2 * modes * CHANNELS, CHANNELS)
        mixed = mm(spread, weights).astype(BF16).astype(F32)
        send_field(mixed, inverse, p, sent)
    out_ref[...] = sent[...].astype(BF16)


def high_low(values):
    high = values.astype(BF16).astype(F32)
    return jnp.concatenate([high, values - high], axis=1)


def unmix_kernel(small, _, outs, __, ___, scratch, loop):
    got_ref, weight_ref, forward_ref, inverse_ref, term_ref, one_ref, two_ref = small
    out_ref, spec_ref = outs
    wide, sent = scratch
    wide[...] = got_ref[...].astype(F32)
    forward = forward_ref[...]
    inverse = inverse_ref[...]
    modes = weight_ref.shape[1]
    row, half = mode_lanes(modes)
    spec_ref[0:32, :] = one_ref[...]
    spec_ref[32:64, :] = two_ref[...]
    sent[...] = jnp.zeros_like(sent)
    terms = high_low(term_ref[...])
    sent[pl.ds(8, 64, stride=16), :] = terms[:CHANNELS]
    sent[pl.ds(9, 64, stride=16), :] = jnp.broadcast_to(
        terms[CHANNELS : CHANNELS + 1], (CHANNELS, LANES)
    )
    for p in range(4):
        spec = own_spectrum(wide, forward, p).astype(BF16)
        spec_ref[64:96, p * CHANNELS : (p + 1) * CHANNELS] = spec
        other = jnp.concatenate([spec[modes:].astype(F32), -spec[:modes].astype(F32)], axis=0)
        products = nt(spec, weight_ref[0, :, p].reshape(modes * CHANNELS, CHANNELS)) + nt(
            other.astype(BF16), weight_ref[1, :, p].reshape(modes * CHANNELS, CHANNELS)
        )
        total = jnp.zeros((32, LANES), F32)
        for pair in range(modes // 2):
            piece = products[:, pair * LANES : (pair + 1) * LANES]
            total = total + jnp.where(row == 2 * pair + half, piece, 0.0)
        mixed = (total + turned(total))[:, :CHANNELS].astype(BF16).astype(F32)
        send_field(mixed, inverse, p, sent, 16)
    out_ref[...] = sent[...].astype(BF16)


def last_kernel(small, _, outs, __, ___, scratch, loop):
    got_ref, forward_ref = small
    (out_ref,) = outs
    (wide,) = scratch
    for d in range(64):
        wide[d * 48 : (d + 1) * 48, :] = got_ref[d * 48 : (d + 1) * 48, :].astype(F32)
    forward = forward_ref[...]
    for p in range(4):
        out_ref[0:32, p * CHANNELS : (p + 1) * CHANNELS] = own_spectrum(
            wide, forward, p, 48
        ).astype(BF16)
    total = jnp.zeros((40, LANES), F32)
    for d in range(64):
        total = total + wide[d * 48 + 8 : (d + 1) * 48, :]
    high = total.astype(BF16)
    low = (total - high.astype(F32)).astype(BF16)
    out_ref[32:64, :] = jnp.concatenate([high[:32], low[:32]], axis=1)
    rows = wide[pl.ds(41, 64, stride=48), :]
    out_ref[64:96, :] = jnp.concatenate([rows[:32], rows[32:]], axis=1).astype(BF16)
    biases = jnp.concatenate(
        [
            high_low(total[32:40, :CHANNELS]),
            jnp.broadcast_to(wide[42:43, :], (8, LANES)),
        ],
        axis=1,
    )
    out_ref[96:112, :] = jnp.concatenate([biases, biases], axis=0).astype(BF16)


CHUNK = ((512, LANES), BF16)
SPECTRUM = ((32, 4 * CHANNELS), BF16)
WIDE = pltpu.VMEM((512, LANES), F32)


def mixing(got, weights, forward, inverse, token):
    return call(
        mix_kernel,
        [CHUNK, SPECTRUM],
        [WIDE, WIDE],
        200_000_000,
        3 << 20,
        got,
        weights,
        forward,
        inverse,
        token=token,
    )


def outer_products(spec, grad, out_ref):
    modes = out_ref.shape[1]
    depth = spec.shape[0]
    lane = lax.broadcasted_iota(jnp.int32, (CHANNELS, depth), 1) % modes
    other = []
    for n in range(depth // (2 * modes)):
        at = n * 2 * modes
        other += [grad[at + modes : at + 2 * modes], -grad[at : at + modes]]
    other = jnp.concatenate(other, axis=0)
    for p in range(4):
        cut = slice(p * CHANNELS, (p + 1) * CHANNELS)
        both = jnp.concatenate([grad[:, cut], other[:, cut]], axis=1).astype(BF16)
        tall = spec[:, cut].T
        for m in range(modes):
            out = mm(jnp.where(lane == m, tall, 0.0).astype(BF16), both).astype(BF16)
            out_ref[0, m, p] = out[:, :CHANNELS]
            out_ref[1, m, p] = out[:, CHANNELS:]


def rows_of(ref, step, at):
    count = ref.shape[0] // step
    return jnp.concatenate(
        [ref[n * step + at : n * step + at + 32, :] for n in range(count)], axis=0
    ).astype(F32)


def weight_two_kernel(small, _, __, ___, plain, scratch, loop):
    (all_ref,) = small
    (out_ref,) = plain
    outer_products(rows_of(all_ref, 96, 32), rows_of(all_ref, 96, 64), out_ref)


def weight_one_kernel(factor, small, _, __, ___, plain, scratch, loop):
    early_ref, all_ref = small
    out_ref, one_ref, two_ref, bias_ref = plain
    sums = all_ref[32:112, :].astype(F32)
    for n in range(1, all_ref.shape[0] // 112):
        sums = sums + all_ref[n * 112 + 32 : (n + 1) * 112, :].astype(F32)
    sums = sums * factor
    one = sums[:32, :LANES] + sums[:32, LANES:]
    one_ref[0:32, :] = one[:, :CHANNELS]
    one_ref[32:64, :] = one[:, CHANNELS:]
    two = jnp.concatenate([sums[32:64, :LANES], sums[32:64, LANES:]], axis=0)
    two_ref[...] = (two + turned(two))[:, :CHANNELS]
    bias = jnp.concatenate([sums[64:72, :LANES], sums[64:72, LANES:]], axis=0)
    bias_ref[...] = bias + turned(bias)
    outer_products(rows_of(early_ref, 96, 0), rows_of(all_ref, 112, 0), out_ref)


TILES = 128
PAIRS = TILES // 2
TILE = 2 * CHANNELS


def unpack_modes(got_ref, second_ref, depth, block=8):
    second = second_ref[...]
    left = side(32)
    for k in range(MZ):
        near = jnp.concatenate(
            [got_ref[d * block : d * block + 8, :] for d in range(k * 4, k * 4 + 4)], axis=0
        ) if block > 8 else got_ref[k * 32 : (k + 1) * 32, :].astype(F32)
        far = turned(near)
        top = jnp.concatenate([jnp.where(left, near, 0.0), jnp.where(left, far, 0.0)], axis=1)
        low = jnp.concatenate([jnp.where(left, 0.0, far), jnp.where(left, 0.0, near)], axis=1)
        out = mm(second, jnp.concatenate([top, low], axis=0).astype(BF16))
        for x in range(2):
            cut = slice(x * LANES, (x + 1) * LANES)
            depth[pl.ds(x * 2048 + k, 64, stride=32), :] = out[:64, cut]
            depth[pl.ds(x * 2048 + MZ + k, 64, stride=32), :] = out[64:, cut]


def pack_modes(spec, second_ref, out_ref, block=8):
    second = second_ref[...]
    left = side(32)
    for k in range(MZ):
        planes = [
            jnp.concatenate(
                [
                    spec[pl.ds(x * 2048 + k, 64, stride=32), :],
                    spec[pl.ds(x * 2048 + MZ + k, 64, stride=32), :],
                ],
                axis=0,
            )
            for x in range(2)
        ]
        out = mm(second, jnp.concatenate(planes, axis=1).astype(BF16))
        near, far = out[:, :LANES], out[:, LANES:]
        packed = jnp.where(left, near[:32] + turned(near[32:]), turned(far[:32]) + far[32:])
        if block == 8:
            out_ref[k * 32 : (k + 1) * 32, :] = packed.astype(out_ref.dtype)
        else:
            for d in range(4):
                at = (k * 4 + d) * block
                out_ref[at : at + 8, :] = packed[d * 8 : (d + 1) * 8]


def branch_of(depth, third, pair):
    at = pl.multiple_of(pair * 64, 64)
    wide = tn(depth[pl.ds(at, 64), :].astype(BF16), third)
    return wide[:, :LANES], wide[:, LANES:]


def store_spectrum(spec, third, pair, first, second):
    done = nt(third, jnp.concatenate([first, second], axis=0))
    at = pl.multiple_of(pair * 64, 64)
    spec[pl.ds(at, 32), :] = done[:, :LANES]
    spec[pl.ds(at + 32, 32), :] = done[:, LANES:]


def tile_at(tile):
    return pl.ds(pl.multiple_of(tile * TILE, TILE), TILE)


def gelu(preact):
    inner = preact * (ROOT + (ROOT * CUBIC) * (preact * preact))
    halved = 0.5 * preact
    return halved + halved * jnp.tanh(inner)


def gelu_slope(preact):
    square = preact * preact
    tangent = jnp.tanh(preact * (ROOT + (ROOT * CUBIC) * square))
    steep = (0.5 * preact) * (ROOT + (3.0 * ROOT * CUBIC) * square)
    return 0.5 + 0.5 * tangent + steep * (1.0 - tangent * tangent)


def hidden_kernel(small, big, outs, kinds, _, scratch, loop):
    got, inv2, inv3, fwd3, fwd2 = small
    (base,) = big
    hidden, preact = kinds
    depth, spec = scratch
    unpack_modes(got, inv2, depth)
    third_back = inv3[...]
    third = fwd3[...]

    def body(pair, carry):
        made = []
        for e, branch in enumerate(branch_of(depth, third_back, pair)):
            at = tile_at(2 * pair + e)
            pre = base[at, :].astype(F32) + branch
            preact[at, :] = pre.astype(BF16)
            value = gelu(pre).astype(BF16)
            hidden[at, :] = value
            made.append(value)
        store_spectrum(spec, third, pair, *made)
        return carry

    loop(body)
    pack_modes(spec, fwd2, outs[0])


def grad_two_kernel(small, big, outs, kinds, _, scratch, loop):
    got, inv2, inv3, fwd3, fwd2 = small
    base, cot = big
    (grad,) = kinds
    depth, spec = scratch
    unpack_modes(got, inv2, depth)
    third_back = inv3[...]
    third = fwd3[...]

    def body(pair, carry):
        made = []
        for e, branch in enumerate(branch_of(depth, third_back, pair)):
            at = tile_at(2 * pair + e)
            slope = gelu_slope(base[at, :].astype(F32) + branch)
            value = (cot[at, :].astype(F32) * slope).astype(BF16)
            grad[at, :] = value
            made.append(value)
        store_spectrum(spec, third, pair, *made)
        return carry

    loop(body)
    pack_modes(spec, fwd2, outs[0])


def grad_one_kernel(small, big, outs, _, __, scratch, loop):
    got, inv2, inv3, fwd3, fwd2 = small
    base, slope, values = big
    (out,) = outs
    depth, spec, wide, sent = scratch
    wide[...] = got[...].astype(F32)
    unpack_modes(wide, inv2, depth, 16)
    third_back = inv3[...]
    third = fwd3[...]
    ones = jnp.ones((16, 4 * LANES), BF16)

    def body(pair, total):
        made = []
        for e, branch in enumerate(branch_of(depth, third_back, pair)):
            at = tile_at(2 * pair + e)
            back = base[at, :].astype(F32) + branch
            made.append((back * slope[at, :].astype(F32)).astype(BF16))
        store_spectrum(spec, third, pair, *made)
        left = jnp.concatenate(
            [wide_tile(values, 2 * pair), wide_tile(values, 2 * pair + 1)], axis=1
        )
        right = jnp.concatenate(
            [part for tile in made for part in (tile[:CHANNELS], tile[CHANNELS:])], axis=1
        )
        return total + nt(jnp.concatenate([left, ones], axis=0), right)

    total = loop(body, jnp.zeros((CHANNELS + 16, CHANNELS), F32))
    pack_modes(spec, fwd2, sent, 48)
    left = side(1)

    def arrived_sum(place):
        row = jnp.sum(wide[pl.ds(place, 64, stride=16), :], axis=0, keepdims=True)
        row = row + turned(row)
        high = row.astype(BF16).astype(F32)
        return jnp.where(left, high, row - high)

    bias = jnp.concatenate([total[64:65], total[64:65]], axis=1)
    terms = jnp.concatenate(
        [
            jnp.concatenate([total[:32], total[32:64]], axis=1),
            bias,
            arrived_sum(8),
            arrived_sum(9),
            jnp.zeros((5, LANES), F32),
        ],
        axis=0,
    )
    for d in range(64):
        sent[d * 48 + 8 : (d + 1) * 48, :] = terms
    for d in range(64):
        out[d * 48 : (d + 1) * 48, :] = sent[d * 48 : (d + 1) * 48, :].astype(BF16)


def planes(kernel, kinds, *operands, big, token):
    scratch = [pltpu.VMEM((4096, LANES), F32), pltpu.VMEM((4096, LANES), F32)]
    return call(
        kernel,
        [CHUNK],
        scratch,
        1_000_000_000,
        20 << 20,
        *operands,
        big=big,
        kinds=kinds,
        token=token,
    )


def wide_tile(ref, tile):
    at = pl.multiple_of(tile * TILE, TILE)
    return jnp.concatenate(
        [ref[pl.ds(at, CHANNELS), :], ref[pl.ds(at + CHANNELS, CHANNELS), :]], axis=1
    )


def store_wide(ref, tile, wide):
    at = pl.multiple_of(tile * TILE, TILE)
    ref[pl.ds(at, CHANNELS), :] = wide[:, :LANES].astype(BF16)
    ref[pl.ds(at + CHANNELS, CHANNELS), :] = wide[:, LANES:].astype(BF16)


def layer_two_kernel(small, big, _, kinds, __, scratch, loop):
    point, bias = small
    weights = point[...]
    shift = jnp.concatenate([bias[...], bias[...]], axis=1)

    def body(pair, carry):
        for tile in (2 * pair, 2 * pair + 1):
            store_wide(kinds[0], tile, mm(weights, wide_tile(big[0], tile)) + shift)
        return carry

    loop(body)


def slope_kernel(small, big, _, kinds, __, scratch, loop):
    def body(pair, carry):
        for tile in (2 * pair, 2 * pair + 1):
            at = tile_at(tile)
            kinds[0][at, :] = gelu_slope(big[0][at, :].astype(F32)).astype(BF16)
        return carry

    loop(body, unroll=2)


def point_back_kernel(small, big, outs, kinds, _, scratch, loop):
    weights = small[0][...]
    hidden, grad = big
    ones = jnp.ones((16, 4 * LANES), BF16)

    def body(pair, total):
        right = [wide_tile(grad, 2 * pair + e) for e in range(2)]
        for e in range(2):
            store_wide(kinds[0], 2 * pair + e, mm(weights, right[e]))
        left = jnp.concatenate(
            [wide_tile(hidden, 2 * pair), wide_tile(hidden, 2 * pair + 1)], axis=1
        )
        return total + nt(
            jnp.concatenate([left, ones], axis=0), jnp.concatenate(right, axis=1)
        )

    outs[0][...] = loop(body, jnp.zeros((CHANNELS + 16, CHANNELS), F32))


def body(field_in, cotangent, spectral_one, spectral_two, point_one, point_two, bias_one, bias_two):
    forward_c, inverse_c = complex_tables(LANES, MY)
    forward_z, inverse_z = real_tables(LANES, MZ)
    shape = spectral_one.shape
    const = lambda table: jnp.asarray(np.ascontiguousarray(table))

    natural_second = const(second_natural(forward_c))
    third_forward = const(forward_z.T)
    third_adjoint = const(inverse_z)
    third_inverse = const(twice_diagonal(inverse_z))
    third_back = const(twice_diagonal(forward_z.T))
    second_fwd = const(second_paired(forward_c))
    second_adj = const(second_paired(flipped(inverse_c)))
    second_inv = const(second_inverse(inverse_c))
    second_back = const(second_inverse(flipped(forward_c)))
    first_fwd = const(first_forward(forward_c))
    first_adj = const(first_forward(flipped(inverse_c)))
    first_inv = const(first_inverse(inverse_c))
    first_back = const(first_inverse(flipped(forward_c)))

    def exchange(chunk):
        return lax.all_to_all(chunk, "space", split_axis=0, concat_axis=0, tiled=True)

    def samples(spectrum):
        return lax.all_gather(spectrum, "dp", axis=0, tiled=True)

    spread = lambda bias: jnp.broadcast_to(bias[:, None], (CHANNELS, LANES))

    chunk = first_partial(field_in, third_forward, natural_second)
    got = exchange(chunk)
    values, base = relay(field_in, point_one.T, spread(bias_one), token=chunk)

    chunk, spec_one = mixing(got, spectral_one, first_fwd, first_inv, token=base)
    got = exchange(chunk)
    cot = relay(cotangent, token=chunk)[0]

    chunk, hidden, preact = planes(
        hidden_kernel,
        [BF16, BF16],
        got,
        second_inv,
        third_inverse,
        third_forward,
        second_fwd,
        big=[base],
        token=cot,
    )
    got = exchange(chunk)
    base = call(
        layer_two_kernel,
        [],
        [],
        500_000_000,
        12 << 20,
        point_two.T,
        spread(bias_two),
        big=[hidden],
        kinds=[BF16],
    )[0]

    chunk, spec_two = mixing(got, spectral_two, first_fwd, first_inv, token=base)
    got = exchange(chunk)
    slope = call(
        slope_kernel, [], [], 500_000_000, 12 << 20, big=[preact], kinds=[BF16], token=chunk
    )[0]

    chunk, grad_two = planes(
        grad_two_kernel,
        [BF16],
        got,
        second_inv,
        third_inverse,
        third_adjoint,
        second_adj,
        big=[base, cot],
        token=slope,
    )
    got = exchange(chunk)
    term_two, base = call(
        point_back_kernel,
        [((CHANNELS + 16, CHANNELS), F32)],
        [],
        1_000_000_000,
        12 << 20,
        point_two,
        big=[hidden, grad_two],
        kinds=[BF16],
    )

    chunk, early = call(
        unmix_kernel,
        [((1024, LANES), BF16), ((96, 4 * CHANNELS), BF16)],
        [WIDE, pltpu.VMEM((1024, LANES), F32)],
        200_000_000,
        3 << 20,
        got,
        spectral_two,
        first_adj,
        first_back,
        term_two,
        spec_one,
        spec_two,
    )
    got = exchange(chunk)
    early = samples(early)
    spectral_grad_two = call(
        weight_two_kernel,
        [],
        [],
        200_000_000,
        3 << 20,
        early,
        plain=[jax.ShapeDtypeStruct(shape, BF16)],
        token=chunk,
    )[0]

    chunk = call(
        grad_one_kernel,
        [((3072, LANES), BF16)],
        [
            pltpu.VMEM((4096, LANES), F32),
            pltpu.VMEM((4096, LANES), F32),
            pltpu.VMEM((1024, LANES), F32),
            pltpu.VMEM((3072, LANES), F32),
        ],
        1_500_000_000,
        20 << 20,
        got,
        second_back,
        third_back,
        third_adjoint,
        second_adj,
        big=[base, slope, values],
        token=spectral_grad_two,
    )[0]
    got = exchange(chunk)
    late = call(
        last_kernel,
        [((112, 4 * CHANNELS), BF16)],
        [pltpu.VMEM((3072, LANES), F32)],
        50_000_000,
        1 << 20,
        got,
        first_adj,
    )[0]
    late = samples(late)
    cells = lax.axis_size("dp") * lax.axis_size("space") * 2 * LANES * LANES
    square = jax.ShapeDtypeStruct((CHANNELS, CHANNELS), F32)
    spectral_grad_one, point_grad_one, point_grad_two, biases = call(
        functools.partial(weight_one_kernel, 1.0 / math.sqrt(cells)),
        [],
        [],
        200_000_000,
        3 << 20,
        early,
        late,
        plain=[
            jax.ShapeDtypeStruct(shape, BF16),
            square,
            square,
            jax.ShapeDtypeStruct((16, LANES), F32),
        ],
    )
    return (
        spectral_grad_one,
        spectral_grad_two,
        point_grad_one,
        point_grad_two,
        biases[0, :CHANNELS],
        biases[8, :CHANNELS],
    )


def solution(mesh):
    field = P("dp", None, "space", None, None)
    modes = P(None, None, "space", None, None)
    return jax.shard_map(
        body,
        mesh=mesh,
        in_specs=(field, field, modes, modes, P(), P(), P(), P()),
        out_specs=(modes, modes, P(), P(), P(), P()),
        check_vma=False,
    )
```

```python
import functools
import math

import jax
import jax.numpy as jnp
import numpy as np
from jax import lax
from jax.experimental import pallas as pl
from jax.experimental.pallas import tpu as pltpu
from jax.sharding import PartitionSpec as P

MY = 16
MZ = 16
CHANNELS = 64
LANES = 128
ROOT = math.sqrt(2.0 / math.pi)
CUBIC = 0.044715
F32 = jnp.float32
BF16 = jnp.bfloat16
VMEM_LIMIT = 44 * 1024 * 1024


def angles(length, modes, two_sided):
    places = np.arange(length, dtype=np.int64)[:, None]
    orders = np.arange(modes, dtype=np.int64)[None, :]
    if two_sided:
        orders = np.where(orders < modes // 2, orders, orders - modes + length)
    phases = places * orders % length
    return np.float32(2.0 * math.pi / length) * phases.astype(np.float32)


def complex_tables(length, modes):
    radians = angles(length, modes, True)
    factor = np.float32(1.0 / math.sqrt(length))
    cosines = np.cos(radians) * factor
    sines = np.sin(radians) * factor
    forward = np.stack(
        [np.stack([cosines, -sines], axis=1), np.stack([sines, cosines], axis=1)], axis=0
    )
    inverse = np.stack(
        [np.stack([cosines.T, sines.T], axis=1), np.stack([-sines.T, cosines.T], axis=1)], axis=0
    )
    return forward.astype(BF16), inverse.astype(BF16)


def real_tables(length, modes):
    radians = angles(length, modes, False)
    factor = np.float32(1.0 / math.sqrt(length))
    cosines = np.cos(radians) * factor
    sines = np.sin(radians) * factor
    forward = np.concatenate([cosines, -sines], axis=1)
    doubled = np.where(np.arange(modes) == 0, 1.0, 2.0).astype(np.float32)[None, :]
    inverse = np.concatenate([(cosines * doubled).T, (-sines * doubled).T], axis=0)
    return forward.astype(BF16), inverse.astype(BF16)


def flipped(table):
    return np.transpose(table, (2, 3, 0, 1))


def second_natural(table):
    length = table.shape[1]
    split = table.reshape(2, length, 2, MY // 4, 4)
    return split.transpose(3, 2, 4, 0, 1).reshape(2 * MY, 2 * length)


def second_paired(table):
    length = table.shape[1]
    split = table.reshape(2, length // 2, 2, 2, MY // 4, 4)
    return split.transpose(2, 4, 3, 5, 0, 1).reshape(4 * MY, length)


def second_inverse(table):
    length = table.shape[3]
    split = table.reshape(2, MY // 4, 4, 2, length // 2, 2)
    return split.transpose(3, 4, 5, 1, 0, 2).reshape(length, 4 * MY)


def first_forward(table):
    length, modes = table.shape[1], table.shape[3]
    split = table.reshape(2, length // 2, 2, 2, modes)
    return split.transpose(2, 3, 4, 0, 1).reshape(4 * modes, length)


def first_inverse(table):
    modes, length = table.shape[1], table.shape[3]
    split = table.reshape(2, modes, 2, length // 2, 2)
    return split.transpose(2, 3, 4, 0, 1).reshape(length, 4 * modes)


def twice_diagonal(table):
    zero = np.zeros_like(table)
    return np.block([[table, zero], [zero, table]])


def mm(left, right):
    return lax.dot_general(left, right, (((1,), (0,)), ((), ())), preferred_element_type=F32)


def nt(left, right):
    return lax.dot_general(left, right, (((1,), (1,)), ((), ())), preferred_element_type=F32)


def tn(left, right):
    return lax.dot_general(left, right, (((0,), (0,)), ((), ())), preferred_element_type=F32)


def side(rows):
    return lax.broadcasted_iota(jnp.int32, (rows, LANES), 1) < LANES // 2


def turned(values):
    return pltpu.roll(values, LANES // 2, 1)


def whole(shape):
    return pl.BlockSpec(shape, lambda *_: (0,) * len(shape))


VM = pl.BlockSpec(memory_space=pltpu.VMEM)


GROUPS = 8
ROWS = 2 * LANES * CHANNELS


def near(value):
    return pltpu.with_memory_space_constraint(value, pltpu.VMEM)


def afar(value):
    return pltpu.with_memory_space_constraint(value, pltpu.HBM)


def call(
    kernel, outs, scratch, flops, moved, *operands, big=(), kinds=(), plain=(), token=None
):
    cut = ROWS // GROUPS
    counts = [
        len(operands),
        len(big),
        0 if token is None else 1,
        len(outs),
        len(kinds),
        len(plain),
        len(scratch),
        len(outs),
        len(big),
        len(kinds),
        3,
    ]

    def whole_kernel(*refs):
        parts = []
        at = 0
        for count in counts:
            parts.append(refs[at : at + count])
            at += count
        small, big_far, _, outs_far, kinds_far, plains, own, outs_near, big_near, kinds_near, sems = parts
        in_sem, out_sem, end_sem = sems

        def group_of(far, close, sem, index, group, out):
            rows = pl.ds(pl.multiple_of(group * cut, cut), cut)
            pair = (close.at[rows], far.at[rows]) if out else (far.at[rows], close.at[rows])
            return pltpu.make_async_copy(*pair, sem.at[index, group])

        def coming(index, group):
            return group_of(big_far[index], big_near[index], in_sem, index, group, False)

        def going(index, group):
            return group_of(kinds_far[index], kinds_near[index], out_sem, index, group, True)

        for group in range(GROUPS):
            for index in range(len(big)):
                coming(index, group).start()

        def loop(body, carry=0, unroll=4):
            per = PAIRS // GROUPS

            def some(i, carry):
                for j in range(unroll):
                    carry = body(i * unroll + j, carry)
                return carry

            def each(group, carry):
                for index in range(len(big)):
                    coming(index, group).wait()
                first = group * (per // unroll)
                carry = lax.fori_loop(first, first + per // unroll, some, carry)
                for index in range(len(kinds)):
                    going(index, group).start()
                return carry

            return lax.fori_loop(0, GROUPS, each, carry)

        kernel(small, big_near, outs_near, kinds_near, plains, own, loop)
        last = [
            pltpu.make_async_copy(close, far, end_sem.at[index])
            for index, (close, far) in enumerate(zip(outs_near, outs_far))
        ]
        for copy in last:
            copy.start()
        for index in range(len(kinds)):
            for group in range(GROUPS):
                going(index, group).wait()
        for copy in last:
            copy.wait()

    operands = [near(operand) for operand in operands]
    far = pl.BlockSpec(memory_space=pl.ANY)
    extra = [] if token is None else [token]
    shapes = [pltpu.HBM(shape, kind) for shape, kind in outs]
    shapes += [pltpu.HBM((ROWS, LANES), kind) for kind in kinds]
    return pl.pallas_call(
        whole_kernel,
        out_shape=shapes + list(plain),
        in_specs=[VM] * len(operands) + [far] * (len(big) + len(extra)),
        out_specs=[far] * len(shapes) + [VM] * len(plain),
        scratch_shapes=list(scratch)
        + [pltpu.VMEM(shape, kind) for shape, kind in outs]
        + [pltpu.VMEM((ROWS, LANES), array.dtype) for array in big]
        + [pltpu.VMEM((ROWS, LANES), kind) for kind in kinds]
        + [
            pltpu.SemaphoreType.DMA((max(len(big), 1), GROUPS)),
            pltpu.SemaphoreType.DMA((max(len(kinds), 1), GROUPS)),
            pltpu.SemaphoreType.DMA((max(len(outs), 1),)),
        ],
        cost_estimate=pl.CostEstimate(flops=flops, bytes_accessed=moved, transcendentals=0),
        compiler_params=pltpu.CompilerParams(vmem_limit_bytes=VMEM_LIMIT),
    )(*operands, *[afar(array) for array in (*big, *extra)])


C_STEP = 8


def spectrum_kernel(field, third_far, second_far, out_far, near_field, third_ref, second_ref, chunk, spec, sems, extra):
    def coming(step):
        cut = pl.ds(step * C_STEP, C_STEP)
        return pltpu.make_async_copy(field.at[0, cut], near_field.at[cut], sems.at[step])

    tables = [
        pltpu.make_async_copy(third_far, third_ref, extra.at[0]),
        pltpu.make_async_copy(second_far, second_ref, extra.at[1]),
    ]
    for copy in tables:
        copy.start()
    for step in range(CHANNELS // C_STEP):
        coming(step).start()
    for copy in tables:
        copy.wait()
    third = third_ref[...]

    def some(step, carry):
        coming(step).wait()
        for x in range(2):
            rows = near_field[pl.ds(step * C_STEP, C_STEP), x].reshape(C_STEP * LANES, LANES)
            done = nt(third, rows)
            for c in range(C_STEP):
                place = pl.multiple_of((x * CHANNELS + step * C_STEP + c) * 2 * MZ, 2 * MZ)
                spec[pl.ds(place, 2 * MZ), :] = done[:, c * LANES : (c + 1) * LANES]
        return carry

    lax.fori_loop(0, CHANNELS // C_STEP, some, 0)
    second = second_ref[...]
    for k in range(MZ):
        real = spec[pl.ds(k, LANES, stride=2 * MZ), :]
        imag = spec[pl.ds(MZ + k, LANES, stride=2 * MZ), :]
        both = jnp.concatenate([real, imag], axis=1).astype(BF16)
        chunk[k * 32 : (k + 1) * 32, :] = nt(second, both).astype(BF16)
    out = pltpu.make_async_copy(chunk, out_far, extra.at[2])
    out.start()
    out.wait()


def first_partial(field, third, second):
    far = pl.BlockSpec(memory_space=pl.ANY)
    return pl.pallas_call(
        spectrum_kernel,
        out_shape=pltpu.HBM((512, LANES), BF16),
        in_specs=[far] * 3,
        out_specs=far,
        scratch_shapes=[
            pltpu.VMEM(field.shape[1:], BF16),
            pltpu.VMEM(third.shape, BF16),
            pltpu.VMEM(second.shape, BF16),
            pltpu.VMEM((512, LANES), BF16),
            pltpu.VMEM((4096, LANES), F32),
            pltpu.SemaphoreType.DMA((CHANNELS // C_STEP,)),
            pltpu.SemaphoreType.DMA((3,)),
        ],
        cost_estimate=pl.CostEstimate(
            flops=600_000_000, bytes_accessed=6 << 20, transcendentals=0
        ),
        compiler_params=pltpu.CompilerParams(vmem_limit_bytes=VMEM_LIMIT),
    )(afar(field), afar(third), afar(second))


Y_STEP = 16
Y_STEPS = LANES // Y_STEP
Y_ROWS = Y_STEP * CHANNELS


def relay_kernel(pointed, *refs):
    if pointed:
        point_ref, bias_ref = refs[:2]
        refs = refs[2:]
    outs = 2 if pointed else 1
    field = refs[0]
    out_far = refs[2 : 2 + outs]
    near_field = refs[2 + outs]
    out_near = refs[3 + outs : 3 + 2 * outs]
    rows_ref, in_sem, out_sem = refs[3 + 2 * outs :]

    def coming(step):
        x = step // Y_STEPS
        cut = pl.ds(pl.multiple_of((step % Y_STEPS) * Y_STEP, Y_STEP), Y_STEP)
        return pltpu.make_async_copy(
            field.at[0, :, x, cut], near_field.at[:, x, cut], in_sem.at[step]
        )

    def going(index, step):
        cut = pl.ds(pl.multiple_of(step * Y_ROWS, Y_ROWS), Y_ROWS)
        return pltpu.make_async_copy(
            out_near[index].at[cut], out_far[index].at[cut], out_sem.at[index, step]
        )

    for step in range(2 * Y_STEPS):
        coming(step).start()
    if pointed:
        point = point_ref[...]
        shift = jnp.concatenate([bias_ref[...], bias_ref[...]], axis=1)

    def some(step, carry):
        coming(step).wait()
        at = pl.multiple_of((step % Y_STEPS) * Y_STEP, Y_STEP)
        rows_ref[...] = (
            near_field[:, step // Y_STEPS, pl.ds(at, Y_STEP), :].astype(F32).reshape(Y_ROWS, LANES)
        )
        for y in range(0, Y_STEP, 2):
            pair = [rows_ref[pl.ds(y + e, CHANNELS, stride=Y_STEP), :] for e in range(2)]
            tile = step * (Y_STEP // 2) + y // 2
            out_near[0][tile_at(tile), :] = jnp.concatenate(pair, axis=0).astype(BF16)
            if pointed:
                wide = jnp.concatenate(pair, axis=1).astype(BF16)
                store_wide(out_near[1], tile, mm(point, wide) + shift)
        for index in range(outs):
            going(index, step).start()
        return carry

    lax.fori_loop(0, 2 * Y_STEPS, some, 0)
    for step in range(2 * Y_STEPS):
        for index in range(outs):
            going(index, step).wait()


def relay(field, *operands, token):
    far = pl.BlockSpec(memory_space=pl.ANY)
    pointed = bool(operands)
    outs = 2 if pointed else 1
    return pl.pallas_call(
        functools.partial(relay_kernel, pointed),
        out_shape=[pltpu.HBM((ROWS, LANES), BF16)] * outs,
        in_specs=[VM] * len(operands) + [far] * 2,
        out_specs=[far] * outs,
        scratch_shapes=[pltpu.VMEM(field.shape[1:], BF16)]
        + [pltpu.VMEM((ROWS, LANES), BF16)] * outs
        + [
            pltpu.VMEM((Y_ROWS, LANES), F32),
            pltpu.SemaphoreType.DMA((2 * Y_STEPS,)),
            pltpu.SemaphoreType.DMA((outs, 2 * Y_STEPS)),
        ],
        cost_estimate=pl.CostEstimate(
            flops=600_000_000, bytes_accessed=12 << 20, transcendentals=0
        ),
        compiler_params=pltpu.CompilerParams(vmem_limit_bytes=VMEM_LIMIT),
    )(*[near(operand) for operand in operands], afar(field), afar(token))


def own_spectrum(wide, table, place, block=8):
    real = wide[pl.ds(place, 64, stride=block), :]
    imag = wide[pl.ds(4 + place, 64, stride=block), :]
    both = mm(table, jnp.concatenate([real, imag], axis=0).astype(BF16))
    return both[:32, :CHANNELS] + both[32:, CHANNELS:]


def send_field(mixed, table, place, sent, block=8):
    twin = jnp.concatenate([mixed, mixed], axis=1)
    left = side(32)
    both = jnp.concatenate([jnp.where(left, twin, 0.0), jnp.where(left, 0.0, twin)], axis=0)
    out = mm(table, both.astype(BF16))
    sent[pl.ds(place, 64, stride=block), :] = out[:64]
    sent[pl.ds(4 + place, 64, stride=block), :] = out[64:]


def mode_lanes(modes):
    row = lax.broadcasted_iota(jnp.int32, (32, LANES), 0) % modes
    half = lax.broadcasted_iota(jnp.int32, (32, LANES), 1) // CHANNELS
    return row, half


def mix_kernel(small, _, outs, __, ___, scratch, loop):
    got_ref, weight_ref, forward_ref, inverse_ref = small
    out_ref, spec_ref = outs
    wide, sent = scratch
    wide[...] = got_ref[...].astype(F32)
    forward = forward_ref[...]
    inverse = inverse_ref[...]
    modes = weight_ref.shape[1]
    row, half = mode_lanes(modes)
    for p in range(4):
        spec = own_spectrum(wide, forward, p).astype(BF16)
        spec_ref[:, p * CHANNELS : (p + 1) * CHANNELS] = spec
        spec = spec.astype(F32)
        other = jnp.concatenate([-spec[modes:], spec[:modes]], axis=0)
        pieces = []
        for part in (spec, other):
            twin = jnp.concatenate([part, part], axis=1)
            for pair in range(modes // 2):
                pieces.append(jnp.where(row == 2 * pair + half, twin, 0.0).astype(BF16))
        spread = jnp.concatenate(pieces, axis=1)
        weights = weight_ref[:, :, p].reshape(2 * modes * CHANNELS, CHANNELS)
        mixed = mm(spread, weights).astype(BF16).astype(F32)
        send_field(mixed, inverse, p, sent)
    out_ref[...] = sent[...].astype(BF16)


def high_low(values):
    high = values.astype(BF16).astype(F32)
    return jnp.concatenate([high, values - high], axis=1)


def unmix_kernel(small, _, outs, __, ___, scratch, loop):
    got_ref, weight_ref, forward_ref, inverse_ref, term_ref, one_ref, two_ref = small
    out_ref, spec_ref = outs
    wide, sent = scratch
    wide[...] = got_ref[...].astype(F32)
    forward = forward_ref[...]
    inverse = inverse_ref[...]
    modes = weight_ref.shape[1]
    row, half = mode_lanes(modes)
    spec_ref[0:32, :] = one_ref[...]
    spec_ref[32:64, :] = two_ref[...]
    sent[...] = jnp.zeros_like(sent)
    terms = high_low(term_ref[...])
    sent[pl.ds(8, 64, stride=16), :] = terms[:CHANNELS]
    sent[pl.ds(9, 64, stride=16), :] = jnp.broadcast_to(
        terms[CHANNELS : CHANNELS + 1], (CHANNELS, LANES)
    )
    for p in range(4):
        spec = own_spectrum(wide, forward, p).astype(BF16)
        spec_ref[64:96, p * CHANNELS : (p + 1) * CHANNELS] = spec
        other = jnp.concatenate([spec[modes:].astype(F32), -spec[:modes].astype(F32)], axis=0)
        products = nt(spec, weight_ref[0, :, p].reshape(modes * CHANNELS, CHANNELS)) + nt(
            other.astype(BF16), weight_ref[1, :, p].reshape(modes * CHANNELS, CHANNELS)
        )
        total = jnp.zeros((32, LANES), F32)
        for pair in range(modes // 2):
            piece = products[:, pair * LANES : (pair + 1) * LANES]
            total = total + jnp.where(row == 2 * pair + half, piece, 0.0)
        mixed = (total + turned(total))[:, :CHANNELS].astype(BF16).astype(F32)
        send_field(mixed, inverse, p, sent, 16)
    out_ref[...] = sent[...].astype(BF16)


def last_kernel(small, _, outs, __, ___, scratch, loop):
    got_ref, forward_ref = small
    (out_ref,) = outs
    (wide,) = scratch
    for d in range(64):
        wide[d * 48 : (d + 1) * 48, :] = got_ref[d * 48 : (d + 1) * 48, :].astype(F32)
    forward = forward_ref[...]
    for p in range(4):
        out_ref[0:32, p * CHANNELS : (p + 1) * CHANNELS] = own_spectrum(
            wide, forward, p, 48
        ).astype(BF16)
    total = jnp.zeros((40, LANES), F32)
    for d in range(64):
        total = total + wide[d * 48 + 8 : (d + 1) * 48, :]
    high = total.astype(BF16)
    low = (total - high.astype(F32)).astype(BF16)
    out_ref[32:64, :] = jnp.concatenate([high[:32], low[:32]], axis=1)
    rows = wide[pl.ds(41, 64, stride=48), :]
    out_ref[64:96, :] = jnp.concatenate([rows[:32], rows[32:]], axis=1).astype(BF16)
    biases = jnp.concatenate(
        [
            high_low(total[32:40, :CHANNELS]),
            jnp.broadcast_to(wide[42:43, :], (8, LANES)),
        ],
        axis=1,
    )
    out_ref[96:112, :] = jnp.concatenate([biases, biases], axis=0).astype(BF16)


CHUNK = ((512, LANES), BF16)
SPECTRUM = ((32, 4 * CHANNELS), BF16)
WIDE = pltpu.VMEM((512, LANES), F32)


def mixing(got, weights, forward, inverse, token):
    return call(
        mix_kernel,
        [CHUNK, SPECTRUM],
        [WIDE, WIDE],
        200_000_000,
        3 << 20,
        got,
        weights,
        forward,
        inverse,
        token=token,
    )


def outer_products(spec, grad, out_ref):
    modes = out_ref.shape[1]
    depth = spec.shape[0]
    lane = lax.broadcasted_iota(jnp.int32, (CHANNELS, depth), 1) % modes
    other = []
    for n in range(depth // (2 * modes)):
        at = n * 2 * modes
        other += [grad[at + modes : at + 2 * modes], -grad[at : at + modes]]
    other = jnp.concatenate(other, axis=0)
    for p in range(4):
        cut = slice(p * CHANNELS, (p + 1) * CHANNELS)
        both = jnp.concatenate([grad[:, cut], other[:, cut]], axis=1).astype(BF16)
        tall = spec[:, cut].T
        for m in range(modes):
            out = mm(jnp.where(lane == m, tall, 0.0).astype(BF16), both).astype(BF16)
            out_ref[0, m, p] = out[:, :CHANNELS]
            out_ref[1, m, p] = out[:, CHANNELS:]


def rows_of(ref, step, at):
    count = ref.shape[0] // step
    return jnp.concatenate(
        [ref[n * step + at : n * step + at + 32, :] for n in range(count)], axis=0
    ).astype(F32)


def weight_two_kernel(small, _, __, ___, plain, scratch, loop):
    (all_ref,) = small
    (out_ref,) = plain
    outer_products(rows_of(all_ref, 96, 32), rows_of(all_ref, 96, 64), out_ref)


def weight_one_kernel(factor, small, _, __, ___, plain, scratch, loop):
    early_ref, all_ref = small
    out_ref, one_ref, two_ref, bias_ref = plain
    sums = all_ref[32:112, :].astype(F32)
    for n in range(1, all_ref.shape[0] // 112):
        sums = sums + all_ref[n * 112 + 32 : (n + 1) * 112, :].astype(F32)
    sums = sums * factor
    one = sums[:32, :LANES] + sums[:32, LANES:]
    one_ref[0:32, :] = one[:, :CHANNELS]
    one_ref[32:64, :] = one[:, CHANNELS:]
    two = jnp.concatenate([sums[32:64, :LANES], sums[32:64, LANES:]], axis=0)
    two_ref[...] = (two + turned(two))[:, :CHANNELS]
    bias = jnp.concatenate([sums[64:72, :LANES], sums[64:72, LANES:]], axis=0)
    bias_ref[...] = bias + turned(bias)
    outer_products(rows_of(early_ref, 96, 0), rows_of(all_ref, 112, 0), out_ref)


TILES = 128
PAIRS = TILES // 2
TILE = 2 * CHANNELS


def unpack_modes(got_ref, second_ref, depth, block=8):
    second = second_ref[...]
    left = side(32)
    for k in range(MZ):
        near = jnp.concatenate(
            [got_ref[d * block : d * block + 8, :] for d in range(k * 4, k * 4 + 4)], axis=0
        ) if block > 8 else got_ref[k * 32 : (k + 1) * 32, :].astype(F32)
        far = turned(near)
        top = jnp.concatenate([jnp.where(left, near, 0.0), jnp.where(left, far, 0.0)], axis=1)
        low = jnp.concatenate([jnp.where(left, 0.0, far), jnp.where(left, 0.0, near)], axis=1)
        out = mm(second, jnp.concatenate([top, low], axis=0).astype(BF16))
        for x in range(2):
            cut = slice(x * LANES, (x + 1) * LANES)
            depth[pl.ds(x * 2048 + k, 64, stride=32), :] = out[:64, cut]
            depth[pl.ds(x * 2048 + MZ + k, 64, stride=32), :] = out[64:, cut]


def pack_modes(spec, second_ref, out_ref, block=8):
    second = second_ref[...]
    left = side(32)
    for k in range(MZ):
        planes = [
            jnp.concatenate(
                [
                    spec[pl.ds(x * 2048 + k, 64, stride=32), :],
                    spec[pl.ds(x * 2048 + MZ + k, 64, stride=32), :],
                ],
                axis=0,
            )
            for x in range(2)
        ]
        out = mm(second, jnp.concatenate(planes, axis=1).astype(BF16))
        near, far = out[:, :LANES], out[:, LANES:]
        packed = jnp.where(left, near[:32] + turned(near[32:]), turned(far[:32]) + far[32:])
        if block == 8:
            out_ref[k * 32 : (k + 1) * 32, :] = packed.astype(out_ref.dtype)
        else:
            for d in range(4):
                at = (k * 4 + d) * block
                out_ref[at : at + 8, :] = packed[d * 8 : (d + 1) * 8]


def branch_of(depth, third, pair):
    at = pl.multiple_of(pair * 64, 64)
    wide = tn(depth[pl.ds(at, 64), :].astype(BF16), third)
    return wide[:, :LANES], wide[:, LANES:]


def store_spectrum(spec, third, pair, first, second):
    done = nt(third, jnp.concatenate([first, second], axis=0))
    at = pl.multiple_of(pair * 64, 64)
    spec[pl.ds(at, 32), :] = done[:, :LANES]
    spec[pl.ds(at + 32, 32), :] = done[:, LANES:]


def tile_at(tile):
    return pl.ds(pl.multiple_of(tile * TILE, TILE), TILE)


def gelu(preact):
    inner = preact * (ROOT + (ROOT * CUBIC) * (preact * preact))
    halved = 0.5 * preact
    return halved + halved * jnp.tanh(inner)


def gelu_slope(preact):
    square = preact * preact
    tangent = jnp.tanh(preact * (ROOT + (ROOT * CUBIC) * square))
    steep = (0.5 * preact) * (ROOT + (3.0 * ROOT * CUBIC) * square)
    return 0.5 + 0.5 * tangent + steep * (1.0 - tangent * tangent)


def hidden_kernel(small, big, outs, kinds, _, scratch, loop):
    got, inv2, inv3, fwd3, fwd2 = small
    (base,) = big
    hidden, preact = kinds
    depth, spec = scratch
    unpack_modes(got, inv2, depth)
    third_back = inv3[...]
    third = fwd3[...]

    def body(pair, carry):
        made = []
        for e, branch in enumerate(branch_of(depth, third_back, pair)):
            at = tile_at(2 * pair + e)
            pre = base[at, :].astype(F32) + branch
            preact[at, :] = pre.astype(BF16)
            value = gelu(pre).astype(BF16)
            hidden[at, :] = value
            made.append(value)
        store_spectrum(spec, third, pair, *made)
        return carry

    loop(body)
    pack_modes(spec, fwd2, outs[0])


def grad_two_kernel(small, big, outs, kinds, _, scratch, loop):
    got, inv2, inv3, fwd3, fwd2 = small
    base, cot = big
    (grad,) = kinds
    depth, spec = scratch
    unpack_modes(got, inv2, depth)
    third_back = inv3[...]
    third = fwd3[...]

    def body(pair, carry):
        made = []
        for e, branch in enumerate(branch_of(depth, third_back, pair)):
            at = tile_at(2 * pair + e)
            slope = gelu_slope(base[at, :].astype(F32) + branch)
            value = (cot[at, :].astype(F32) * slope).astype(BF16)
            grad[at, :] = value
            made.append(value)
        store_spectrum(spec, third, pair, *made)
        return carry

    loop(body)
    pack_modes(spec, fwd2, outs[0])


def grad_one_kernel(small, big, outs, _, __, scratch, loop):
    got, inv2, inv3, fwd3, fwd2 = small
    base, slope, values = big
    (out,) = outs
    depth, spec, wide, sent = scratch
    wide[...] = got[...].astype(F32)
    unpack_modes(wide, inv2, depth, 16)
    third_back = inv3[...]
    third = fwd3[...]
    ones = jnp.ones((16, 4 * LANES), BF16)

    def body(pair, total):
        made = []
        for e, branch in enumerate(branch_of(depth, third_back, pair)):
            at = tile_at(2 * pair + e)
            back = base[at, :].astype(F32) + branch
            made.append((back * slope[at, :].astype(F32)).astype(BF16))
        store_spectrum(spec, third, pair, *made)
        left = jnp.concatenate(
            [wide_tile(values, 2 * pair), wide_tile(values, 2 * pair + 1)], axis=1
        )
        right = jnp.concatenate(
            [part for tile in made for part in (tile[:CHANNELS], tile[CHANNELS:])], axis=1
        )
        return total + nt(jnp.concatenate([left, ones], axis=0), right)

    total = loop(body, jnp.zeros((CHANNELS + 16, CHANNELS), F32))
    pack_modes(spec, fwd2, sent, 48)
    left = side(1)

    def arrived_sum(place):
        row = jnp.sum(wide[pl.ds(place, 64, stride=16), :], axis=0, keepdims=True)
        row = row + turned(row)
        high = row.astype(BF16).astype(F32)
        return jnp.where(left, high, row - high)

    bias = jnp.concatenate([total[64:65], total[64:65]], axis=1)
    terms = jnp.concatenate(
        [
            jnp.concatenate([total[:32], total[32:64]], axis=1),
            bias,
            arrived_sum(8),
            arrived_sum(9),
            jnp.zeros((5, LANES), F32),
        ],
        axis=0,
    )
    for d in range(64):
        sent[d * 48 + 8 : (d + 1) * 48, :] = terms
    for d in range(64):
        out[d * 48 : (d + 1) * 48, :] = sent[d * 48 : (d + 1) * 48, :].astype(BF16)


def planes(kernel, kinds, *operands, big, token):
    scratch = [pltpu.VMEM((4096, LANES), F32), pltpu.VMEM((4096, LANES), F32)]
    return call(
        kernel,
        [CHUNK],
        scratch,
        1_000_000_000,
        20 << 20,
        *operands,
        big=big,
        kinds=kinds,
        token=token,
    )


def wide_tile(ref, tile):
    at = pl.multiple_of(tile * TILE, TILE)
    return jnp.concatenate(
        [ref[pl.ds(at, CHANNELS), :], ref[pl.ds(at + CHANNELS, CHANNELS), :]], axis=1
    )


def store_wide(ref, tile, wide):
    at = pl.multiple_of(tile * TILE, TILE)
    ref[pl.ds(at, CHANNELS), :] = wide[:, :LANES].astype(BF16)
    ref[pl.ds(at + CHANNELS, CHANNELS), :] = wide[:, LANES:].astype(BF16)


def layer_two_kernel(small, big, _, kinds, __, scratch, loop):
    point, bias = small
    weights = point[...]
    shift = jnp.concatenate([bias[...], bias[...]], axis=1)

    def body(pair, carry):
        for tile in (2 * pair, 2 * pair + 1):
            store_wide(kinds[0], tile, mm(weights, wide_tile(big[0], tile)) + shift)
        return carry

    loop(body)


def slope_kernel(small, big, _, kinds, __, scratch, loop):
    def body(pair, carry):
        for tile in (2 * pair, 2 * pair + 1):
            at = tile_at(tile)
            kinds[0][at, :] = gelu_slope(big[0][at, :].astype(F32)).astype(BF16)
        return carry

    loop(body, unroll=2)


def point_back_kernel(small, big, outs, kinds, _, scratch, loop):
    weights = small[0][...]
    hidden, grad = big
    ones = jnp.ones((16, 4 * LANES), BF16)

    def body(pair, total):
        right = [wide_tile(grad, 2 * pair + e) for e in range(2)]
        for e in range(2):
            store_wide(kinds[0], 2 * pair + e, mm(weights, right[e]))
        left = jnp.concatenate(
            [wide_tile(hidden, 2 * pair), wide_tile(hidden, 2 * pair + 1)], axis=1
        )
        return total + nt(
            jnp.concatenate([left, ones], axis=0), jnp.concatenate(right, axis=1)
        )

    outs[0][...] = loop(body, jnp.zeros((CHANNELS + 16, CHANNELS), F32))


def body(field_in, cotangent, spectral_one, spectral_two, point_one, point_two, bias_one, bias_two):
    forward_c, inverse_c = complex_tables(LANES, MY)
    forward_z, inverse_z = real_tables(LANES, MZ)
    shape = spectral_one.shape
    const = lambda table: jnp.asarray(np.ascontiguousarray(table))

    natural_second = const(second_natural(forward_c))
    third_forward = const(forward_z.T)
    third_adjoint = const(inverse_z)
    third_inverse = const(twice_diagonal(inverse_z))
    third_back = const(twice_diagonal(forward_z.T))
    second_fwd = const(second_paired(forward_c))
    second_adj = const(second_paired(flipped(inverse_c)))
    second_inv = const(second_inverse(inverse_c))
    second_back = const(second_inverse(flipped(forward_c)))
    first_fwd = const(first_forward(forward_c))
    first_adj = const(first_forward(flipped(inverse_c)))
    first_inv = const(first_inverse(inverse_c))
    first_back = const(first_inverse(flipped(forward_c)))

    def exchange(chunk):
        return lax.all_to_all(chunk, "space", split_axis=0, concat_axis=0, tiled=True)

    def samples(spectrum):
        return lax.all_gather(spectrum, "dp", axis=0, tiled=True)

    spread = lambda bias: jnp.broadcast_to(bias[:, None], (CHANNELS, LANES))

    chunk = first_partial(field_in, third_forward, natural_second)
    got = exchange(chunk)
    values, base = relay(field_in, point_one.T, spread(bias_one), token=chunk)

    chunk, spec_one = mixing(got, spectral_one, first_fwd, first_inv, token=base)
    got = exchange(chunk)
    cot = relay(cotangent, token=chunk)[0]

    chunk, hidden, preact = planes(
        hidden_kernel,
        [BF16, BF16],
        got,
        second_inv,
        third_inverse,
        third_forward,
        second_fwd,
        big=[base],
        token=cot,
    )
    got = exchange(chunk)
    base = call(
        layer_two_kernel,
        [],
        [],
        500_000_000,
        12 << 20,
        point_two.T,
        spread(bias_two),
        big=[hidden],
        kinds=[BF16],
    )[0]

    chunk, spec_two = mixing(got, spectral_two, first_fwd, first_inv, token=base)
    got = exchange(chunk)
    slope = call(
        slope_kernel, [], [], 500_000_000, 12 << 20, big=[preact], kinds=[BF16], token=chunk
    )[0]

    chunk, grad_two = planes(
        grad_two_kernel,
        [BF16],
        got,
        second_inv,
        third_inverse,
        third_adjoint,
        second_adj,
        big=[base, cot],
        token=slope,
    )
    got = exchange(chunk)
    term_two, base = call(
        point_back_kernel,
        [((CHANNELS + 16, CHANNELS), F32)],
        [],
        1_000_000_000,
        12 << 20,
        point_two,
        big=[hidden, grad_two],
        kinds=[BF16],
    )

    chunk, early = call(
        unmix_kernel,
        [((1024, LANES), BF16), ((96, 4 * CHANNELS), BF16)],
        [WIDE, pltpu.VMEM((1024, LANES), F32)],
        200_000_000,
        3 << 20,
        got,
        spectral_two,
        first_adj,
        first_back,
        term_two,
        spec_one,
        spec_two,
    )
    got = exchange(chunk)
    early = samples(early)
    spectral_grad_two = call(
        weight_two_kernel,
        [],
        [],
        200_000_000,
        3 << 20,
        early,
        plain=[jax.ShapeDtypeStruct(shape, BF16)],
        token=chunk,
    )[0]

    chunk = call(
        grad_one_kernel,
        [((3072, LANES), BF16)],
        [
            pltpu.VMEM((4096, LANES), F32),
            pltpu.VMEM((4096, LANES), F32),
            pltpu.VMEM((1024, LANES), F32),
            pltpu.VMEM((3072, LANES), F32),
        ],
        1_500_000_000,
        20 << 20,
        got,
        second_back,
        third_back,
        third_adjoint,
        second_adj,
        big=[base, slope, values],
        token=spectral_grad_two,
    )[0]
    got = exchange(chunk)
    late = call(
        last_kernel,
        [((112, 4 * CHANNELS), BF16)],
        [pltpu.VMEM((3072, LANES), F32)],
        50_000_000,
        1 << 20,
        got,
        first_adj,
    )[0]
    late = samples(late)
    cells = lax.axis_size("dp") * lax.axis_size("space") * 2 * LANES * LANES
    square = jax.ShapeDtypeStruct((CHANNELS, CHANNELS), F32)
    spectral_grad_one, point_grad_one, point_grad_two, biases = call(
        functools.partial(weight_one_kernel, 1.0 / math.sqrt(cells)),
        [],
        [],
        200_000_000,
        3 << 20,
        early,
        late,
        plain=[
            jax.ShapeDtypeStruct(shape, BF16),
            square,
            square,
            jax.ShapeDtypeStruct((16, LANES), F32),
        ],
    )
    return (
        spectral_grad_one,
        spectral_grad_two,
        point_grad_one,
        point_grad_two,
        biases[0, :CHANNELS],
        biases[8, :CHANNELS],
    )


def solution(mesh):
    field = P("dp", None, "space", None, None)
    modes = P(None, None, "space", None, None)
    return jax.shard_map(
        body,
        mesh=mesh,
        in_specs=(field, field, modes, modes, P(), P(), P(), P()),
        out_specs=(modes, modes, P(), P(), P(), P()),
        check_vma=False,
    )
```

```python
import functools
import math

import jax
import jax.numpy as jnp
import numpy as np
from jax import lax
from jax.experimental import pallas as pl
from jax.experimental.pallas import tpu as pltpu
from jax.sharding import PartitionSpec as P

MY = 16
MZ = 16
CHANNELS = 64
LANES = 128
ROOT = math.sqrt(2.0 / math.pi)
CUBIC = 0.044715
F32 = jnp.float32
BF16 = jnp.bfloat16
VMEM_LIMIT = 44 * 1024 * 1024


def angles(length, modes, two_sided):
    places = np.arange(length, dtype=np.int64)[:, None]
    orders = np.arange(modes, dtype=np.int64)[None, :]
    if two_sided:
        orders = np.where(orders < modes // 2, orders, orders - modes + length)
    phases = places * orders % length
    return np.float32(2.0 * math.pi / length) * phases.astype(np.float32)


def complex_tables(length, modes):
    radians = angles(length, modes, True)
    factor = np.float32(1.0 / math.sqrt(length))
    cosines = np.cos(radians) * factor
    sines = np.sin(radians) * factor
    forward = np.stack(
        [np.stack([cosines, -sines], axis=1), np.stack([sines, cosines], axis=1)], axis=0
    )
    inverse = np.stack(
        [np.stack([cosines.T, sines.T], axis=1), np.stack([-sines.T, cosines.T], axis=1)], axis=0
    )
    return forward.astype(BF16), inverse.astype(BF16)


def real_tables(length, modes):
    radians = angles(length, modes, False)
    factor = np.float32(1.0 / math.sqrt(length))
    cosines = np.cos(radians) * factor
    sines = np.sin(radians) * factor
    forward = np.concatenate([cosines, -sines], axis=1)
    doubled = np.where(np.arange(modes) == 0, 1.0, 2.0).astype(np.float32)[None, :]
    inverse = np.concatenate([(cosines * doubled).T, (-sines * doubled).T], axis=0)
    return forward.astype(BF16), inverse.astype(BF16)


def flipped(table):
    return np.transpose(table, (2, 3, 0, 1))


def second_natural(table):
    length = table.shape[1]
    split = table.reshape(2, length, 2, MY // 4, 4)
    return split.transpose(3, 2, 4, 0, 1).reshape(2 * MY, 2 * length)


def second_paired(table):
    length = table.shape[1]
    split = table.reshape(2, length // 2, 2, 2, MY // 4, 4)
    return split.transpose(2, 4, 3, 5, 0, 1).reshape(4 * MY, length)


def second_inverse(table):
    length = table.shape[3]
    split = table.reshape(2, MY // 4, 4, 2, length // 2, 2)
    return split.transpose(3, 4, 5, 1, 0, 2).reshape(length, 4 * MY)


def first_forward(table):
    length, modes = table.shape[1], table.shape[3]
    split = table.reshape(2, length // 2, 2, 2, modes)
    return split.transpose(2, 3, 4, 0, 1).reshape(4 * modes, length)


def first_inverse(table):
    modes, length = table.shape[1], table.shape[3]
    split = table.reshape(2, modes, 2, length // 2, 2)
    return split.transpose(2, 3, 4, 0, 1).reshape(length, 4 * modes)


def twice_diagonal(table):
    zero = np.zeros_like(table)
    return np.block([[table, zero], [zero, table]])


def mm(left, right):
    return lax.dot_general(left, right, (((1,), (0,)), ((), ())), preferred_element_type=F32)


def nt(left, right):
    return lax.dot_general(left, right, (((1,), (1,)), ((), ())), preferred_element_type=F32)


def tn(left, right):
    return lax.dot_general(left, right, (((0,), (0,)), ((), ())), preferred_element_type=F32)


def side(rows):
    return lax.broadcasted_iota(jnp.int32, (rows, LANES), 1) < LANES // 2


def turned(values):
    return pltpu.roll(values, LANES // 2, 1)


def whole(shape):
    return pl.BlockSpec(shape, lambda *_: (0,) * len(shape))


VM = pl.BlockSpec(memory_space=pltpu.VMEM)


GROUPS = 4
ROWS = 2 * LANES * CHANNELS


def near(value):
    return pltpu.with_memory_space_constraint(value, pltpu.VMEM)


def afar(value):
    return pltpu.with_memory_space_constraint(value, pltpu.HBM)


def call(
    kernel, outs, scratch, flops, moved, *operands, big=(), kinds=(), plain=(), token=None
):
    cut = ROWS // GROUPS
    counts = [
        len(operands),
        len(big),
        0 if token is None else 1,
        len(outs),
        len(kinds),
        len(plain),
        len(scratch),
        len(outs),
        len(big),
        len(kinds),
        3,
    ]

    def whole_kernel(*refs):
        parts = []
        at = 0
        for count in counts:
            parts.append(refs[at : at + count])
            at += count
        small, big_far, _, outs_far, kinds_far, plains, own, outs_near, big_near, kinds_near, sems = parts
        in_sem, out_sem, end_sem = sems

        def group_of(far, close, sem, index, group, out):
            rows = pl.ds(pl.multiple_of(group * cut, cut), cut)
            pair = (close.at[rows], far.at[rows]) if out else (far.at[rows], close.at[rows])
            return pltpu.make_async_copy(*pair, sem.at[index, group])

        def coming(index, group):
            return group_of(big_far[index], big_near[index], in_sem, index, group, False)

        def going(index, group):
            return group_of(kinds_far[index], kinds_near[index], out_sem, index, group, True)

        for group in range(GROUPS):
            for index in range(len(big)):
                coming(index, group).start()

        def loop(body, carry=0, unroll=PAIRS // GROUPS):
            per = PAIRS // GROUPS

            def some(i, carry):
                for j in range(unroll):
                    carry = body(i * unroll + j, carry)
                return carry

            def each(group, carry):
                for index in range(len(big)):
                    coming(index, group).wait()
                first = group * (per // unroll)
                carry = lax.fori_loop(first, first + per // unroll, some, carry)
                for index in range(len(kinds)):
                    going(index, group).start()
                return carry

            return lax.fori_loop(0, GROUPS, each, carry)

        kernel(small, big_near, outs_near, kinds_near, plains, own, loop)
        last = [
            pltpu.make_async_copy(close, far, end_sem.at[index])
            for index, (close, far) in enumerate(zip(outs_near, outs_far))
        ]
        for copy in last:
            copy.start()
        for index in range(len(kinds)):
            for group in range(GROUPS):
                going(index, group).wait()
        for copy in last:
            copy.wait()

    operands = [near(operand) for operand in operands]
    far = pl.BlockSpec(memory_space=pl.ANY)
    extra = [] if token is None else [token]
    shapes = [pltpu.HBM(shape, kind) for shape, kind in outs]
    shapes += [pltpu.HBM((ROWS, LANES), kind) for kind in kinds]
    return pl.pallas_call(
        whole_kernel,
        out_shape=shapes + list(plain),
        in_specs=[VM] * len(operands) + [far] * (len(big) + len(extra)),
        out_specs=[far] * len(shapes) + [VM] * len(plain),
        scratch_shapes=list(scratch)
        + [pltpu.VMEM(shape, kind) for shape, kind in outs]
        + [pltpu.VMEM((ROWS, LANES), array.dtype) for array in big]
        + [pltpu.VMEM((ROWS, LANES), kind) for kind in kinds]
        + [
            pltpu.SemaphoreType.DMA((max(len(big), 1), GROUPS)),
            pltpu.SemaphoreType.DMA((max(len(kinds), 1), GROUPS)),
            pltpu.SemaphoreType.DMA((max(len(outs), 1),)),
        ],
        cost_estimate=pl.CostEstimate(flops=flops, bytes_accessed=moved, transcendentals=0),
        compiler_params=pltpu.CompilerParams(vmem_limit_bytes=VMEM_LIMIT),
    )(*operands, *[afar(array) for array in (*big, *extra)])


C_STEP = 8


def spectrum_kernel(field, third_far, second_far, out_far, near_field, third_ref, second_ref, chunk, spec, sems, extra):
    def coming(step):
        cut = pl.ds(step * C_STEP, C_STEP)
        return pltpu.make_async_copy(field.at[0, cut], near_field.at[cut], sems.at[step])

    tables = [
        pltpu.make_async_copy(third_far, third_ref, extra.at[0]),
        pltpu.make_async_copy(second_far, second_ref, extra.at[1]),
    ]
    for copy in tables:
        copy.start()
    for step in range(CHANNELS // C_STEP):
        coming(step).start()
    for copy in tables:
        copy.wait()
    third = third_ref[...]

    def some(step, carry):
        coming(step).wait()
        for x in range(2):
            rows = near_field[pl.ds(step * C_STEP, C_STEP), x].reshape(C_STEP * LANES, LANES)
            done = nt(third, rows)
            for c in range(C_STEP):
                place = pl.multiple_of((x * CHANNELS + step * C_STEP + c) * 2 * MZ, 2 * MZ)
                spec[pl.ds(place, 2 * MZ), :] = done[:, c * LANES : (c + 1) * LANES]
        return carry

    lax.fori_loop(0, CHANNELS // C_STEP, some, 0)
    second = second_ref[...]
    for k in range(MZ):
        real = spec[pl.ds(k, LANES, stride=2 * MZ), :]
        imag = spec[pl.ds(MZ + k, LANES, stride=2 * MZ), :]
        both = jnp.concatenate([real, imag], axis=1).astype(BF16)
        chunk[k * 32 : (k + 1) * 32, :] = nt(second, both).astype(BF16)
    out = pltpu.make_async_copy(chunk, out_far, extra.at[2])
    out.start()
    out.wait()


def first_partial(field, third, second):
    far = pl.BlockSpec(memory_space=pl.ANY)
    return pl.pallas_call(
        spectrum_kernel,
        out_shape=pltpu.HBM((512, LANES), BF16),
        in_specs=[far] * 3,
        out_specs=far,
        scratch_shapes=[
            pltpu.VMEM(field.shape[1:], BF16),
            pltpu.VMEM(third.shape, BF16),
            pltpu.VMEM(second.shape, BF16),
            pltpu.VMEM((512, LANES), BF16),
            pltpu.VMEM((4096, LANES), F32),
            pltpu.SemaphoreType.DMA((CHANNELS // C_STEP,)),
            pltpu.SemaphoreType.DMA((3,)),
        ],
        cost_estimate=pl.CostEstimate(
            flops=600_000_000, bytes_accessed=6 << 20, transcendentals=0
        ),
        compiler_params=pltpu.CompilerParams(vmem_limit_bytes=VMEM_LIMIT),
    )(afar(field), afar(third), afar(second))


Y_STEP = 16
Y_STEPS = LANES // Y_STEP
Y_ROWS = Y_STEP * CHANNELS


def relay_kernel(field, _, out_far, near_field, out_near, rows_ref, in_sem, out_sem):
    def coming(step):
        x = step // Y_STEPS
        cut = pl.ds(pl.multiple_of((step % Y_STEPS) * Y_STEP, Y_STEP), Y_STEP)
        return pltpu.make_async_copy(
            field.at[0, :, x, cut], near_field.at[:, x, cut], in_sem.at[step]
        )

    def going(step):
        cut = pl.ds(pl.multiple_of(step * Y_ROWS, Y_ROWS), Y_ROWS)
        return pltpu.make_async_copy(out_near.at[cut], out_far.at[cut], out_sem.at[step])

    for step in range(2 * Y_STEPS):
        coming(step).start()

    def some(step, carry):
        coming(step).wait()
        at = pl.multiple_of((step % Y_STEPS) * Y_STEP, Y_STEP)
        rows_ref[...] = (
            near_field[:, step // Y_STEPS, pl.ds(at, Y_STEP), :].astype(F32).reshape(Y_ROWS, LANES)
        )
        for y in range(0, Y_STEP, 2):
            pair = [rows_ref[pl.ds(y + e, CHANNELS, stride=Y_STEP), :] for e in range(2)]
            tile = step * (Y_STEP // 2) + y // 2
            out_near[tile_at(tile), :] = jnp.concatenate(pair, axis=0).astype(BF16)
        going(step).start()
        return carry

    lax.fori_loop(0, 2 * Y_STEPS, some, 0)
    for step in range(2 * Y_STEPS):
        going(step).wait()


def relay(field, token):
    far = pl.BlockSpec(memory_space=pl.ANY)
    return pl.pallas_call(
        relay_kernel,
        out_shape=pltpu.HBM((ROWS, LANES), BF16),
        in_specs=[far] * 2,
        out_specs=far,
        scratch_shapes=[
            pltpu.VMEM(field.shape[1:], BF16),
            pltpu.VMEM((ROWS, LANES), BF16),
            pltpu.VMEM((Y_ROWS, LANES), F32),
            pltpu.SemaphoreType.DMA((2 * Y_STEPS,)),
            pltpu.SemaphoreType.DMA((2 * Y_STEPS,)),
        ],
        cost_estimate=pl.CostEstimate(
            flops=600_000_000, bytes_accessed=12 << 20, transcendentals=0
        ),
        compiler_params=pltpu.CompilerParams(vmem_limit_bytes=VMEM_LIMIT),
    )(afar(field), afar(token))


def own_spectrum(wide, table, place, block=8):
    real = wide[pl.ds(place, 64, stride=block), :]
    imag = wide[pl.ds(4 + place, 64, stride=block), :]
    both = mm(table, jnp.concatenate([real, imag], axis=0).astype(BF16))
    return both[:32, :CHANNELS] + both[32:, CHANNELS:]


def send_field(mixed, table, place, sent, block=8):
    twin = jnp.concatenate([mixed, mixed], axis=1)
    left = side(32)
    both = jnp.concatenate([jnp.where(left, twin, 0.0), jnp.where(left, 0.0, twin)], axis=0)
    out = mm(table, both.astype(BF16))
    sent[pl.ds(place, 64, stride=block), :] = out[:64]
    sent[pl.ds(4 + place, 64, stride=block), :] = out[64:]


def mode_lanes(modes):
    row = lax.broadcasted_iota(jnp.int32, (32, LANES), 0) % modes
    half = lax.broadcasted_iota(jnp.int32, (32, LANES), 1) // CHANNELS
    return row, half


def mix_kernel(small, _, outs, __, ___, scratch, loop):
    got_ref, weight_ref, forward_ref, inverse_ref = small
    out_ref, spec_ref = outs
    wide, sent = scratch
    wide[...] = got_ref[...].astype(F32)
    forward = forward_ref[...]
    inverse = inverse_ref[...]
    modes = weight_ref.shape[1]
    row, half = mode_lanes(modes)
    for p in range(4):
        spec = own_spectrum(wide, forward, p).astype(BF16)
        spec_ref[:, p * CHANNELS : (p + 1) * CHANNELS] = spec
        spec = spec.astype(F32)
        other = jnp.concatenate([-spec[modes:], spec[:modes]], axis=0)
        pieces = []
        for part in (spec, other):
            twin = jnp.concatenate([part, part], axis=1)
            for pair in range(modes // 2):
                pieces.append(jnp.where(row == 2 * pair + half, twin, 0.0).astype(BF16))
        spread = jnp.concatenate(pieces, axis=1)
        weights = weight_ref[:, :, p].reshape(2 * modes * CHANNELS, CHANNELS)
        mixed = mm(spread, weights).astype(BF16).astype(F32)
        send_field(mixed, inverse, p, sent)
    out_ref[...] = sent[...].astype(BF16)


def high_low(values):
    high = values.astype(BF16).astype(F32)
    return jnp.concatenate([high, values - high], axis=1)


def unmix_kernel(small, _, outs, __, ___, scratch, loop):
    got_ref, weight_ref, forward_ref, inverse_ref, term_ref, one_ref, two_ref = small
    out_ref, spec_ref = outs
    wide, sent = scratch
    wide[...] = got_ref[...].astype(F32)
    forward = forward_ref[...]
    inverse = inverse_ref[...]
    modes = weight_ref.shape[1]
    row, half = mode_lanes(modes)
    spec_ref[0:32, :] = one_ref[...]
    spec_ref[32:64, :] = two_ref[...]
    sent[...] = jnp.zeros_like(sent)
    terms = high_low(term_ref[...])
    sent[pl.ds(8, 64, stride=16), :] = terms[:CHANNELS]
    sent[pl.ds(9, 64, stride=16), :] = jnp.broadcast_to(
        terms[CHANNELS : CHANNELS + 1], (CHANNELS, LANES)
    )
    for p in range(4):
        spec = own_spectrum(wide, forward, p).astype(BF16)
        spec_ref[64:96, p * CHANNELS : (p + 1) * CHANNELS] = spec
        other = jnp.concatenate([spec[modes:].astype(F32), -spec[:modes].astype(F32)], axis=0)
        products = nt(spec, weight_ref[0, :, p].reshape(modes * CHANNELS, CHANNELS)) + nt(
            other.astype(BF16), weight_ref[1, :, p].reshape(modes * CHANNELS, CHANNELS)
        )
        total = jnp.zeros((32, LANES), F32)
        for pair in range(modes // 2):
            piece = products[:, pair * LANES : (pair + 1) * LANES]
            total = total + jnp.where(row == 2 * pair + half, piece, 0.0)
        mixed = (total + turned(total))[:, :CHANNELS].astype(BF16).astype(F32)
        send_field(mixed, inverse, p, sent, 16)
    out_ref[...] = sent[...].astype(BF16)


def last_kernel(small, _, outs, __, ___, scratch, loop):
    got_ref, forward_ref = small
    (out_ref,) = outs
    (wide,) = scratch
    for d in range(64):
        wide[d * 48 : (d + 1) * 48, :] = got_ref[d * 48 : (d + 1) * 48, :].astype(F32)
    forward = forward_ref[...]
    for p in range(4):
        out_ref[0:32, p * CHANNELS : (p + 1) * CHANNELS] = own_spectrum(
            wide, forward, p, 48
        ).astype(BF16)
    total = jnp.zeros((40, LANES), F32)
    for d in range(64):
        total = total + wide[d * 48 + 8 : (d + 1) * 48, :]
    high = total.astype(BF16)
    low = (total - high.astype(F32)).astype(BF16)
    out_ref[32:64, :] = jnp.concatenate([high[:32], low[:32]], axis=1)
    rows = wide[pl.ds(41, 64, stride=48), :]
    out_ref[64:96, :] = jnp.concatenate([rows[:32], rows[32:]], axis=1).astype(BF16)
    biases = jnp.concatenate(
        [
            high_low(total[32:40, :CHANNELS]),
            jnp.broadcast_to(wide[42:43, :], (8, LANES)),
        ],
        axis=1,
    )
    out_ref[96:112, :] = jnp.concatenate([biases, biases], axis=0).astype(BF16)


CHUNK = ((512, LANES), BF16)
SPECTRUM = ((32, 4 * CHANNELS), BF16)
WIDE = pltpu.VMEM((512, LANES), F32)


def mixing(got, weights, forward, inverse, token):
    return call(
        mix_kernel,
        [CHUNK, SPECTRUM],
        [WIDE, WIDE],
        200_000_000,
        3 << 20,
        got,
        weights,
        forward,
        inverse,
        token=token,
    )


def outer_products(spec, grad, out_ref):
    modes = out_ref.shape[1]
    depth = spec.shape[0]
    lane = lax.broadcasted_iota(jnp.int32, (CHANNELS, depth), 1) % modes
    other = []
    for n in range(depth // (2 * modes)):
        at = n * 2 * modes
        other += [grad[at + modes : at + 2 * modes], -grad[at : at + modes]]
    other = jnp.concatenate(other, axis=0)
    for p in range(4):
        cut = slice(p * CHANNELS, (p + 1) * CHANNELS)
        both = jnp.concatenate([grad[:, cut], other[:, cut]], axis=1).astype(BF16)
        tall = spec[:, cut].T
        for m in range(modes):
            out = mm(jnp.where(lane == m, tall, 0.0).astype(BF16), both).astype(BF16)
            out_ref[0, m, p] = out[:, :CHANNELS]
            out_ref[1, m, p] = out[:, CHANNELS:]


def rows_of(ref, step, at):
    count = ref.shape[0] // step
    return jnp.concatenate(
        [ref[n * step + at : n * step + at + 32, :] for n in range(count)], axis=0
    ).astype(F32)


def weight_two_kernel(small, _, __, ___, plain, scratch, loop):
    (all_ref,) = small
    (out_ref,) = plain
    outer_products(rows_of(all_ref, 96, 32), rows_of(all_ref, 96, 64), out_ref)


def weight_one_kernel(factor, small, _, __, ___, plain, scratch, loop):
    early_ref, all_ref = small
    out_ref, one_ref, two_ref, bias_one_ref, bias_two_ref = plain
    sums = all_ref[32:112, :].astype(F32)
    for n in range(1, all_ref.shape[0] // 112):
        sums = sums + all_ref[n * 112 + 32 : (n + 1) * 112, :].astype(F32)
    sums = sums * factor
    one = sums[:32, :LANES] + sums[:32, LANES:]
    one_ref[0:32, :] = one[:, :CHANNELS]
    one_ref[32:64, :] = one[:, CHANNELS:]
    two = jnp.concatenate([sums[32:64, :LANES], sums[32:64, LANES:]], axis=0)
    two_ref[...] = (two + turned(two))[:, :CHANNELS]
    bias = jnp.concatenate([sums[64:72, :LANES], sums[64:72, LANES:]], axis=0)
    bias = bias + turned(bias)
    bias_one_ref[...] = bias[0:1, :CHANNELS]
    bias_two_ref[...] = bias[8:9, :CHANNELS]
    outer_products(rows_of(early_ref, 96, 0), rows_of(all_ref, 112, 0), out_ref)


TILES = 128
PAIRS = TILES // 2
TILE = 2 * CHANNELS


def unpack_modes(got_ref, second_ref, depth, block=8):
    second = second_ref[...]
    left = side(32)
    for k in range(MZ):
        near = jnp.concatenate(
            [got_ref[d * block : d * block + 8, :] for d in range(k * 4, k * 4 + 4)], axis=0
        ) if block > 8 else got_ref[k * 32 : (k + 1) * 32, :].astype(F32)
        far = turned(near)
        top = jnp.concatenate([jnp.where(left, near, 0.0), jnp.where(left, far, 0.0)], axis=1)
        low = jnp.concatenate([jnp.where(left, 0.0, far), jnp.where(left, 0.0, near)], axis=1)
        out = mm(second, jnp.concatenate([top, low], axis=0).astype(BF16))
        for x in range(2):
            cut = slice(x * LANES, (x + 1) * LANES)
            depth[pl.ds(x * 2048 + k, 64, stride=32), :] = out[:64, cut]
            depth[pl.ds(x * 2048 + MZ + k, 64, stride=32), :] = out[64:, cut]


def pack_modes(spec, second_ref, out_ref, block=8):
    second = second_ref[...]
    left = side(32)
    for k in range(MZ):
        planes = [
            jnp.concatenate(
                [
                    spec[pl.ds(x * 2048 + k, 64, stride=32), :],
                    spec[pl.ds(x * 2048 + MZ + k, 64, stride=32), :],
                ],
                axis=0,
            )
            for x in range(2)
        ]
        out = mm(second, jnp.concatenate(planes, axis=1).astype(BF16))
        near, far = out[:, :LANES], out[:, LANES:]
        packed = jnp.where(left, near[:32] + turned(near[32:]), turned(far[:32]) + far[32:])
        if block == 8:
            out_ref[k * 32 : (k + 1) * 32, :] = packed.astype(out_ref.dtype)
        else:
            for d in range(4):
                at = (k * 4 + d) * block
                out_ref[at : at + 8, :] = packed[d * 8 : (d + 1) * 8]


def branch_of(depth, third, pair):
    at = pl.multiple_of(pair * 64, 64)
    wide = tn(depth[pl.ds(at, 64), :].astype(BF16), third)
    return wide[:, :LANES], wide[:, LANES:]


def store_spectrum(spec, third, pair, first, second):
    done = nt(third, jnp.concatenate([first, second], axis=0))
    at = pl.multiple_of(pair * 64, 64)
    spec[pl.ds(at, 32), :] = done[:, :LANES]
    spec[pl.ds(at + 32, 32), :] = done[:, LANES:]


def tile_at(tile):
    return pl.ds(pl.multiple_of(tile * TILE, TILE), TILE)


def gelu(preact):
    inner = preact * (ROOT + (ROOT * CUBIC) * (preact * preact))
    halved = 0.5 * preact
    return halved + halved * jnp.tanh(inner)


def gelu_slope(preact):
    square = preact * preact
    tangent = jnp.tanh(preact * (ROOT + (ROOT * CUBIC) * square))
    steep = (0.5 * preact) * (ROOT + (3.0 * ROOT * CUBIC) * square)
    return 0.5 + 0.5 * tangent + steep * (1.0 - tangent * tangent)


def hidden_kernel(small, big, outs, kinds, _, scratch, loop):
    got, inv2, inv3, fwd3, fwd2 = small
    (base,) = big
    hidden, preact = kinds
    depth, spec = scratch
    unpack_modes(got, inv2, depth)
    third_back = inv3[...]
    third = fwd3[...]

    def body(pair, carry):
        made = []
        for e, branch in enumerate(branch_of(depth, third_back, pair)):
            at = tile_at(2 * pair + e)
            pre = base[at, :].astype(F32) + branch
            preact[at, :] = pre.astype(BF16)
            value = gelu(pre).astype(BF16)
            hidden[at, :] = value
            made.append(value)
        store_spectrum(spec, third, pair, *made)
        return carry

    loop(body)
    pack_modes(spec, fwd2, outs[0])


def grad_two_kernel(small, big, outs, kinds, _, scratch, loop):
    got, inv2, inv3, fwd3, fwd2 = small
    base, cot = big
    (grad,) = kinds
    depth, spec = scratch
    unpack_modes(got, inv2, depth)
    third_back = inv3[...]
    third = fwd3[...]

    def body(pair, carry):
        made = []
        for e, branch in enumerate(branch_of(depth, third_back, pair)):
            at = tile_at(2 * pair + e)
            slope = gelu_slope(base[at, :].astype(F32) + branch)
            value = (cot[at, :].astype(F32) * slope).astype(BF16)
            grad[at, :] = value
            made.append(value)
        store_spectrum(spec, third, pair, *made)
        return carry

    loop(body)
    pack_modes(spec, fwd2, outs[0])


def grad_one_kernel(small, big, outs, _, __, scratch, loop):
    got, inv2, inv3, fwd3, fwd2 = small
    base, slope, values = big
    (out,) = outs
    depth, spec, wide, sent = scratch
    wide[...] = got[...].astype(F32)
    unpack_modes(wide, inv2, depth, 16)
    third_back = inv3[...]
    third = fwd3[...]
    ones = jnp.ones((16, 4 * LANES), BF16)

    def body(pair, total):
        made = []
        for e, branch in enumerate(branch_of(depth, third_back, pair)):
            at = tile_at(2 * pair + e)
            back = base[at, :].astype(F32) + branch
            made.append((back * slope[at, :].astype(F32)).astype(BF16))
        store_spectrum(spec, third, pair, *made)
        left = jnp.concatenate(
            [wide_tile(values, 2 * pair), wide_tile(values, 2 * pair + 1)], axis=1
        )
        right = jnp.concatenate(
            [part for tile in made for part in (tile[:CHANNELS], tile[CHANNELS:])], axis=1
        )
        return total + nt(jnp.concatenate([left, ones], axis=0), right)

    total = loop(body, jnp.zeros((CHANNELS + 16, CHANNELS), F32))
    pack_modes(spec, fwd2, sent, 48)
    left = side(1)

    def arrived_sum(place):
        row = jnp.sum(wide[pl.ds(place, 64, stride=16), :], axis=0, keepdims=True)
        row = row + turned(row)
        high = row.astype(BF16).astype(F32)
        return jnp.where(left, high, row - high)

    bias = jnp.concatenate([total[64:65], total[64:65]], axis=1)
    terms = jnp.concatenate(
        [
            jnp.concatenate([total[:32], total[32:64]], axis=1),
            bias,
            arrived_sum(8),
            arrived_sum(9),
            jnp.zeros((5, LANES), F32),
        ],
        axis=0,
    )
    for d in range(64):
        sent[d * 48 + 8 : (d + 1) * 48, :] = terms
    for d in range(64):
        out[d * 48 : (d + 1) * 48, :] = sent[d * 48 : (d + 1) * 48, :].astype(BF16)


def planes(kernel, kinds, *operands, big, token):
    scratch = [pltpu.VMEM((4096, LANES), F32), pltpu.VMEM((4096, LANES), F32)]
    return call(
        kernel,
        [CHUNK],
        scratch,
        1_000_000_000,
        20 << 20,
        *operands,
        big=big,
        kinds=kinds,
        token=token,
    )


def wide_tile(ref, tile):
    at = pl.multiple_of(tile * TILE, TILE)
    return jnp.concatenate(
        [ref[pl.ds(at, CHANNELS), :], ref[pl.ds(at + CHANNELS, CHANNELS), :]], axis=1
    )


def store_wide(ref, tile, wide):
    at = pl.multiple_of(tile * TILE, TILE)
    ref[pl.ds(at, CHANNELS), :] = wide[:, :LANES].astype(BF16)
    ref[pl.ds(at + CHANNELS, CHANNELS), :] = wide[:, LANES:].astype(BF16)


def point_kernel(small, big, _, kinds, __, scratch, loop):
    point, bias = small
    weights = point[...]
    shift = jnp.concatenate([bias[...], bias[...]], axis=1)

    def body(pair, carry):
        for tile in (2 * pair, 2 * pair + 1):
            store_wide(kinds[0], tile, mm(weights, wide_tile(big[0], tile)) + shift)
        return carry

    loop(body)


def slope_kernel(small, big, _, kinds, __, scratch, loop):
    def body(pair, carry):
        for tile in (2 * pair, 2 * pair + 1):
            at = tile_at(tile)
            kinds[0][at, :] = gelu_slope(big[0][at, :].astype(F32)).astype(BF16)
        return carry

    loop(body)


def point_back_kernel(small, big, outs, kinds, _, scratch, loop):
    weights = small[0][...]
    hidden, grad = big
    ones = jnp.ones((16, 4 * LANES), BF16)

    def body(pair, total):
        right = [wide_tile(grad, 2 * pair + e) for e in range(2)]
        for e in range(2):
            store_wide(kinds[0], 2 * pair + e, mm(weights, right[e]))
        left = jnp.concatenate(
            [wide_tile(hidden, 2 * pair), wide_tile(hidden, 2 * pair + 1)], axis=1
        )
        return total + nt(
            jnp.concatenate([left, ones], axis=0), jnp.concatenate(right, axis=1)
        )

    outs[0][...] = loop(body, jnp.zeros((CHANNELS + 16, CHANNELS), F32))


def body(field_in, cotangent, spectral_one, spectral_two, point_one, point_two, bias_one, bias_two):
    forward_c, inverse_c = complex_tables(LANES, MY)
    forward_z, inverse_z = real_tables(LANES, MZ)
    shape = spectral_one.shape
    const = lambda table: jnp.asarray(np.ascontiguousarray(table))

    natural_second = const(second_natural(forward_c))
    third_forward = const(forward_z.T)
    third_adjoint = const(inverse_z)
    third_inverse = const(twice_diagonal(inverse_z))
    third_back = const(twice_diagonal(forward_z.T))
    second_fwd = const(second_paired(forward_c))
    second_adj = const(second_paired(flipped(inverse_c)))
    second_inv = const(second_inverse(inverse_c))
    second_back = const(second_inverse(flipped(forward_c)))
    first_fwd = const(first_forward(forward_c))
    first_adj = const(first_forward(flipped(inverse_c)))
    first_inv = const(first_inverse(inverse_c))
    first_back = const(first_inverse(flipped(forward_c)))

    def exchange(chunk):
        return lax.all_to_all(chunk, "space", split_axis=0, concat_axis=0, tiled=True)

    def point_map(values, point, bias, token):
        return call(
            point_kernel,
            [],
            [],
            500_000_000,
            12 << 20,
            point.T,
            spread(bias),
            big=[values],
            kinds=[BF16],
            token=token,
        )[0]

    def samples(spectrum):
        return lax.all_gather(spectrum, "dp", axis=0, tiled=True)

    spread = lambda bias: jnp.broadcast_to(bias[:, None], (CHANNELS, LANES))

    chunk = first_partial(field_in, third_forward, natural_second)
    got = exchange(chunk)
    values = relay(field_in, chunk)

    chunk, spec_one = mixing(got, spectral_one, first_fwd, first_inv, token=values)
    got = exchange(chunk)
    base = point_map(values, point_one, bias_one, chunk)

    chunk, hidden, preact = planes(
        hidden_kernel,
        [BF16, BF16],
        got,
        second_inv,
        third_inverse,
        third_forward,
        second_fwd,
        big=[base],
        token=spec_one,
    )
    got = exchange(chunk)
    base = point_map(hidden, point_two, bias_two, chunk)

    chunk, spec_two = mixing(got, spectral_two, first_fwd, first_inv, token=base)
    got = exchange(chunk)
    cot = relay(cotangent, chunk)

    chunk, grad_two = planes(
        grad_two_kernel,
        [BF16],
        got,
        second_inv,
        third_inverse,
        third_adjoint,
        second_adj,
        big=[base, cot],
        token=spec_two,
    )
    got = exchange(chunk)
    term_two, base = call(
        point_back_kernel,
        [((CHANNELS + 16, CHANNELS), F32)],
        [],
        1_000_000_000,
        12 << 20,
        point_two,
        big=[hidden, grad_two],
        kinds=[BF16],
    )

    chunk, early = call(
        unmix_kernel,
        [((1024, LANES), BF16), ((96, 4 * CHANNELS), BF16)],
        [WIDE, pltpu.VMEM((1024, LANES), F32)],
        200_000_000,
        3 << 20,
        got,
        spectral_two,
        first_adj,
        first_back,
        term_two,
        spec_one,
        spec_two,
    )
    got = exchange(chunk)
    early = samples(early)
    slope = call(
        slope_kernel, [], [], 500_000_000, 12 << 20, big=[preact], kinds=[BF16], token=chunk
    )[0]

    chunk = call(
        grad_one_kernel,
        [((3072, LANES), BF16)],
        [
            pltpu.VMEM((4096, LANES), F32),
            pltpu.VMEM((4096, LANES), F32),
            pltpu.VMEM((1024, LANES), F32),
            pltpu.VMEM((3072, LANES), F32),
        ],
        1_500_000_000,
        20 << 20,
        got,
        second_back,
        third_back,
        third_adjoint,
        second_adj,
        big=[base, slope, values],
        token=early,
    )[0]
    got = exchange(chunk)
    late = call(
        last_kernel,
        [((112, 4 * CHANNELS), BF16)],
        [pltpu.VMEM((3072, LANES), F32)],
        50_000_000,
        1 << 20,
        got,
        first_adj,
    )[0]
    spectral_grad_two = call(
        weight_two_kernel,
        [],
        [],
        200_000_000,
        3 << 20,
        early,
        plain=[jax.ShapeDtypeStruct(shape, BF16)],
        token=late,
    )[0]
    late = samples(late)
    cells = lax.axis_size("dp") * lax.axis_size("space") * 2 * LANES * LANES
    square = jax.ShapeDtypeStruct((CHANNELS, CHANNELS), F32)
    line = jax.ShapeDtypeStruct((1, CHANNELS), F32)
    spectral_grad_one, point_grad_one, point_grad_two, bias_grad_one, bias_grad_two = call(
        functools.partial(weight_one_kernel, 1.0 / math.sqrt(cells)),
        [],
        [],
        200_000_000,
        3 << 20,
        early,
        late,
        plain=[
            jax.ShapeDtypeStruct(shape, BF16),
            square,
            square,
            line,
            line,
        ],
        token=spectral_grad_two,
    )
    return (
        spectral_grad_one,
        spectral_grad_two,
        point_grad_one,
        point_grad_two,
        bias_grad_one.reshape(CHANNELS),
        bias_grad_two.reshape(CHANNELS),
    )


def solution(mesh):
    field = P("dp", None, "space", None, None)
    modes = P(None, None, "space", None, None)
    return jax.shard_map(
        body,
        mesh=mesh,
        in_specs=(field, field, modes, modes, P(), P(), P(), P()),
        out_specs=(modes, modes, P(), P(), P(), P()),
        check_vma=False,
    )
```

```python
import functools
import math

import jax
import jax.numpy as jnp
import numpy as np
from jax import lax
from jax.experimental import pallas as pl
from jax.experimental.pallas import tpu as pltpu
from jax.sharding import PartitionSpec as P

MY = 16
MZ = 16
CHANNELS = 64
LANES = 128
ROOT = math.sqrt(2.0 / math.pi)
CUBIC = 0.044715
F32 = jnp.float32
BF16 = jnp.bfloat16
VMEM_LIMIT = 44 * 1024 * 1024


def angles(length, modes, two_sided):
    places = np.arange(length, dtype=np.int64)[:, None]
    orders = np.arange(modes, dtype=np.int64)[None, :]
    if two_sided:
        orders = np.where(orders < modes // 2, orders, orders - modes + length)
    phases = places * orders % length
    return np.float32(2.0 * math.pi / length) * phases.astype(np.float32)


def complex_tables(length, modes):
    radians = angles(length, modes, True)
    factor = np.float32(1.0 / math.sqrt(length))
    cosines = np.cos(radians) * factor
    sines = np.sin(radians) * factor
    forward = np.stack(
        [np.stack([cosines, -sines], axis=1), np.stack([sines, cosines], axis=1)], axis=0
    )
    inverse = np.stack(
        [np.stack([cosines.T, sines.T], axis=1), np.stack([-sines.T, cosines.T], axis=1)], axis=0
    )
    return forward.astype(BF16), inverse.astype(BF16)


def real_tables(length, modes):
    radians = angles(length, modes, False)
    factor = np.float32(1.0 / math.sqrt(length))
    cosines = np.cos(radians) * factor
    sines = np.sin(radians) * factor
    forward = np.concatenate([cosines, -sines], axis=1)
    doubled = np.where(np.arange(modes) == 0, 1.0, 2.0).astype(np.float32)[None, :]
    inverse = np.concatenate([(cosines * doubled).T, (-sines * doubled).T], axis=0)
    return forward.astype(BF16), inverse.astype(BF16)


def flipped(table):
    return np.transpose(table, (2, 3, 0, 1))


def second_natural(table):
    length = table.shape[1]
    split = table.reshape(2, length, 2, MY // 4, 4)
    return split.transpose(3, 2, 4, 0, 1).reshape(2 * MY, 2 * length)


def second_paired(table):
    length = table.shape[1]
    split = table.reshape(2, length // 2, 2, 2, MY // 4, 4)
    return split.transpose(2, 4, 3, 5, 0, 1).reshape(4 * MY, length)


def second_inverse(table):
    length = table.shape[3]
    split = table.reshape(2, MY // 4, 4, 2, length // 2, 2)
    return split.transpose(3, 4, 5, 1, 0, 2).reshape(length, 4 * MY)


def first_forward(table):
    length, modes = table.shape[1], table.shape[3]
    split = table.reshape(2, length // 2, 2, 2, modes)
    return split.transpose(2, 3, 4, 0, 1).reshape(4 * modes, length)


def first_inverse(table):
    modes, length = table.shape[1], table.shape[3]
    split = table.reshape(2, modes, 2, length // 2, 2)
    return split.transpose(2, 3, 4, 0, 1).reshape(length, 4 * modes)


def twice_diagonal(table):
    zero = np.zeros_like(table)
    return np.block([[table, zero], [zero, table]])


def mm(left, right):
    return lax.dot_general(left, right, (((1,), (0,)), ((), ())), preferred_element_type=F32)


def nt(left, right):
    return lax.dot_general(left, right, (((1,), (1,)), ((), ())), preferred_element_type=F32)


def tn(left, right):
    return lax.dot_general(left, right, (((0,), (0,)), ((), ())), preferred_element_type=F32)


def side(rows):
    return lax.broadcasted_iota(jnp.int32, (rows, LANES), 1) < LANES // 2


def turned(values):
    return pltpu.roll(values, LANES // 2, 1)


def whole(shape):
    return pl.BlockSpec(shape, lambda *_: (0,) * len(shape))


VM = pl.BlockSpec(memory_space=pltpu.VMEM)


GROUPS = 4
ROWS = 2 * LANES * CHANNELS


def near(value):
    return pltpu.with_memory_space_constraint(value, pltpu.VMEM)


def afar(value):
    return pltpu.with_memory_space_constraint(value, pltpu.HBM)


def call(
    kernel, outs, scratch, flops, moved, *operands, big=(), kinds=(), plain=(), token=None
):
    cut = ROWS // GROUPS
    extra = [] if token is None else list(token) if isinstance(token, list) else [token]
    counts = [
        len(operands),
        len(big),
        len(extra),
        len(outs),
        len(kinds),
        len(plain),
        len(scratch),
        len(outs),
        len(big),
        len(kinds),
        3,
    ]

    def whole_kernel(*refs):
        parts = []
        at = 0
        for count in counts:
            parts.append(refs[at : at + count])
            at += count
        small, big_far, _, outs_far, kinds_far, plains, own, outs_near, big_near, kinds_near, sems = parts
        in_sem, out_sem, end_sem = sems

        def group_of(far, close, sem, index, group, out):
            rows = pl.ds(pl.multiple_of(group * cut, cut), cut)
            pair = (close.at[rows], far.at[rows]) if out else (far.at[rows], close.at[rows])
            return pltpu.make_async_copy(*pair, sem.at[index, group])

        def coming(index, group):
            return group_of(big_far[index], big_near[index], in_sem, index, group, False)

        def going(index, group):
            return group_of(kinds_far[index], kinds_near[index], out_sem, index, group, True)

        for group in range(GROUPS):
            for index in range(len(big)):
                coming(index, group).start()

        def loop(body, carry=0, unroll=PAIRS // GROUPS):
            per = PAIRS // GROUPS

            def some(i, carry):
                for j in range(unroll):
                    carry = body(i * unroll + j, carry)
                return carry

            def each(group, carry):
                for index in range(len(big)):
                    coming(index, group).wait()
                first = group * (per // unroll)
                carry = lax.fori_loop(first, first + per // unroll, some, carry)
                for index in range(len(kinds)):
                    going(index, group).start()
                return carry

            return lax.fori_loop(0, GROUPS, each, carry)

        kernel(small, big_near, outs_near, kinds_near, plains, own, loop)
        last = [
            pltpu.make_async_copy(close, far, end_sem.at[index])
            for index, (close, far) in enumerate(zip(outs_near, outs_far))
        ]
        for copy in last:
            copy.start()
        for index in range(len(kinds)):
            for group in range(GROUPS):
                going(index, group).wait()
        for copy in last:
            copy.wait()

    operands = [near(operand) for operand in operands]
    far = pl.BlockSpec(memory_space=pl.ANY)
    shapes = [pltpu.HBM(shape, kind) for shape, kind in outs]
    shapes += [pltpu.HBM((ROWS, LANES), kind) for kind in kinds]
    return pl.pallas_call(
        whole_kernel,
        out_shape=shapes + list(plain),
        in_specs=[VM] * len(operands) + [far] * (len(big) + len(extra)),
        out_specs=[far] * len(shapes) + [VM] * len(plain),
        scratch_shapes=list(scratch)
        + [pltpu.VMEM(shape, kind) for shape, kind in outs]
        + [pltpu.VMEM((ROWS, LANES), array.dtype) for array in big]
        + [pltpu.VMEM((ROWS, LANES), kind) for kind in kinds]
        + [
            pltpu.SemaphoreType.DMA((max(len(big), 1), GROUPS)),
            pltpu.SemaphoreType.DMA((max(len(kinds), 1), GROUPS)),
            pltpu.SemaphoreType.DMA((max(len(outs), 1),)),
        ],
        cost_estimate=pl.CostEstimate(flops=flops, bytes_accessed=moved, transcendentals=0),
        compiler_params=pltpu.CompilerParams(vmem_limit_bytes=VMEM_LIMIT),
    )(*operands, *[afar(array) for array in (*big, *extra)])


C_STEP = 8


def spectrum_kernel(field, third_far, second_far, out_far, near_field, third_ref, second_ref, chunk, spec, sems, extra):
    def coming(step):
        cut = pl.ds(step * C_STEP, C_STEP)
        return pltpu.make_async_copy(field.at[0, cut], near_field.at[cut], sems.at[step])

    tables = [
        pltpu.make_async_copy(third_far, third_ref, extra.at[0]),
        pltpu.make_async_copy(second_far, second_ref, extra.at[1]),
    ]
    for copy in tables:
        copy.start()
    for step in range(CHANNELS // C_STEP):
        coming(step).start()
    for copy in tables:
        copy.wait()
    third = third_ref[...]

    def some(step, carry):
        coming(step).wait()
        for x in range(2):
            rows = near_field[pl.ds(step * C_STEP, C_STEP), x].reshape(C_STEP * LANES, LANES)
            done = nt(third, rows)
            for c in range(C_STEP):
                place = pl.multiple_of((x * CHANNELS + step * C_STEP + c) * 2 * MZ, 2 * MZ)
                spec[pl.ds(place, 2 * MZ), :] = done[:, c * LANES : (c + 1) * LANES]
        return carry

    lax.fori_loop(0, CHANNELS // C_STEP, some, 0)
    second = second_ref[...]
    for k in range(MZ):
        real = spec[pl.ds(k, LANES, stride=2 * MZ), :]
        imag = spec[pl.ds(MZ + k, LANES, stride=2 * MZ), :]
        both = jnp.concatenate([real, imag], axis=1).astype(BF16)
        chunk[k * 32 : (k + 1) * 32, :] = nt(second, both).astype(BF16)
    out = pltpu.make_async_copy(chunk, out_far, extra.at[2])
    out.start()
    out.wait()


def first_partial(field, third, second):
    far = pl.BlockSpec(memory_space=pl.ANY)
    return pl.pallas_call(
        spectrum_kernel,
        out_shape=pltpu.HBM((512, LANES), BF16),
        in_specs=[far] * 3,
        out_specs=far,
        scratch_shapes=[
            pltpu.VMEM(field.shape[1:], BF16),
            pltpu.VMEM(third.shape, BF16),
            pltpu.VMEM(second.shape, BF16),
            pltpu.VMEM((512, LANES), BF16),
            pltpu.VMEM((4096, LANES), F32),
            pltpu.SemaphoreType.DMA((CHANNELS // C_STEP,)),
            pltpu.SemaphoreType.DMA((3,)),
        ],
        cost_estimate=pl.CostEstimate(
            flops=600_000_000, bytes_accessed=6 << 20, transcendentals=0
        ),
        compiler_params=pltpu.CompilerParams(vmem_limit_bytes=VMEM_LIMIT),
    )(afar(field), afar(third), afar(second))


Y_STEP = 16
Y_STEPS = LANES // Y_STEP
Y_ROWS = Y_STEP * CHANNELS


def relay_kernel(field, _, out_far, near_field, out_near, rows_ref, in_sem, out_sem):
    def coming(step):
        x = step // Y_STEPS
        cut = pl.ds(pl.multiple_of((step % Y_STEPS) * Y_STEP, Y_STEP), Y_STEP)
        return pltpu.make_async_copy(
            field.at[0, :, x, cut], near_field.at[:, x, cut], in_sem.at[step]
        )

    def going(step):
        cut = pl.ds(pl.multiple_of(step * Y_ROWS, Y_ROWS), Y_ROWS)
        return pltpu.make_async_copy(out_near.at[cut], out_far.at[cut], out_sem.at[step])

    for step in range(2 * Y_STEPS):
        coming(step).start()

    def some(step, carry):
        coming(step).wait()
        at = pl.multiple_of((step % Y_STEPS) * Y_STEP, Y_STEP)
        rows_ref[...] = (
            near_field[:, step // Y_STEPS, pl.ds(at, Y_STEP), :].astype(F32).reshape(Y_ROWS, LANES)
        )
        for y in range(0, Y_STEP, 2):
            pair = [rows_ref[pl.ds(y + e, CHANNELS, stride=Y_STEP), :] for e in range(2)]
            tile = step * (Y_STEP // 2) + y // 2
            out_near[tile_at(tile), :] = jnp.concatenate(pair, axis=0).astype(BF16)
        going(step).start()
        return carry

    lax.fori_loop(0, 2 * Y_STEPS, some, 0)
    for step in range(2 * Y_STEPS):
        going(step).wait()


def relay(field, token):
    far = pl.BlockSpec(memory_space=pl.ANY)
    return pl.pallas_call(
        relay_kernel,
        out_shape=pltpu.HBM((ROWS, LANES), BF16),
        in_specs=[far] * 2,
        out_specs=far,
        scratch_shapes=[
            pltpu.VMEM(field.shape[1:], BF16),
            pltpu.VMEM((ROWS, LANES), BF16),
            pltpu.VMEM((Y_ROWS, LANES), F32),
            pltpu.SemaphoreType.DMA((2 * Y_STEPS,)),
            pltpu.SemaphoreType.DMA((2 * Y_STEPS,)),
        ],
        cost_estimate=pl.CostEstimate(
            flops=600_000_000, bytes_accessed=12 << 20, transcendentals=0
        ),
        compiler_params=pltpu.CompilerParams(vmem_limit_bytes=VMEM_LIMIT),
    )(afar(field), afar(token))


def own_spectrum(wide, table, place, block=8):
    real = wide[pl.ds(place, 64, stride=block), :]
    imag = wide[pl.ds(4 + place, 64, stride=block), :]
    both = mm(table, jnp.concatenate([real, imag], axis=0).astype(BF16))
    return both[:32, :CHANNELS] + both[32:, CHANNELS:]


def send_field(mixed, table, place, sent, block=8):
    twin = jnp.concatenate([mixed, mixed], axis=1)
    left = side(32)
    both = jnp.concatenate([jnp.where(left, twin, 0.0), jnp.where(left, 0.0, twin)], axis=0)
    out = mm(table, both.astype(BF16))
    sent[pl.ds(place, 64, stride=block), :] = out[:64]
    sent[pl.ds(4 + place, 64, stride=block), :] = out[64:]


def mode_lanes(modes):
    row = lax.broadcasted_iota(jnp.int32, (32, LANES), 0) % modes
    half = lax.broadcasted_iota(jnp.int32, (32, LANES), 1) // CHANNELS
    return row, half


def mix_kernel(small, _, outs, __, ___, scratch, loop):
    got_ref, weight_ref, forward_ref, inverse_ref = small
    out_ref, spec_ref = outs
    wide, sent = scratch
    wide[...] = got_ref[...].astype(F32)
    forward = forward_ref[...]
    inverse = inverse_ref[...]
    modes = weight_ref.shape[1]
    row, half = mode_lanes(modes)
    for p in range(4):
        spec = own_spectrum(wide, forward, p).astype(BF16)
        spec_ref[:, p * CHANNELS : (p + 1) * CHANNELS] = spec
        spec = spec.astype(F32)
        other = jnp.concatenate([-spec[modes:], spec[:modes]], axis=0)
        pieces = []
        for part in (spec, other):
            twin = jnp.concatenate([part, part], axis=1)
            for pair in range(modes // 2):
                pieces.append(jnp.where(row == 2 * pair + half, twin, 0.0).astype(BF16))
        spread = jnp.concatenate(pieces, axis=1)
        weights = weight_ref[:, :, p].reshape(2 * modes * CHANNELS, CHANNELS)
        mixed = mm(spread, weights).astype(BF16).astype(F32)
        send_field(mixed, inverse, p, sent)
    out_ref[...] = sent[...].astype(BF16)


def high_low(values):
    high = values.astype(BF16).astype(F32)
    return jnp.concatenate([high, values - high], axis=1)


def unmix_kernel(small, _, outs, __, ___, scratch, loop):
    got_ref, weight_ref, forward_ref, inverse_ref, term_ref, one_ref, two_ref = small
    out_ref, spec_ref = outs
    wide, sent = scratch
    wide[...] = got_ref[...].astype(F32)
    forward = forward_ref[...]
    inverse = inverse_ref[...]
    modes = weight_ref.shape[1]
    row, half = mode_lanes(modes)
    spec_ref[0:32, :] = one_ref[...]
    spec_ref[32:64, :] = two_ref[...]
    sent[...] = jnp.zeros_like(sent)
    terms = high_low(term_ref[...])
    sent[pl.ds(8, 64, stride=16), :] = terms[:CHANNELS]
    sent[pl.ds(9, 64, stride=16), :] = jnp.broadcast_to(
        terms[CHANNELS : CHANNELS + 1], (CHANNELS, LANES)
    )
    for p in range(4):
        spec = own_spectrum(wide, forward, p).astype(BF16)
        spec_ref[64:96, p * CHANNELS : (p + 1) * CHANNELS] = spec
        other = jnp.concatenate([spec[modes:].astype(F32), -spec[:modes].astype(F32)], axis=0)
        products = nt(spec, weight_ref[0, :, p].reshape(modes * CHANNELS, CHANNELS)) + nt(
            other.astype(BF16), weight_ref[1, :, p].reshape(modes * CHANNELS, CHANNELS)
        )
        total = jnp.zeros((32, LANES), F32)
        for pair in range(modes // 2):
            piece = products[:, pair * LANES : (pair + 1) * LANES]
            total = total + jnp.where(row == 2 * pair + half, piece, 0.0)
        mixed = (total + turned(total))[:, :CHANNELS].astype(BF16).astype(F32)
        send_field(mixed, inverse, p, sent, 16)
    out_ref[...] = sent[...].astype(BF16)


def last_kernel(small, _, outs, __, ___, scratch, loop):
    got_ref, forward_ref = small
    (out_ref,) = outs
    (wide,) = scratch
    for d in range(64):
        wide[d * 48 : (d + 1) * 48, :] = got_ref[d * 48 : (d + 1) * 48, :].astype(F32)
    forward = forward_ref[...]
    for p in range(4):
        out_ref[0:32, p * CHANNELS : (p + 1) * CHANNELS] = own_spectrum(
            wide, forward, p, 48
        ).astype(BF16)
    total = jnp.zeros((40, LANES), F32)
    for d in range(64):
        total = total + wide[d * 48 + 8 : (d + 1) * 48, :]
    high = total.astype(BF16)
    low = (total - high.astype(F32)).astype(BF16)
    out_ref[32:64, :] = jnp.concatenate([high[:32], low[:32]], axis=1)
    rows = wide[pl.ds(41, 64, stride=48), :]
    out_ref[64:96, :] = jnp.concatenate([rows[:32], rows[32:]], axis=1).astype(BF16)
    biases = jnp.concatenate(
        [
            high_low(total[32:40, :CHANNELS]),
            jnp.broadcast_to(wide[42:43, :], (8, LANES)),
        ],
        axis=1,
    )
    out_ref[96:112, :] = jnp.concatenate([biases, biases], axis=0).astype(BF16)


CHUNK = ((512, LANES), BF16)
SPECTRUM = ((32, 4 * CHANNELS), BF16)
WIDE = pltpu.VMEM((512, LANES), F32)


def mixing(got, weights, forward, inverse, token):
    return call(
        mix_kernel,
        [CHUNK, SPECTRUM],
        [WIDE, WIDE],
        200_000_000,
        3 << 20,
        got,
        weights,
        forward,
        inverse,
        token=token,
    )


def outer_products(spec, grad, out_ref):
    modes = out_ref.shape[1]
    depth = spec.shape[0]
    lane = lax.broadcasted_iota(jnp.int32, (CHANNELS, depth), 1) % modes
    other = []
    for n in range(depth // (2 * modes)):
        at = n * 2 * modes
        other += [grad[at + modes : at + 2 * modes], -grad[at : at + modes]]
    other = jnp.concatenate(other, axis=0)
    for p in range(4):
        cut = slice(p * CHANNELS, (p + 1) * CHANNELS)
        both = jnp.concatenate([grad[:, cut], other[:, cut]], axis=1).astype(BF16)
        tall = spec[:, cut].T
        for m in range(modes):
            out = mm(jnp.where(lane == m, tall, 0.0).astype(BF16), both).astype(BF16)
            out_ref[0, m, p] = out[:, :CHANNELS]
            out_ref[1, m, p] = out[:, CHANNELS:]


def rows_of(ref, step, at):
    count = ref.shape[0] // step
    return jnp.concatenate(
        [ref[n * step + at : n * step + at + 32, :] for n in range(count)], axis=0
    ).astype(F32)


def in_order(index, parts, ordered):
    rows = parts[0].shape[0]
    for k, part in enumerate(parts):
        at = pl.multiple_of((index ^ k) * rows, 16)
        ordered[pl.ds(at, rows), :] = part[...].astype(F32)


def weight_two_kernel(index_ref, *refs):
    early, _, out_ref, ordered = refs[:4], refs[4], refs[5], refs[6]
    in_order(index_ref[0], early, ordered)
    outer_products(rows_of(ordered, 96, 32), rows_of(ordered, 96, 64), out_ref)


def weight_one_kernel(factor, index_ref, *refs):
    early, late = refs[:4], refs[4:8]
    out_ref, one_ref, two_ref, bias_one_ref, bias_two_ref, early_all, late_all = refs[9:]
    in_order(index_ref[0], early, early_all)
    in_order(index_ref[0], late, late_all)
    sums = late_all[32:112, :]
    for n in range(1, 4):
        sums = sums + late_all[n * 112 + 32 : (n + 1) * 112, :]
    sums = sums * factor
    one = sums[:32, :LANES] + sums[:32, LANES:]
    one_ref[0:32, :] = one[:, :CHANNELS]
    one_ref[32:64, :] = one[:, CHANNELS:]
    two = jnp.concatenate([sums[32:64, :LANES], sums[32:64, LANES:]], axis=0)
    two_ref[...] = (two + turned(two))[:, :CHANNELS]
    bias = jnp.concatenate([sums[64:72, :LANES], sums[64:72, LANES:]], axis=0)
    bias = bias + turned(bias)
    bias_one_ref[...] = bias[0:1, :CHANNELS]
    bias_two_ref[...] = bias[8:9, :CHANNELS]
    outer_products(rows_of(early_all, 96, 0), rows_of(late_all, 112, 0), out_ref)


def weight_call(kernel, outs, index, parts, token):
    wide = 4 * CHANNELS
    heights = [4 * part.shape[0] for part in parts[::4]]
    return pl.pallas_call(
        kernel,
        out_shape=outs,
        in_specs=[pl.BlockSpec(memory_space=pltpu.SMEM)]
        + [VM] * len(parts)
        + [pl.BlockSpec(memory_space=pl.ANY)],
        out_specs=[VM] * len(outs),
        scratch_shapes=[pltpu.VMEM((height, wide), F32) for height in heights],
        cost_estimate=pl.CostEstimate(
            flops=200_000_000, bytes_accessed=3 << 20, transcendentals=0
        ),
        compiler_params=pltpu.CompilerParams(vmem_limit_bytes=VMEM_LIMIT),
    )(index, *[near(part) for part in parts], token)


TILES = 128
PAIRS = TILES // 2
TILE = 2 * CHANNELS


def unpack_modes(got_ref, second_ref, depth, block=8):
    second = second_ref[...]
    left = side(32)
    for k in range(MZ):
        near = jnp.concatenate(
            [got_ref[d * block : d * block + 8, :] for d in range(k * 4, k * 4 + 4)], axis=0
        ) if block > 8 else got_ref[k * 32 : (k + 1) * 32, :].astype(F32)
        far = turned(near)
        top = jnp.concatenate([jnp.where(left, near, 0.0), jnp.where(left, far, 0.0)], axis=1)
        low = jnp.concatenate([jnp.where(left, 0.0, far), jnp.where(left, 0.0, near)], axis=1)
        out = mm(second, jnp.concatenate([top, low], axis=0).astype(BF16))
        for x in range(2):
            cut = slice(x * LANES, (x + 1) * LANES)
            depth[pl.ds(x * 2048 + k, 64, stride=32), :] = out[:64, cut]
            depth[pl.ds(x * 2048 + MZ + k, 64, stride=32), :] = out[64:, cut]


def pack_modes(spec, second_ref, out_ref, block=8):
    second = second_ref[...]
    left = side(32)
    for k in range(MZ):
        planes = [
            jnp.concatenate(
                [
                    spec[pl.ds(x * 2048 + k, 64, stride=32), :],
                    spec[pl.ds(x * 2048 + MZ + k, 64, stride=32), :],
                ],
                axis=0,
            )
            for x in range(2)
        ]
        out = mm(second, jnp.concatenate(planes, axis=1).astype(BF16))
        near, far = out[:, :LANES], out[:, LANES:]
        packed = jnp.where(left, near[:32] + turned(near[32:]), turned(far[:32]) + far[32:])
        if block == 8:
            out_ref[k * 32 : (k + 1) * 32, :] = packed.astype(out_ref.dtype)
        else:
            for d in range(4):
                at = (k * 4 + d) * block
                out_ref[at : at + 8, :] = packed[d * 8 : (d + 1) * 8]


def branch_of(depth, third, pair):
    at = pl.multiple_of(pair * 64, 64)
    wide = tn(depth[pl.ds(at, 64), :].astype(BF16), third)
    return wide[:, :LANES], wide[:, LANES:]


def store_spectrum(spec, third, pair, first, second):
    done = nt(third, jnp.concatenate([first, second], axis=0))
    at = pl.multiple_of(pair * 64, 64)
    spec[pl.ds(at, 32), :] = done[:, :LANES]
    spec[pl.ds(at + 32, 32), :] = done[:, LANES:]


def tile_at(tile):
    return pl.ds(pl.multiple_of(tile * TILE, TILE), TILE)


def gelu(preact):
    inner = preact * (ROOT + (ROOT * CUBIC) * (preact * preact))
    halved = 0.5 * preact
    return halved + halved * jnp.tanh(inner)


def gelu_slope(preact):
    square = preact * preact
    tangent = jnp.tanh(preact * (ROOT + (ROOT * CUBIC) * square))
    steep = (0.5 * preact) * (ROOT + (3.0 * ROOT * CUBIC) * square)
    return 0.5 + 0.5 * tangent + steep * (1.0 - tangent * tangent)


def hidden_kernel(small, big, outs, kinds, _, scratch, loop):
    got, inv2, inv3, fwd3, fwd2 = small
    (base,) = big
    hidden, preact = kinds
    depth, spec = scratch
    unpack_modes(got, inv2, depth)
    third_back = inv3[...]
    third = fwd3[...]

    def body(pair, carry):
        made = []
        for e, branch in enumerate(branch_of(depth, third_back, pair)):
            at = tile_at(2 * pair + e)
            pre = base[at, :].astype(F32) + branch
            preact[at, :] = pre.astype(BF16)
            value = gelu(pre).astype(BF16)
            hidden[at, :] = value
            made.append(value)
        store_spectrum(spec, third, pair, *made)
        return carry

    loop(body)
    pack_modes(spec, fwd2, outs[0])


def grad_two_kernel(small, big, outs, kinds, _, scratch, loop):
    got, inv2, inv3, fwd3, fwd2 = small
    base, cot = big
    (grad,) = kinds
    depth, spec = scratch
    unpack_modes(got, inv2, depth)
    third_back = inv3[...]
    third = fwd3[...]

    def body(pair, carry):
        made = []
        for e, branch in enumerate(branch_of(depth, third_back, pair)):
            at = tile_at(2 * pair + e)
            slope = gelu_slope(base[at, :].astype(F32) + branch)
            value = (cot[at, :].astype(F32) * slope).astype(BF16)
            grad[at, :] = value
            made.append(value)
        store_spectrum(spec, third, pair, *made)
        return carry

    loop(body)
    pack_modes(spec, fwd2, outs[0])


def grad_one_kernel(small, big, outs, _, __, scratch, loop):
    got, inv2, inv3, fwd3, fwd2 = small
    base, slope, values = big
    (out,) = outs
    depth, spec, wide, sent = scratch
    wide[...] = got[...].astype(F32)
    unpack_modes(wide, inv2, depth, 16)
    third_back = inv3[...]
    third = fwd3[...]
    ones = jnp.ones((16, 4 * LANES), BF16)

    def body(pair, total):
        made = []
        for e, branch in enumerate(branch_of(depth, third_back, pair)):
            at = tile_at(2 * pair + e)
            back = base[at, :].astype(F32) + branch
            made.append((back * slope[at, :].astype(F32)).astype(BF16))
        store_spectrum(spec, third, pair, *made)
        left = jnp.concatenate(
            [wide_tile(values, 2 * pair), wide_tile(values, 2 * pair + 1)], axis=1
        )
        right = jnp.concatenate(
            [part for tile in made for part in (tile[:CHANNELS], tile[CHANNELS:])], axis=1
        )
        return total + nt(jnp.concatenate([left, ones], axis=0), right)

    total = loop(body, jnp.zeros((CHANNELS + 16, CHANNELS), F32))
    pack_modes(spec, fwd2, sent, 48)
    left = side(1)

    def arrived_sum(place):
        row = jnp.sum(wide[pl.ds(place, 64, stride=16), :], axis=0, keepdims=True)
        row = row + turned(row)
        high = row.astype(BF16).astype(F32)
        return jnp.where(left, high, row - high)

    bias = jnp.concatenate([total[64:65], total[64:65]], axis=1)
    terms = jnp.concatenate(
        [
            jnp.concatenate([total[:32], total[32:64]], axis=1),
            bias,
            arrived_sum(8),
            arrived_sum(9),
            jnp.zeros((5, LANES), F32),
        ],
        axis=0,
    )
    for d in range(64):
        sent[d * 48 + 8 : (d + 1) * 48, :] = terms
    for d in range(64):
        out[d * 48 : (d + 1) * 48, :] = sent[d * 48 : (d + 1) * 48, :].astype(BF16)


def planes(kernel, kinds, *operands, big, token):
    scratch = [pltpu.VMEM((4096, LANES), F32), pltpu.VMEM((4096, LANES), F32)]
    return call(
        kernel,
        [CHUNK],
        scratch,
        1_000_000_000,
        20 << 20,
        *operands,
        big=big,
        kinds=kinds,
        token=token,
    )


def wide_tile(ref, tile):
    at = pl.multiple_of(tile * TILE, TILE)
    return jnp.concatenate(
        [ref[pl.ds(at, CHANNELS), :], ref[pl.ds(at + CHANNELS, CHANNELS), :]], axis=1
    )


def store_wide(ref, tile, wide):
    at = pl.multiple_of(tile * TILE, TILE)
    ref[pl.ds(at, CHANNELS), :] = wide[:, :LANES].astype(BF16)
    ref[pl.ds(at + CHANNELS, CHANNELS), :] = wide[:, LANES:].astype(BF16)


def point_kernel(small, big, _, kinds, __, scratch, loop):
    point, bias = small
    weights = point[...]
    shift = jnp.concatenate([bias[...], bias[...]], axis=1)

    def body(pair, carry):
        for tile in (2 * pair, 2 * pair + 1):
            store_wide(kinds[0], tile, mm(weights, wide_tile(big[0], tile)) + shift)
        return carry

    loop(body)


def slope_kernel(small, big, _, kinds, __, scratch, loop):
    def body(pair, carry):
        for tile in (2 * pair, 2 * pair + 1):
            at = tile_at(tile)
            kinds[0][at, :] = gelu_slope(big[0][at, :].astype(F32)).astype(BF16)
        return carry

    loop(body)


def point_back_kernel(small, big, outs, kinds, _, scratch, loop):
    weights = small[0][...]
    hidden, grad = big
    ones = jnp.ones((16, 4 * LANES), BF16)

    def body(pair, total):
        right = [wide_tile(grad, 2 * pair + e) for e in range(2)]
        for e in range(2):
            store_wide(kinds[0], 2 * pair + e, mm(weights, right[e]))
        left = jnp.concatenate(
            [wide_tile(hidden, 2 * pair), wide_tile(hidden, 2 * pair + 1)], axis=1
        )
        return total + nt(
            jnp.concatenate([left, ones], axis=0), jnp.concatenate(right, axis=1)
        )

    outs[0][...] = loop(body, jnp.zeros((CHANNELS + 16, CHANNELS), F32))


def body(field_in, cotangent, spectral_one, spectral_two, point_one, point_two, bias_one, bias_two):
    forward_c, inverse_c = complex_tables(LANES, MY)
    forward_z, inverse_z = real_tables(LANES, MZ)
    shape = spectral_one.shape
    const = lambda table: jnp.asarray(np.ascontiguousarray(table))

    natural_second = const(second_natural(forward_c))
    third_forward = const(forward_z.T)
    third_adjoint = const(inverse_z)
    third_inverse = const(twice_diagonal(inverse_z))
    third_back = const(twice_diagonal(forward_z.T))
    second_fwd = const(second_paired(forward_c))
    second_adj = const(second_paired(flipped(inverse_c)))
    second_inv = const(second_inverse(inverse_c))
    second_back = const(second_inverse(flipped(forward_c)))
    first_fwd = const(first_forward(forward_c))
    first_adj = const(first_forward(flipped(inverse_c)))
    first_inv = const(first_inverse(inverse_c))
    first_back = const(first_inverse(flipped(forward_c)))

    def exchange(chunk):
        return lax.all_to_all(chunk, "space", split_axis=0, concat_axis=0, tiled=True)

    def point_map(values, point, bias, token):
        return call(
            point_kernel,
            [],
            [],
            500_000_000,
            12 << 20,
            point.T,
            spread(bias),
            big=[values],
            kinds=[BF16],
            token=token,
        )[0]

    def samples(spectrum):
        size = 4
        return [spectrum] + [
            lax.ppermute(spectrum, "dp", [(i, i ^ k) for i in range(size)])
            for k in range(1, size)
        ]

    spread = lambda bias: jnp.broadcast_to(bias[:, None], (CHANNELS, LANES))

    chunk = first_partial(field_in, third_forward, natural_second)
    got = exchange(chunk)
    values = relay(field_in, chunk)

    chunk, spec_one = mixing(got, spectral_one, first_fwd, first_inv, token=values)
    got = exchange(chunk)
    base = point_map(values, point_one, bias_one, chunk)

    chunk, hidden, preact = planes(
        hidden_kernel,
        [BF16, BF16],
        got,
        second_inv,
        third_inverse,
        third_forward,
        second_fwd,
        big=[base],
        token=spec_one,
    )
    got = exchange(chunk)
    base = point_map(hidden, point_two, bias_two, chunk)

    chunk, spec_two = mixing(got, spectral_two, first_fwd, first_inv, token=base)
    got = exchange(chunk)
    cot = relay(cotangent, chunk)

    chunk, grad_two = planes(
        grad_two_kernel,
        [BF16],
        got,
        second_inv,
        third_inverse,
        third_adjoint,
        second_adj,
        big=[base, cot],
        token=spec_two,
    )
    got = exchange(chunk)
    term_two, base = call(
        point_back_kernel,
        [((CHANNELS + 16, CHANNELS), F32)],
        [],
        1_000_000_000,
        12 << 20,
        point_two,
        big=[hidden, grad_two],
        kinds=[BF16],
    )

    chunk, early = call(
        unmix_kernel,
        [((1024, LANES), BF16), ((96, 4 * CHANNELS), BF16)],
        [WIDE, pltpu.VMEM((1024, LANES), F32)],
        200_000_000,
        3 << 20,
        got,
        spectral_two,
        first_adj,
        first_back,
        term_two,
        spec_one,
        spec_two,
    )
    got = exchange(chunk)
    early = samples(early)
    slope = call(
        slope_kernel, [], [], 500_000_000, 12 << 20, big=[preact], kinds=[BF16], token=chunk
    )[0]

    chunk = call(
        grad_one_kernel,
        [((3072, LANES), BF16)],
        [
            pltpu.VMEM((4096, LANES), F32),
            pltpu.VMEM((4096, LANES), F32),
            pltpu.VMEM((1024, LANES), F32),
            pltpu.VMEM((3072, LANES), F32),
        ],
        1_500_000_000,
        20 << 20,
        got,
        second_back,
        third_back,
        third_adjoint,
        second_adj,
        big=[base, slope, values],
        token=early[1:],
    )[0]
    got = exchange(chunk)
    late = call(
        last_kernel,
        [((112, 4 * CHANNELS), BF16)],
        [pltpu.VMEM((3072, LANES), F32)],
        50_000_000,
        1 << 20,
        got,
        first_adj,
    )[0]
    index = lax.axis_index("dp").astype(jnp.int32).reshape(1)
    weights = jax.ShapeDtypeStruct(shape, BF16)
    spectral_grad_two = weight_call(weight_two_kernel, [weights], index, early, late)[0]
    late = samples(late)
    cells = lax.axis_size("dp") * lax.axis_size("space") * 2 * LANES * LANES
    square = jax.ShapeDtypeStruct((CHANNELS, CHANNELS), F32)
    line = jax.ShapeDtypeStruct((1, CHANNELS), F32)
    spectral_grad_one, point_grad_one, point_grad_two, bias_grad_one, bias_grad_two = weight_call(
        functools.partial(weight_one_kernel, 1.0 / math.sqrt(cells)),
        [weights, square, square, line, line],
        index,
        early + late,
        spectral_grad_two,
    )
    return (
        spectral_grad_one,
        spectral_grad_two,
        point_grad_one,
        point_grad_two,
        bias_grad_one.reshape(CHANNELS),
        bias_grad_two.reshape(CHANNELS),
    )


def solution(mesh):
    field = P("dp", None, "space", None, None)
    modes = P(None, None, "space", None, None)
    return jax.shard_map(
        body,
        mesh=mesh,
        in_specs=(field, field, modes, modes, P(), P(), P(), P()),
        out_specs=(modes, modes, P(), P(), P(), P()),
        check_vma=False,
    )
```

```python
import functools
import math

import jax
import jax.numpy as jnp
import numpy as np
from jax import lax
from jax.experimental import pallas as pl
from jax.experimental.pallas import tpu as pltpu
from jax.sharding import PartitionSpec as P

MY = 16
MZ = 16
CHANNELS = 64
LANES = 128
ROOT = math.sqrt(2.0 / math.pi)
CUBIC = 0.044715
F32 = jnp.float32
BF16 = jnp.bfloat16
VMEM_LIMIT = 44 * 1024 * 1024


def angles(length, modes, two_sided):
    places = np.arange(length, dtype=np.int64)[:, None]
    orders = np.arange(modes, dtype=np.int64)[None, :]
    if two_sided:
        orders = np.where(orders < modes // 2, orders, orders - modes + length)
    phases = places * orders % length
    return np.float32(2.0 * math.pi / length) * phases.astype(np.float32)


def complex_tables(length, modes):
    radians = angles(length, modes, True)
    factor = np.float32(1.0 / math.sqrt(length))
    cosines = np.cos(radians) * factor
    sines = np.sin(radians) * factor
    forward = np.stack(
        [np.stack([cosines, -sines], axis=1), np.stack([sines, cosines], axis=1)], axis=0
    )
    inverse = np.stack(
        [np.stack([cosines.T, sines.T], axis=1), np.stack([-sines.T, cosines.T], axis=1)], axis=0
    )
    return forward.astype(BF16), inverse.astype(BF16)


def real_tables(length, modes):
    radians = angles(length, modes, False)
    factor = np.float32(1.0 / math.sqrt(length))
    cosines = np.cos(radians) * factor
    sines = np.sin(radians) * factor
    forward = np.concatenate([cosines, -sines], axis=1)
    doubled = np.where(np.arange(modes) == 0, 1.0, 2.0).astype(np.float32)[None, :]
    inverse = np.concatenate([(cosines * doubled).T, (-sines * doubled).T], axis=0)
    return forward.astype(BF16), inverse.astype(BF16)


def flipped(table):
    return np.transpose(table, (2, 3, 0, 1))


def second_natural(table):
    length = table.shape[1]
    split = table.reshape(2, length, 2, MY // 4, 4)
    return split.transpose(3, 2, 4, 0, 1).reshape(2 * MY, 2 * length)


def second_paired(table):
    length = table.shape[1]
    split = table.reshape(2, length // 2, 2, 2, MY // 4, 4)
    return split.transpose(2, 4, 3, 5, 0, 1).reshape(4 * MY, length)


def second_inverse(table):
    length = table.shape[3]
    split = table.reshape(2, MY // 4, 4, 2, length // 2, 2)
    return split.transpose(3, 4, 5, 1, 0, 2).reshape(length, 4 * MY)


def first_forward(table):
    length, modes = table.shape[1], table.shape[3]
    split = table.reshape(2, length // 2, 2, 2, modes)
    return split.transpose(2, 3, 4, 0, 1).reshape(4 * modes, length)


def first_inverse(table):
    modes, length = table.shape[1], table.shape[3]
    split = table.reshape(2, modes, 2, length // 2, 2)
    return split.transpose(2, 3, 4, 0, 1).reshape(length, 4 * modes)


def twice_diagonal(table):
    zero = np.zeros_like(table)
    return np.block([[table, zero], [zero, table]])


def mm(left, right):
    return lax.dot_general(left, right, (((1,), (0,)), ((), ())), preferred_element_type=F32)


def nt(left, right):
    return lax.dot_general(left, right, (((1,), (1,)), ((), ())), preferred_element_type=F32)


def tn(left, right):
    return lax.dot_general(left, right, (((0,), (0,)), ((), ())), preferred_element_type=F32)


def side(rows):
    return lax.broadcasted_iota(jnp.int32, (rows, LANES), 1) < LANES // 2


def turned(values):
    return pltpu.roll(values, LANES // 2, 1)


def whole(shape):
    return pl.BlockSpec(shape, lambda *_: (0,) * len(shape))


VM = pl.BlockSpec(memory_space=pltpu.VMEM)


GROUPS = 4
ROWS = 2 * LANES * CHANNELS


def near(value):
    return pltpu.with_memory_space_constraint(value, pltpu.VMEM)


def afar(value):
    return pltpu.with_memory_space_constraint(value, pltpu.HBM)


def call(
    kernel, outs, scratch, flops, moved, *operands, big=(), kinds=(), plain=(), token=None
):
    cut = ROWS // GROUPS
    extra = [] if token is None else list(token) if isinstance(token, list) else [token]
    counts = [
        len(operands),
        len(big),
        len(extra),
        len(outs),
        len(kinds),
        len(plain),
        len(scratch),
        len(outs),
        len(big),
        len(kinds),
        3,
    ]

    def whole_kernel(*refs):
        parts = []
        at = 0
        for count in counts:
            parts.append(refs[at : at + count])
            at += count
        small, big_far, _, outs_far, kinds_far, plains, own, outs_near, big_near, kinds_near, sems = parts
        in_sem, out_sem, end_sem = sems

        def group_of(far, close, sem, index, group, out):
            rows = pl.ds(pl.multiple_of(group * cut, cut), cut)
            pair = (close.at[rows], far.at[rows]) if out else (far.at[rows], close.at[rows])
            return pltpu.make_async_copy(*pair, sem.at[index, group])

        def coming(index, group):
            return group_of(big_far[index], big_near[index], in_sem, index, group, False)

        def going(index, group):
            return group_of(kinds_far[index], kinds_near[index], out_sem, index, group, True)

        for group in range(GROUPS):
            for index in range(len(big)):
                coming(index, group).start()

        def loop(body, carry=0, unroll=PAIRS // GROUPS):
            per = PAIRS // GROUPS

            def some(i, carry):
                for j in range(unroll):
                    carry = body(i * unroll + j, carry)
                return carry

            def each(group, carry):
                for index in range(len(big)):
                    coming(index, group).wait()
                first = group * (per // unroll)
                carry = lax.fori_loop(first, first + per // unroll, some, carry)
                for index in range(len(kinds)):
                    going(index, group).start()
                return carry

            return lax.fori_loop(0, GROUPS, each, carry)

        kernel(small, big_near, outs_near, kinds_near, plains, own, loop)
        last = [
            pltpu.make_async_copy(close, far, end_sem.at[index])
            for index, (close, far) in enumerate(zip(outs_near, outs_far))
        ]
        for copy in last:
            copy.start()
        for index in range(len(kinds)):
            for group in range(GROUPS):
                going(index, group).wait()
        for copy in last:
            copy.wait()

    operands = [near(operand) for operand in operands]
    far = pl.BlockSpec(memory_space=pl.ANY)
    shapes = [pltpu.HBM(shape, kind) for shape, kind in outs]
    shapes += [pltpu.HBM((ROWS, LANES), kind) for kind in kinds]
    return pl.pallas_call(
        whole_kernel,
        out_shape=shapes + list(plain),
        in_specs=[VM] * len(operands) + [far] * (len(big) + len(extra)),
        out_specs=[far] * len(shapes) + [VM] * len(plain),
        scratch_shapes=list(scratch)
        + [pltpu.VMEM(shape, kind) for shape, kind in outs]
        + [pltpu.VMEM((ROWS, LANES), array.dtype) for array in big]
        + [pltpu.VMEM((ROWS, LANES), kind) for kind in kinds]
        + [
            pltpu.SemaphoreType.DMA((max(len(big), 1), GROUPS)),
            pltpu.SemaphoreType.DMA((max(len(kinds), 1), GROUPS)),
            pltpu.SemaphoreType.DMA((max(len(outs), 1),)),
        ],
        cost_estimate=pl.CostEstimate(flops=flops, bytes_accessed=moved, transcendentals=0),
        compiler_params=pltpu.CompilerParams(vmem_limit_bytes=VMEM_LIMIT),
    )(*operands, *[afar(array) for array in (*big, *extra)])


C_STEP = 8


def spectrum_kernel(field, third_far, second_far, out_far, near_field, third_ref, second_ref, chunk, spec, sems, extra):
    def coming(step):
        cut = pl.ds(step * C_STEP, C_STEP)
        return pltpu.make_async_copy(field.at[0, cut], near_field.at[cut], sems.at[step])

    tables = [
        pltpu.make_async_copy(third_far, third_ref, extra.at[0]),
        pltpu.make_async_copy(second_far, second_ref, extra.at[1]),
    ]
    for copy in tables:
        copy.start()
    for step in range(CHANNELS // C_STEP):
        coming(step).start()
    for copy in tables:
        copy.wait()
    third = third_ref[...]

    def some(step, carry):
        coming(step).wait()
        for x in range(2):
            rows = near_field[pl.ds(step * C_STEP, C_STEP), x].reshape(C_STEP * LANES, LANES)
            done = nt(third, rows)
            for c in range(C_STEP):
                place = pl.multiple_of((x * CHANNELS + step * C_STEP + c) * 2 * MZ, 2 * MZ)
                spec[pl.ds(place, 2 * MZ), :] = done[:, c * LANES : (c + 1) * LANES]
        return carry

    lax.fori_loop(0, CHANNELS // C_STEP, some, 0)
    second = second_ref[...]
    for k in range(MZ):
        real = spec[pl.ds(k, LANES, stride=2 * MZ), :]
        imag = spec[pl.ds(MZ + k, LANES, stride=2 * MZ), :]
        both = jnp.concatenate([real, imag], axis=1).astype(BF16)
        chunk[k * 32 : (k + 1) * 32, :] = nt(second, both).astype(BF16)
    out = pltpu.make_async_copy(chunk, out_far, extra.at[2])
    out.start()
    out.wait()


def first_partial(field, third, second):
    far = pl.BlockSpec(memory_space=pl.ANY)
    return pl.pallas_call(
        spectrum_kernel,
        out_shape=pltpu.HBM((512, LANES), BF16),
        in_specs=[far] * 3,
        out_specs=far,
        scratch_shapes=[
            pltpu.VMEM(field.shape[1:], BF16),
            pltpu.VMEM(third.shape, BF16),
            pltpu.VMEM(second.shape, BF16),
            pltpu.VMEM((512, LANES), BF16),
            pltpu.VMEM((4096, LANES), F32),
            pltpu.SemaphoreType.DMA((CHANNELS // C_STEP,)),
            pltpu.SemaphoreType.DMA((3,)),
        ],
        cost_estimate=pl.CostEstimate(
            flops=600_000_000, bytes_accessed=6 << 20, transcendentals=0
        ),
        compiler_params=pltpu.CompilerParams(vmem_limit_bytes=VMEM_LIMIT),
    )(afar(field), afar(third), afar(second))


Y_STEP = 16
Y_STEPS = LANES // Y_STEP
Y_ROWS = Y_STEP * CHANNELS


def relay_kernel(field, _, out_far, near_field, out_near, rows_ref, in_sem, out_sem):
    def coming(step):
        x = step // Y_STEPS
        cut = pl.ds(pl.multiple_of((step % Y_STEPS) * Y_STEP, Y_STEP), Y_STEP)
        return pltpu.make_async_copy(
            field.at[0, :, x, cut], near_field.at[:, x, cut], in_sem.at[step]
        )

    def going(step):
        cut = pl.ds(pl.multiple_of(step * Y_ROWS, Y_ROWS), Y_ROWS)
        return pltpu.make_async_copy(out_near.at[cut], out_far.at[cut], out_sem.at[step])

    for step in range(2 * Y_STEPS):
        coming(step).start()

    def some(step, carry):
        coming(step).wait()
        at = pl.multiple_of((step % Y_STEPS) * Y_STEP, Y_STEP)
        rows_ref[...] = (
            near_field[:, step // Y_STEPS, pl.ds(at, Y_STEP), :].astype(F32).reshape(Y_ROWS, LANES)
        )
        for y in range(0, Y_STEP, 2):
            pair = [rows_ref[pl.ds(y + e, CHANNELS, stride=Y_STEP), :] for e in range(2)]
            tile = step * (Y_STEP // 2) + y // 2
            out_near[tile_at(tile), :] = jnp.concatenate(pair, axis=0).astype(BF16)
        going(step).start()
        return carry

    lax.fori_loop(0, 2 * Y_STEPS, some, 0)
    for step in range(2 * Y_STEPS):
        going(step).wait()


def relay(field, token):
    far = pl.BlockSpec(memory_space=pl.ANY)
    return pl.pallas_call(
        relay_kernel,
        out_shape=pltpu.HBM((ROWS, LANES), BF16),
        in_specs=[far] * 2,
        out_specs=far,
        scratch_shapes=[
            pltpu.VMEM(field.shape[1:], BF16),
            pltpu.VMEM((ROWS, LANES), BF16),
            pltpu.VMEM((Y_ROWS, LANES), F32),
            pltpu.SemaphoreType.DMA((2 * Y_STEPS,)),
            pltpu.SemaphoreType.DMA((2 * Y_STEPS,)),
        ],
        cost_estimate=pl.CostEstimate(
            flops=600_000_000, bytes_accessed=12 << 20, transcendentals=0
        ),
        compiler_params=pltpu.CompilerParams(vmem_limit_bytes=VMEM_LIMIT),
    )(afar(field), afar(token))


def own_spectrum(wide, table, place, block=8):
    real = wide[pl.ds(place, 64, stride=block), :]
    imag = wide[pl.ds(4 + place, 64, stride=block), :]
    both = mm(table, jnp.concatenate([real, imag], axis=0).astype(BF16))
    return both[:32, :CHANNELS] + both[32:, CHANNELS:]


def send_field(mixed, table, place, sent, block=8):
    twin = jnp.concatenate([mixed, mixed], axis=1)
    left = side(32)
    both = jnp.concatenate([jnp.where(left, twin, 0.0), jnp.where(left, 0.0, twin)], axis=0)
    out = mm(table, both.astype(BF16))
    sent[pl.ds(place, 64, stride=block), :] = out[:64]
    sent[pl.ds(4 + place, 64, stride=block), :] = out[64:]


def mode_lanes(modes):
    row = lax.broadcasted_iota(jnp.int32, (32, LANES), 0) % modes
    half = lax.broadcasted_iota(jnp.int32, (32, LANES), 1) // CHANNELS
    return row, half


def mix_kernel(small, _, outs, __, ___, scratch, loop):
    got_ref, weight_ref, forward_ref, inverse_ref = small
    out_ref, spec_ref = outs
    wide, sent = scratch
    wide[...] = got_ref[...].astype(F32)
    forward = forward_ref[...]
    inverse = inverse_ref[...]
    modes = weight_ref.shape[1]
    row, half = mode_lanes(modes)
    for p in range(4):
        spec = own_spectrum(wide, forward, p).astype(BF16)
        spec_ref[:, p * CHANNELS : (p + 1) * CHANNELS] = spec
        spec = spec.astype(F32)
        other = jnp.concatenate([-spec[modes:], spec[:modes]], axis=0)
        pieces = []
        for part in (spec, other):
            twin = jnp.concatenate([part, part], axis=1)
            for pair in range(modes // 2):
                pieces.append(jnp.where(row == 2 * pair + half, twin, 0.0).astype(BF16))
        spread = jnp.concatenate(pieces, axis=1)
        weights = weight_ref[:, :, p].reshape(2 * modes * CHANNELS, CHANNELS)
        mixed = mm(spread, weights).astype(BF16).astype(F32)
        send_field(mixed, inverse, p, sent)
    out_ref[...] = sent[...].astype(BF16)


def high_low(values):
    high = values.astype(BF16).astype(F32)
    return jnp.concatenate([high, values - high], axis=1)


def unmix_kernel(small, _, outs, __, ___, scratch, loop):
    got_ref, weight_ref, forward_ref, inverse_ref, term_ref, one_ref, two_ref = small
    out_ref, spec_ref = outs
    wide, sent = scratch
    wide[...] = got_ref[...].astype(F32)
    forward = forward_ref[...]
    inverse = inverse_ref[...]
    modes = weight_ref.shape[1]
    row, half = mode_lanes(modes)
    spec_ref[0:32, :] = one_ref[...]
    spec_ref[32:64, :] = two_ref[...]
    sent[...] = jnp.zeros_like(sent)
    terms = high_low(term_ref[...])
    sent[pl.ds(8, 64, stride=16), :] = terms[:CHANNELS]
    sent[pl.ds(9, 64, stride=16), :] = jnp.broadcast_to(
        terms[CHANNELS : CHANNELS + 1], (CHANNELS, LANES)
    )
    for p in range(4):
        spec = own_spectrum(wide, forward, p).astype(BF16)
        spec_ref[64:96, p * CHANNELS : (p + 1) * CHANNELS] = spec
        other = jnp.concatenate([spec[modes:].astype(F32), -spec[:modes].astype(F32)], axis=0)
        products = nt(spec, weight_ref[0, :, p].reshape(modes * CHANNELS, CHANNELS)) + nt(
            other.astype(BF16), weight_ref[1, :, p].reshape(modes * CHANNELS, CHANNELS)
        )
        total = jnp.zeros((32, LANES), F32)
        for pair in range(modes // 2):
            piece = products[:, pair * LANES : (pair + 1) * LANES]
            total = total + jnp.where(row == 2 * pair + half, piece, 0.0)
        mixed = (total + turned(total))[:, :CHANNELS].astype(BF16).astype(F32)
        send_field(mixed, inverse, p, sent, 16)
    out_ref[...] = sent[...].astype(BF16)


def last_kernel(small, _, outs, __, ___, scratch, loop):
    got_ref, forward_ref = small
    (out_ref,) = outs
    (wide,) = scratch
    for d in range(64):
        wide[d * 48 : (d + 1) * 48, :] = got_ref[d * 48 : (d + 1) * 48, :].astype(F32)
    forward = forward_ref[...]
    for p in range(4):
        out_ref[0:32, p * CHANNELS : (p + 1) * CHANNELS] = own_spectrum(
            wide, forward, p, 48
        ).astype(BF16)
    total = jnp.zeros((40, LANES), F32)
    for d in range(64):
        total = total + wide[d * 48 + 8 : (d + 1) * 48, :]
    high = total.astype(BF16)
    low = (total - high.astype(F32)).astype(BF16)
    out_ref[32:64, :] = jnp.concatenate([high[:32], low[:32]], axis=1)
    rows = wide[pl.ds(41, 64, stride=48), :]
    out_ref[64:96, :] = jnp.concatenate([rows[:32], rows[32:]], axis=1).astype(BF16)
    biases = jnp.concatenate(
        [
            high_low(total[32:40, :CHANNELS]),
            jnp.broadcast_to(wide[42:43, :], (8, LANES)),
        ],
        axis=1,
    )
    out_ref[96:112, :] = jnp.concatenate([biases, biases], axis=0).astype(BF16)


CHUNK = ((512, LANES), BF16)
SPECTRUM = ((32, 4 * CHANNELS), BF16)
WIDE = pltpu.VMEM((512, LANES), F32)


def mixing(got, weights, forward, inverse, token):
    return call(
        mix_kernel,
        [CHUNK, SPECTRUM],
        [WIDE, WIDE],
        200_000_000,
        3 << 20,
        got,
        weights,
        forward,
        inverse,
        token=token,
    )


def outer_products(spec, grad, out_ref):
    modes = out_ref.shape[1]
    depth = spec.shape[0]
    lane = lax.broadcasted_iota(jnp.int32, (CHANNELS, depth), 1) % modes
    other = []
    for n in range(depth // (2 * modes)):
        at = n * 2 * modes
        other += [grad[at + modes : at + 2 * modes], -grad[at : at + modes]]
    other = jnp.concatenate(other, axis=0)
    for p in range(4):
        cut = slice(p * CHANNELS, (p + 1) * CHANNELS)
        both = jnp.concatenate([grad[:, cut], other[:, cut]], axis=1).astype(BF16)
        tall = spec[:, cut].T
        for m in range(modes):
            out = mm(jnp.where(lane == m, tall, 0.0).astype(BF16), both).astype(BF16)
            out_ref[0, m, p] = out[:, :CHANNELS]
            out_ref[1, m, p] = out[:, CHANNELS:]


def rows_of(ref, step, at):
    count = ref.shape[0] // step
    return jnp.concatenate(
        [ref[n * step + at : n * step + at + 32, :] for n in range(count)], axis=0
    ).astype(F32)


def in_order(index, parts, ordered):
    rows = parts[0].shape[0]
    for k, part in enumerate(parts):
        at = pl.multiple_of((index ^ k) * rows, 16)
        ordered[pl.ds(at, rows), :] = part[...].astype(F32)


def weight_two_kernel(index_ref, *refs):
    early, _, out_ref, ordered = refs[:4], refs[4], refs[5], refs[6]
    in_order(index_ref[0], early, ordered)
    outer_products(rows_of(ordered, 96, 32), rows_of(ordered, 96, 64), out_ref)


def weight_one_kernel(factor, index_ref, *refs):
    early, late = refs[:4], refs[4:8]
    out_ref, one_ref, two_ref, bias_one_ref, bias_two_ref, early_all, late_all = refs[9:]
    in_order(index_ref[0], early, early_all)
    in_order(index_ref[0], late, late_all)
    sums = late_all[32:112, :]
    for n in range(1, 4):
        sums = sums + late_all[n * 112 + 32 : (n + 1) * 112, :]
    sums = sums * factor
    one = sums[:32, :LANES] + sums[:32, LANES:]
    one_ref[0:32, :] = one[:, :CHANNELS]
    one_ref[32:64, :] = one[:, CHANNELS:]
    two = jnp.concatenate([sums[32:64, :LANES], sums[32:64, LANES:]], axis=0)
    two_ref[...] = (two + turned(two))[:, :CHANNELS]
    bias = jnp.concatenate([sums[64:72, :LANES], sums[64:72, LANES:]], axis=0)
    bias = bias + turned(bias)
    bias_one_ref[...] = bias[0:1, :CHANNELS]
    bias_two_ref[...] = bias[8:9, :CHANNELS]
    outer_products(rows_of(early_all, 96, 0), rows_of(late_all, 112, 0), out_ref)


def weight_call(kernel, outs, index, parts, token):
    wide = 4 * CHANNELS
    heights = [4 * part.shape[0] for part in parts[::4]]
    return pl.pallas_call(
        kernel,
        out_shape=outs,
        in_specs=[pl.BlockSpec(memory_space=pltpu.SMEM)]
        + [VM] * len(parts)
        + [pl.BlockSpec(memory_space=pl.ANY)],
        out_specs=[VM] * len(outs),
        scratch_shapes=[pltpu.VMEM((height, wide), F32) for height in heights],
        cost_estimate=pl.CostEstimate(
            flops=200_000_000, bytes_accessed=3 << 20, transcendentals=0
        ),
        compiler_params=pltpu.CompilerParams(vmem_limit_bytes=VMEM_LIMIT),
    )(index, *parts[:4], *[near(part) for part in parts[4:]], token)


TILES = 128
PAIRS = TILES // 2
TILE = 2 * CHANNELS


def unpack_modes(got_ref, second_ref, depth, block=8):
    second = second_ref[...]
    left = side(32)
    for k in range(MZ):
        near = jnp.concatenate(
            [got_ref[d * block : d * block + 8, :] for d in range(k * 4, k * 4 + 4)], axis=0
        ) if block > 8 else got_ref[k * 32 : (k + 1) * 32, :].astype(F32)
        far = turned(near)
        top = jnp.concatenate([jnp.where(left, near, 0.0), jnp.where(left, far, 0.0)], axis=1)
        low = jnp.concatenate([jnp.where(left, 0.0, far), jnp.where(left, 0.0, near)], axis=1)
        out = mm(second, jnp.concatenate([top, low], axis=0).astype(BF16))
        for x in range(2):
            cut = slice(x * LANES, (x + 1) * LANES)
            depth[pl.ds(x * 2048 + k, 64, stride=32), :] = out[:64, cut]
            depth[pl.ds(x * 2048 + MZ + k, 64, stride=32), :] = out[64:, cut]


def pack_modes(spec, second_ref, out_ref, block=8):
    second = second_ref[...]
    left = side(32)
    for k in range(MZ):
        planes = [
            jnp.concatenate(
                [
                    spec[pl.ds(x * 2048 + k, 64, stride=32), :],
                    spec[pl.ds(x * 2048 + MZ + k, 64, stride=32), :],
                ],
                axis=0,
            )
            for x in range(2)
        ]
        out = mm(second, jnp.concatenate(planes, axis=1).astype(BF16))
        near, far = out[:, :LANES], out[:, LANES:]
        packed = jnp.where(left, near[:32] + turned(near[32:]), turned(far[:32]) + far[32:])
        if block == 8:
            out_ref[k * 32 : (k + 1) * 32, :] = packed.astype(out_ref.dtype)
        else:
            for d in range(4):
                at = (k * 4 + d) * block
                out_ref[at : at + 8, :] = packed[d * 8 : (d + 1) * 8]


def branch_of(depth, third, pair):
    at = pl.multiple_of(pair * 64, 64)
    wide = tn(depth[pl.ds(at, 64), :].astype(BF16), third)
    return wide[:, :LANES], wide[:, LANES:]


def store_spectrum(spec, third, pair, first, second):
    done = nt(third, jnp.concatenate([first, second], axis=0))
    at = pl.multiple_of(pair * 64, 64)
    spec[pl.ds(at, 32), :] = done[:, :LANES]
    spec[pl.ds(at + 32, 32), :] = done[:, LANES:]


def tile_at(tile):
    return pl.ds(pl.multiple_of(tile * TILE, TILE), TILE)


def gelu(preact):
    inner = preact * (ROOT + (ROOT * CUBIC) * (preact * preact))
    halved = 0.5 * preact
    return halved + halved * jnp.tanh(inner)


def gelu_slope(preact):
    square = preact * preact
    tangent = jnp.tanh(preact * (ROOT + (ROOT * CUBIC) * square))
    steep = (0.5 * preact) * (ROOT + (3.0 * ROOT * CUBIC) * square)
    return 0.5 + 0.5 * tangent + steep * (1.0 - tangent * tangent)


def hidden_kernel(small, big, outs, kinds, _, scratch, loop):
    got, inv2, inv3, fwd3, fwd2 = small
    (base,) = big
    hidden, preact = kinds
    depth, spec = scratch
    unpack_modes(got, inv2, depth)
    third_back = inv3[...]
    third = fwd3[...]

    def body(pair, carry):
        made = []
        for e, branch in enumerate(branch_of(depth, third_back, pair)):
            at = tile_at(2 * pair + e)
            pre = base[at, :].astype(F32) + branch
            preact[at, :] = pre.astype(BF16)
            value = gelu(pre).astype(BF16)
            hidden[at, :] = value
            made.append(value)
        store_spectrum(spec, third, pair, *made)
        return carry

    loop(body)
    pack_modes(spec, fwd2, outs[0])


def grad_two_kernel(small, big, outs, kinds, _, scratch, loop):
    got, inv2, inv3, fwd3, fwd2 = small
    base, cot = big
    (grad,) = kinds
    depth, spec = scratch
    unpack_modes(got, inv2, depth)
    third_back = inv3[...]
    third = fwd3[...]

    def body(pair, carry):
        made = []
        for e, branch in enumerate(branch_of(depth, third_back, pair)):
            at = tile_at(2 * pair + e)
            slope = gelu_slope(base[at, :].astype(F32) + branch)
            value = (cot[at, :].astype(F32) * slope).astype(BF16)
            grad[at, :] = value
            made.append(value)
        store_spectrum(spec, third, pair, *made)
        return carry

    loop(body)
    pack_modes(spec, fwd2, outs[0])


def grad_one_kernel(small, big, outs, _, __, scratch, loop):
    got, inv2, inv3, fwd3, fwd2 = small
    base, slope, values = big
    (out,) = outs
    depth, spec, wide, sent = scratch
    wide[...] = got[...].astype(F32)
    unpack_modes(wide, inv2, depth, 16)
    third_back = inv3[...]
    third = fwd3[...]
    ones = jnp.ones((16, 4 * LANES), BF16)

    def body(pair, total):
        made = []
        for e, branch in enumerate(branch_of(depth, third_back, pair)):
            at = tile_at(2 * pair + e)
            back = base[at, :].astype(F32) + branch
            made.append((back * slope[at, :].astype(F32)).astype(BF16))
        store_spectrum(spec, third, pair, *made)
        left = jnp.concatenate(
            [wide_tile(values, 2 * pair), wide_tile(values, 2 * pair + 1)], axis=1
        )
        right = jnp.concatenate(
            [part for tile in made for part in (tile[:CHANNELS], tile[CHANNELS:])], axis=1
        )
        return total + nt(jnp.concatenate([left, ones], axis=0), right)

    total = loop(body, jnp.zeros((CHANNELS + 16, CHANNELS), F32))
    pack_modes(spec, fwd2, sent, 48)
    left = side(1)

    def arrived_sum(place):
        row = jnp.sum(wide[pl.ds(place, 64, stride=16), :], axis=0, keepdims=True)
        row = row + turned(row)
        high = row.astype(BF16).astype(F32)
        return jnp.where(left, high, row - high)

    bias = jnp.concatenate([total[64:65], total[64:65]], axis=1)
    terms = jnp.concatenate(
        [
            jnp.concatenate([total[:32], total[32:64]], axis=1),
            bias,
            arrived_sum(8),
            arrived_sum(9),
            jnp.zeros((5, LANES), F32),
        ],
        axis=0,
    )
    for d in range(64):
        sent[d * 48 + 8 : (d + 1) * 48, :] = terms
    for d in range(64):
        out[d * 48 : (d + 1) * 48, :] = sent[d * 48 : (d + 1) * 48, :].astype(BF16)


def planes(kernel, kinds, *operands, big, token):
    scratch = [pltpu.VMEM((4096, LANES), F32), pltpu.VMEM((4096, LANES), F32)]
    return call(
        kernel,
        [CHUNK],
        scratch,
        1_000_000_000,
        20 << 20,
        *operands,
        big=big,
        kinds=kinds,
        token=token,
    )


def wide_tile(ref, tile):
    at = pl.multiple_of(tile * TILE, TILE)
    return jnp.concatenate(
        [ref[pl.ds(at, CHANNELS), :], ref[pl.ds(at + CHANNELS, CHANNELS), :]], axis=1
    )


def store_wide(ref, tile, wide):
    at = pl.multiple_of(tile * TILE, TILE)
    ref[pl.ds(at, CHANNELS), :] = wide[:, :LANES].astype(BF16)
    ref[pl.ds(at + CHANNELS, CHANNELS), :] = wide[:, LANES:].astype(BF16)


def point_kernel(small, big, _, kinds, __, scratch, loop):
    point, bias = small
    weights = point[...]
    shift = jnp.concatenate([bias[...], bias[...]], axis=1)

    def body(pair, carry):
        for tile in (2 * pair, 2 * pair + 1):
            store_wide(kinds[0], tile, mm(weights, wide_tile(big[0], tile)) + shift)
        return carry

    loop(body)


def slope_kernel(small, big, _, kinds, __, scratch, loop):
    def body(pair, carry):
        for tile in (2 * pair, 2 * pair + 1):
            at = tile_at(tile)
            kinds[0][at, :] = gelu_slope(big[0][at, :].astype(F32)).astype(BF16)
        return carry

    loop(body)


def point_back_kernel(small, big, outs, kinds, _, scratch, loop):
    weights = small[0][...]
    hidden, grad = big
    ones = jnp.ones((16, 4 * LANES), BF16)

    def body(pair, total):
        right = [wide_tile(grad, 2 * pair + e) for e in range(2)]
        for e in range(2):
            store_wide(kinds[0], 2 * pair + e, mm(weights, right[e]))
        left = jnp.concatenate(
            [wide_tile(hidden, 2 * pair), wide_tile(hidden, 2 * pair + 1)], axis=1
        )
        return total + nt(
            jnp.concatenate([left, ones], axis=0), jnp.concatenate(right, axis=1)
        )

    outs[0][...] = loop(body, jnp.zeros((CHANNELS + 16, CHANNELS), F32))


def body(field_in, cotangent, spectral_one, spectral_two, point_one, point_two, bias_one, bias_two):
    forward_c, inverse_c = complex_tables(LANES, MY)
    forward_z, inverse_z = real_tables(LANES, MZ)
    shape = spectral_one.shape
    const = lambda table: jnp.asarray(np.ascontiguousarray(table))

    natural_second = const(second_natural(forward_c))
    third_forward = const(forward_z.T)
    third_adjoint = const(inverse_z)
    third_inverse = const(twice_diagonal(inverse_z))
    third_back = const(twice_diagonal(forward_z.T))
    second_fwd = const(second_paired(forward_c))
    second_adj = const(second_paired(flipped(inverse_c)))
    second_inv = const(second_inverse(inverse_c))
    second_back = const(second_inverse(flipped(forward_c)))
    first_fwd = const(first_forward(forward_c))
    first_adj = const(first_forward(flipped(inverse_c)))
    first_inv = const(first_inverse(inverse_c))
    first_back = const(first_inverse(flipped(forward_c)))

    def exchange(chunk):
        return lax.all_to_all(chunk, "space", split_axis=0, concat_axis=0, tiled=True)

    def point_map(values, point, bias, token):
        return call(
            point_kernel,
            [],
            [],
            500_000_000,
            12 << 20,
            point.T,
            spread(bias),
            big=[values],
            kinds=[BF16],
            token=token,
        )[0]

    def samples(spectrum):
        size = 4
        return [spectrum] + [
            lax.ppermute(spectrum, "dp", [(i, i ^ k) for i in range(size)])
            for k in range(1, size)
        ]

    spread = lambda bias: jnp.broadcast_to(bias[:, None], (CHANNELS, LANES))

    chunk = first_partial(field_in, third_forward, natural_second)
    got = exchange(chunk)
    values = relay(field_in, chunk)

    chunk, spec_one = mixing(got, spectral_one, first_fwd, first_inv, token=values)
    got = exchange(chunk)
    base = point_map(values, point_one, bias_one, chunk)

    chunk, hidden, preact = planes(
        hidden_kernel,
        [BF16, BF16],
        got,
        second_inv,
        third_inverse,
        third_forward,
        second_fwd,
        big=[base],
        token=spec_one,
    )
    got = exchange(chunk)
    base = point_map(hidden, point_two, bias_two, chunk)

    chunk, spec_two = mixing(got, spectral_two, first_fwd, first_inv, token=base)
    got = exchange(chunk)
    cot = relay(cotangent, chunk)

    chunk, grad_two = planes(
        grad_two_kernel,
        [BF16],
        got,
        second_inv,
        third_inverse,
        third_adjoint,
        second_adj,
        big=[base, cot],
        token=spec_two,
    )
    got = exchange(chunk)
    term_two, base = call(
        point_back_kernel,
        [((CHANNELS + 16, CHANNELS), F32)],
        [],
        1_000_000_000,
        12 << 20,
        point_two,
        big=[hidden, grad_two],
        kinds=[BF16],
    )

    chunk, early = call(
        unmix_kernel,
        [((1024, LANES), BF16), ((96, 4 * CHANNELS), BF16)],
        [WIDE, pltpu.VMEM((1024, LANES), F32)],
        200_000_000,
        3 << 20,
        got,
        spectral_two,
        first_adj,
        first_back,
        term_two,
        spec_one,
        spec_two,
    )
    got = exchange(chunk)
    early = samples(early)
    slope = call(
        slope_kernel, [], [], 500_000_000, 12 << 20, big=[preact], kinds=[BF16], token=chunk
    )[0]

    chunk = call(
        grad_one_kernel,
        [((3072, LANES), BF16)],
        [
            pltpu.VMEM((4096, LANES), F32),
            pltpu.VMEM((4096, LANES), F32),
            pltpu.VMEM((1024, LANES), F32),
            pltpu.VMEM((3072, LANES), F32),
        ],
        1_500_000_000,
        20 << 20,
        got,
        second_back,
        third_back,
        third_adjoint,
        second_adj,
        big=[base, slope, values],
        token=early[1:],
    )[0]
    got = exchange(chunk)
    late = call(
        last_kernel,
        [((112, 4 * CHANNELS), BF16)],
        [pltpu.VMEM((3072, LANES), F32)],
        50_000_000,
        1 << 20,
        got,
        first_adj,
    )[0]
    index = lax.axis_index("dp").astype(jnp.int32).reshape(1)
    weights = jax.ShapeDtypeStruct(shape, BF16)
    spectral_grad_two = weight_call(weight_two_kernel, [weights], index, early, late)[0]
    late = samples(late)
    cells = lax.axis_size("dp") * lax.axis_size("space") * 2 * LANES * LANES
    square = jax.ShapeDtypeStruct((CHANNELS, CHANNELS), F32)
    line = jax.ShapeDtypeStruct((1, CHANNELS), F32)
    spectral_grad_one, point_grad_one, point_grad_two, bias_grad_one, bias_grad_two = weight_call(
        functools.partial(weight_one_kernel, 1.0 / math.sqrt(cells)),
        [weights, square, square, line, line],
        index,
        early + late,
        spectral_grad_two,
    )
    return (
        spectral_grad_one,
        spectral_grad_two,
        point_grad_one,
        point_grad_two,
        bias_grad_one.reshape(CHANNELS),
        bias_grad_two.reshape(CHANNELS),
    )


def solution(mesh):
    field = P("dp", None, "space", None, None)
    modes = P(None, None, "space", None, None)
    return jax.shard_map(
        body,
        mesh=mesh,
        in_specs=(field, field, modes, modes, P(), P(), P(), P()),
        out_specs=(modes, modes, P(), P(), P(), P()),
        check_vma=False,
    )
```

```python
import functools
import math

import jax
import jax.numpy as jnp
import numpy as np
from jax import lax
from jax.experimental import pallas as pl
from jax.experimental.pallas import tpu as pltpu
from jax.sharding import PartitionSpec as P

MY = 16
MZ = 16
CHANNELS = 64
LANES = 128
ROOT = math.sqrt(2.0 / math.pi)
CUBIC = 0.044715
F32 = jnp.float32
BF16 = jnp.bfloat16
VMEM_LIMIT = 44 * 1024 * 1024


def angles(length, modes, two_sided):
    places = np.arange(length, dtype=np.int64)[:, None]
    orders = np.arange(modes, dtype=np.int64)[None, :]
    if two_sided:
        orders = np.where(orders < modes // 2, orders, orders - modes + length)
    phases = places * orders % length
    return np.float32(2.0 * math.pi / length) * phases.astype(np.float32)


def complex_tables(length, modes):
    radians = angles(length, modes, True)
    factor = np.float32(1.0 / math.sqrt(length))
    cosines = np.cos(radians) * factor
    sines = np.sin(radians) * factor
    forward = np.stack(
        [np.stack([cosines, -sines], axis=1), np.stack([sines, cosines], axis=1)], axis=0
    )
    inverse = np.stack(
        [np.stack([cosines.T, sines.T], axis=1), np.stack([-sines.T, cosines.T], axis=1)], axis=0
    )
    return forward.astype(BF16), inverse.astype(BF16)


def real_tables(length, modes):
    radians = angles(length, modes, False)
    factor = np.float32(1.0 / math.sqrt(length))
    cosines = np.cos(radians) * factor
    sines = np.sin(radians) * factor
    forward = np.concatenate([cosines, -sines], axis=1)
    doubled = np.where(np.arange(modes) == 0, 1.0, 2.0).astype(np.float32)[None, :]
    inverse = np.concatenate([(cosines * doubled).T, (-sines * doubled).T], axis=0)
    return forward.astype(BF16), inverse.astype(BF16)


def flipped(table):
    return np.transpose(table, (2, 3, 0, 1))


def second_natural(table):
    length = table.shape[1]
    split = table.reshape(2, length, 2, MY // 4, 4)
    return split.transpose(3, 2, 4, 0, 1).reshape(2 * MY, 2 * length)


def second_paired(table):
    length = table.shape[1]
    split = table.reshape(2, length // 2, 2, 2, MY // 4, 4)
    return split.transpose(2, 4, 3, 5, 0, 1).reshape(4 * MY, length)


def second_inverse(table):
    length = table.shape[3]
    split = table.reshape(2, MY // 4, 4, 2, length // 2, 2)
    return split.transpose(3, 4, 5, 1, 0, 2).reshape(length, 4 * MY)


def first_forward(table):
    length, modes = table.shape[1], table.shape[3]
    split = table.reshape(2, length // 2, 2, 2, modes)
    return split.transpose(2, 3, 4, 0, 1).reshape(4 * modes, length)


def first_inverse(table):
    modes, length = table.shape[1], table.shape[3]
    split = table.reshape(2, modes, 2, length // 2, 2)
    return split.transpose(2, 3, 4, 0, 1).reshape(length, 4 * modes)


def twice_diagonal(table):
    zero = np.zeros_like(table)
    return np.block([[table, zero], [zero, table]])


def mm(left, right):
    return lax.dot_general(left, right, (((1,), (0,)), ((), ())), preferred_element_type=F32)


def nt(left, right):
    return lax.dot_general(left, right, (((1,), (1,)), ((), ())), preferred_element_type=F32)


def tn(left, right):
    return lax.dot_general(left, right, (((0,), (0,)), ((), ())), preferred_element_type=F32)


def side(rows):
    return lax.broadcasted_iota(jnp.int32, (rows, LANES), 1) < LANES // 2


def turned(values):
    return pltpu.roll(values, LANES // 2, 1)


def whole(shape):
    return pl.BlockSpec(shape, lambda *_: (0,) * len(shape))


VM = pl.BlockSpec(memory_space=pltpu.VMEM)


GROUPS = 4
ROWS = 2 * LANES * CHANNELS


def near(value):
    return pltpu.with_memory_space_constraint(value, pltpu.VMEM)


def afar(value):
    return pltpu.with_memory_space_constraint(value, pltpu.HBM)


def call(
    kernel, outs, scratch, flops, moved, *operands, big=(), kinds=(), plain=(), token=None
):
    cut = ROWS // GROUPS
    extra = [] if token is None else list(token) if isinstance(token, list) else [token]
    counts = [
        len(operands),
        len(big),
        len(extra),
        len(outs),
        len(kinds),
        len(plain),
        len(scratch),
        len(outs),
        len(big),
        len(kinds),
        3,
    ]

    def whole_kernel(*refs):
        parts = []
        at = 0
        for count in counts:
            parts.append(refs[at : at + count])
            at += count
        small, big_far, _, outs_far, kinds_far, plains, own, outs_near, big_near, kinds_near, sems = parts
        in_sem, out_sem, end_sem = sems

        def group_of(far, close, sem, index, group, out):
            rows = pl.ds(pl.multiple_of(group * cut, cut), cut)
            pair = (close.at[rows], far.at[rows]) if out else (far.at[rows], close.at[rows])
            return pltpu.make_async_copy(*pair, sem.at[index, group])

        def coming(index, group):
            return group_of(big_far[index], big_near[index], in_sem, index, group, False)

        def going(index, group):
            return group_of(kinds_far[index], kinds_near[index], out_sem, index, group, True)

        for group in range(GROUPS):
            for index in range(len(big)):
                coming(index, group).start()

        def loop(body, carry=0, unroll=PAIRS // GROUPS):
            per = PAIRS // GROUPS

            def some(i, carry):
                for j in range(unroll):
                    carry = body(i * unroll + j, carry)
                return carry

            def each(group, carry):
                for index in range(len(big)):
                    coming(index, group).wait()
                first = group * (per // unroll)
                carry = lax.fori_loop(first, first + per // unroll, some, carry)
                for index in range(len(kinds)):
                    going(index, group).start()
                return carry

            return lax.fori_loop(0, GROUPS, each, carry)

        kernel(small, big_near, outs_near, kinds_near, plains, own, loop)
        last = [
            pltpu.make_async_copy(close, far, end_sem.at[index])
            for index, (close, far) in enumerate(zip(outs_near, outs_far))
        ]
        for copy in last:
            copy.start()
        for index in range(len(kinds)):
            for group in range(GROUPS):
                going(index, group).wait()
        for copy in last:
            copy.wait()

    operands = [near(operand) for operand in operands]
    far = pl.BlockSpec(memory_space=pl.ANY)
    shapes = [pltpu.HBM(shape, kind) for shape, kind in outs]
    shapes += [pltpu.HBM((ROWS, LANES), kind) for kind in kinds]
    return pl.pallas_call(
        whole_kernel,
        out_shape=shapes + list(plain),
        in_specs=[VM] * len(operands) + [far] * (len(big) + len(extra)),
        out_specs=[far] * len(shapes) + [VM] * len(plain),
        scratch_shapes=list(scratch)
        + [pltpu.VMEM(shape, kind) for shape, kind in outs]
        + [pltpu.VMEM((ROWS, LANES), array.dtype) for array in big]
        + [pltpu.VMEM((ROWS, LANES), kind) for kind in kinds]
        + [
            pltpu.SemaphoreType.DMA((max(len(big), 1), GROUPS)),
            pltpu.SemaphoreType.DMA((max(len(kinds), 1), GROUPS)),
            pltpu.SemaphoreType.DMA((max(len(outs), 1),)),
        ],
        cost_estimate=pl.CostEstimate(flops=flops, bytes_accessed=moved, transcendentals=0),
        compiler_params=pltpu.CompilerParams(vmem_limit_bytes=VMEM_LIMIT),
    )(*operands, *[afar(array) for array in (*big, *extra)])


C_STEP = 8


def spectrum_kernel(field, third_far, second_far, out_far, near_field, third_ref, second_ref, chunk, spec, sems, extra):
    def coming(step):
        cut = pl.ds(step * C_STEP, C_STEP)
        return pltpu.make_async_copy(field.at[0, cut], near_field.at[cut], sems.at[step])

    tables = [
        pltpu.make_async_copy(third_far, third_ref, extra.at[0]),
        pltpu.make_async_copy(second_far, second_ref, extra.at[1]),
    ]
    for copy in tables:
        copy.start()
    for step in range(CHANNELS // C_STEP):
        coming(step).start()
    for copy in tables:
        copy.wait()
    third = third_ref[...]

    def some(step, carry):
        coming(step).wait()
        for x in range(2):
            rows = near_field[pl.ds(step * C_STEP, C_STEP), x].reshape(C_STEP * LANES, LANES)
            done = nt(third, rows)
            for c in range(C_STEP):
                place = pl.multiple_of((x * CHANNELS + step * C_STEP + c) * 2 * MZ, 2 * MZ)
                spec[pl.ds(place, 2 * MZ), :] = done[:, c * LANES : (c + 1) * LANES]
        return carry

    lax.fori_loop(0, CHANNELS // C_STEP, some, 0)
    second = second_ref[...]
    for k in range(MZ):
        real = spec[pl.ds(k, LANES, stride=2 * MZ), :]
        imag = spec[pl.ds(MZ + k, LANES, stride=2 * MZ), :]
        both = jnp.concatenate([real, imag], axis=1).astype(BF16)
        chunk[k * 32 : (k + 1) * 32, :] = nt(second, both).astype(BF16)
    out = pltpu.make_async_copy(chunk, out_far, extra.at[2])
    out.start()
    out.wait()


def first_partial(field, third, second):
    far = pl.BlockSpec(memory_space=pl.ANY)
    return pl.pallas_call(
        spectrum_kernel,
        out_shape=pltpu.HBM((512, LANES), BF16),
        in_specs=[far] * 3,
        out_specs=far,
        scratch_shapes=[
            pltpu.VMEM(field.shape[1:], BF16),
            pltpu.VMEM(third.shape, BF16),
            pltpu.VMEM(second.shape, BF16),
            pltpu.VMEM((512, LANES), BF16),
            pltpu.VMEM((4096, LANES), F32),
            pltpu.SemaphoreType.DMA((CHANNELS // C_STEP,)),
            pltpu.SemaphoreType.DMA((3,)),
        ],
        cost_estimate=pl.CostEstimate(
            flops=600_000_000, bytes_accessed=6 << 20, transcendentals=0
        ),
        compiler_params=pltpu.CompilerParams(vmem_limit_bytes=VMEM_LIMIT),
    )(afar(field), afar(third), afar(second))


Y_STEP = 16
Y_STEPS = LANES // Y_STEP
Y_ROWS = Y_STEP * CHANNELS


def relay_kernel(field, _, out_far, near_field, out_near, rows_ref, in_sem, out_sem):
    def coming(step):
        x = step // Y_STEPS
        cut = pl.ds(pl.multiple_of((step % Y_STEPS) * Y_STEP, Y_STEP), Y_STEP)
        return pltpu.make_async_copy(
            field.at[0, :, x, cut], near_field.at[:, x, cut], in_sem.at[step]
        )

    def going(step):
        cut = pl.ds(pl.multiple_of(step * Y_ROWS, Y_ROWS), Y_ROWS)
        return pltpu.make_async_copy(out_near.at[cut], out_far.at[cut], out_sem.at[step])

    for step in range(2 * Y_STEPS):
        coming(step).start()

    def some(step, carry):
        coming(step).wait()
        at = pl.multiple_of((step % Y_STEPS) * Y_STEP, Y_STEP)
        rows_ref[...] = (
            near_field[:, step // Y_STEPS, pl.ds(at, Y_STEP), :].astype(F32).reshape(Y_ROWS, LANES)
        )
        for y in range(0, Y_STEP, 2):
            pair = [rows_ref[pl.ds(y + e, CHANNELS, stride=Y_STEP), :] for e in range(2)]
            tile = step * (Y_STEP // 2) + y // 2
            out_near[tile_at(tile), :] = jnp.concatenate(pair, axis=0).astype(BF16)
        going(step).start()
        return carry

    lax.fori_loop(0, 2 * Y_STEPS, some, 0)
    for step in range(2 * Y_STEPS):
        going(step).wait()


def relay(field, token):
    far = pl.BlockSpec(memory_space=pl.ANY)
    return pl.pallas_call(
        relay_kernel,
        out_shape=pltpu.HBM((ROWS, LANES), BF16),
        in_specs=[far] * 2,
        out_specs=far,
        scratch_shapes=[
            pltpu.VMEM(field.shape[1:], BF16),
            pltpu.VMEM((ROWS, LANES), BF16),
            pltpu.VMEM((Y_ROWS, LANES), F32),
            pltpu.SemaphoreType.DMA((2 * Y_STEPS,)),
            pltpu.SemaphoreType.DMA((2 * Y_STEPS,)),
        ],
        cost_estimate=pl.CostEstimate(
            flops=600_000_000, bytes_accessed=12 << 20, transcendentals=0
        ),
        compiler_params=pltpu.CompilerParams(vmem_limit_bytes=VMEM_LIMIT),
    )(afar(field), afar(token))


def own_spectrum(wide, table, place, block=8):
    real = wide[pl.ds(place, 64, stride=block), :]
    imag = wide[pl.ds(4 + place, 64, stride=block), :]
    both = mm(table, jnp.concatenate([real, imag], axis=0).astype(BF16))
    return both[:32, :CHANNELS] + both[32:, CHANNELS:]


def send_field(mixed, table, place, sent, block=8):
    twin = jnp.concatenate([mixed, mixed], axis=1)
    left = side(32)
    both = jnp.concatenate([jnp.where(left, twin, 0.0), jnp.where(left, 0.0, twin)], axis=0)
    out = mm(table, both.astype(BF16))
    sent[pl.ds(place, 64, stride=block), :] = out[:64]
    sent[pl.ds(4 + place, 64, stride=block), :] = out[64:]


def mode_lanes(modes):
    row = lax.broadcasted_iota(jnp.int32, (32, LANES), 0) % modes
    half = lax.broadcasted_iota(jnp.int32, (32, LANES), 1) // CHANNELS
    return row, half


def mix_kernel(small, _, outs, __, ___, scratch, loop):
    got_ref, weight_ref, forward_ref, inverse_ref = small
    out_ref, spec_ref = outs
    wide, sent = scratch
    wide[...] = got_ref[...].astype(F32)
    forward = forward_ref[...]
    inverse = inverse_ref[...]
    modes = weight_ref.shape[1]
    row, half = mode_lanes(modes)
    for p in range(4):
        spec = own_spectrum(wide, forward, p).astype(BF16)
        spec_ref[:, p * CHANNELS : (p + 1) * CHANNELS] = spec
        spec = spec.astype(F32)
        other = jnp.concatenate([-spec[modes:], spec[:modes]], axis=0)
        pieces = []
        for part in (spec, other):
            twin = jnp.concatenate([part, part], axis=1)
            for pair in range(modes // 2):
                pieces.append(jnp.where(row == 2 * pair + half, twin, 0.0).astype(BF16))
        spread = jnp.concatenate(pieces, axis=1)
        weights = weight_ref[:, :, p].reshape(2 * modes * CHANNELS, CHANNELS)
        mixed = mm(spread, weights).astype(BF16).astype(F32)
        send_field(mixed, inverse, p, sent)
    out_ref[...] = sent[...].astype(BF16)


def high_low(values):
    high = values.astype(BF16).astype(F32)
    return jnp.concatenate([high, values - high], axis=1)


def unmix_kernel(small, _, outs, __, ___, scratch, loop):
    got_ref, weight_ref, forward_ref, inverse_ref, term_ref, one_ref, two_ref = small
    out_ref, spec_ref = outs
    wide, sent = scratch
    wide[...] = got_ref[...].astype(F32)
    forward = forward_ref[...]
    inverse = inverse_ref[...]
    modes = weight_ref.shape[1]
    row, half = mode_lanes(modes)
    spec_ref[0:32, :] = one_ref[...]
    spec_ref[32:64, :] = two_ref[...]
    sent[...] = jnp.zeros_like(sent)
    terms = high_low(term_ref[...])
    sent[pl.ds(8, 64, stride=16), :] = terms[:CHANNELS]
    sent[pl.ds(9, 64, stride=16), :] = jnp.broadcast_to(
        terms[CHANNELS : CHANNELS + 1], (CHANNELS, LANES)
    )
    for p in range(4):
        spec = own_spectrum(wide, forward, p).astype(BF16)
        spec_ref[64:96, p * CHANNELS : (p + 1) * CHANNELS] = spec
        other = jnp.concatenate([spec[modes:].astype(F32), -spec[:modes].astype(F32)], axis=0)
        products = nt(spec, weight_ref[0, :, p].reshape(modes * CHANNELS, CHANNELS)) + nt(
            other.astype(BF16), weight_ref[1, :, p].reshape(modes * CHANNELS, CHANNELS)
        )
        total = jnp.zeros((32, LANES), F32)
        for pair in range(modes // 2):
            piece = products[:, pair * LANES : (pair + 1) * LANES]
            total = total + jnp.where(row == 2 * pair + half, piece, 0.0)
        mixed = (total + turned(total))[:, :CHANNELS].astype(BF16).astype(F32)
        send_field(mixed, inverse, p, sent, 16)
    out_ref[...] = sent[...].astype(BF16)


def last_kernel(small, _, outs, __, ___, scratch, loop):
    got_ref, forward_ref = small
    (out_ref,) = outs
    (wide,) = scratch
    for d in range(64):
        wide[d * 48 : (d + 1) * 48, :] = got_ref[d * 48 : (d + 1) * 48, :].astype(F32)
    forward = forward_ref[...]
    for p in range(4):
        out_ref[0:32, p * CHANNELS : (p + 1) * CHANNELS] = own_spectrum(
            wide, forward, p, 48
        ).astype(BF16)
    total = jnp.zeros((40, LANES), F32)
    for d in range(64):
        total = total + wide[d * 48 + 8 : (d + 1) * 48, :]
    high = total.astype(BF16)
    low = (total - high.astype(F32)).astype(BF16)
    out_ref[32:64, :] = jnp.concatenate([high[:32], low[:32]], axis=1)
    rows = wide[pl.ds(41, 64, stride=48), :]
    out_ref[64:96, :] = jnp.concatenate([rows[:32], rows[32:]], axis=1).astype(BF16)
    biases = jnp.concatenate(
        [
            high_low(total[32:40, :CHANNELS]),
            jnp.broadcast_to(wide[42:43, :], (8, LANES)),
        ],
        axis=1,
    )
    out_ref[96:112, :] = jnp.concatenate([biases, biases], axis=0).astype(BF16)


CHUNK = ((512, LANES), BF16)
SPECTRUM = ((32, 4 * CHANNELS), BF16)
WIDE = pltpu.VMEM((512, LANES), F32)


def mixing(got, weights, forward, inverse, token):
    return call(
        mix_kernel,
        [CHUNK, SPECTRUM],
        [WIDE, WIDE],
        200_000_000,
        3 << 20,
        got,
        weights,
        forward,
        inverse,
        token=token,
    )


def outer_products(spec, grad, out_ref):
    modes = out_ref.shape[1]
    depth = spec.shape[0]
    lane = lax.broadcasted_iota(jnp.int32, (CHANNELS, depth), 1) % modes
    other = []
    for n in range(depth // (2 * modes)):
        at = n * 2 * modes
        other += [grad[at + modes : at + 2 * modes], -grad[at : at + modes]]
    other = jnp.concatenate(other, axis=0)
    for p in range(4):
        cut = slice(p * CHANNELS, (p + 1) * CHANNELS)
        both = jnp.concatenate([grad[:, cut], other[:, cut]], axis=1).astype(BF16)
        tall = spec[:, cut].T
        for m in range(modes):
            out = mm(jnp.where(lane == m, tall, 0.0).astype(BF16), both).astype(BF16)
            out_ref[0, m, p] = out[:, :CHANNELS]
            out_ref[1, m, p] = out[:, CHANNELS:]


def rows_of(ref, step, at):
    count = ref.shape[0] // step
    return jnp.concatenate(
        [ref[n * step + at : n * step + at + 32, :] for n in range(count)], axis=0
    ).astype(F32)


def in_order(index, parts, ordered, sems):
    rows = parts[0].shape[0]
    copies = []
    for k, part in enumerate(parts):
        at = pl.multiple_of((index ^ k) * rows, 16)
        copies.append(pltpu.make_async_copy(part, ordered.at[pl.ds(at, rows)], sems.at[k]))
    for copy in copies:
        copy.start()
    return copies


def weight_two_kernel(index_ref, *refs):
    early, _, out_ref, ordered, sems = refs[:4], refs[4], refs[5], refs[6], refs[7]
    for copy in in_order(index_ref[0], early, ordered, sems):
        copy.wait()
    outer_products(rows_of(ordered, 96, 32), rows_of(ordered, 96, 64), out_ref)


def weight_one_kernel(factor, index_ref, *refs):
    early, late = refs[:4], refs[4:8]
    out_ref, one_ref, two_ref, bias_one_ref, bias_two_ref = refs[9:14]
    early_all, late_all, early_sems, late_sems = refs[14:]
    copies = in_order(index_ref[0], early, early_all, early_sems)
    copies += in_order(index_ref[0], late, late_all, late_sems)
    for copy in copies:
        copy.wait()
    sums = late_all[32:112, :].astype(F32)
    for n in range(1, 4):
        sums = sums + late_all[n * 112 + 32 : (n + 1) * 112, :].astype(F32)
    sums = sums * factor
    one = sums[:32, :LANES] + sums[:32, LANES:]
    one_ref[0:32, :] = one[:, :CHANNELS]
    one_ref[32:64, :] = one[:, CHANNELS:]
    two = jnp.concatenate([sums[32:64, :LANES], sums[32:64, LANES:]], axis=0)
    two_ref[...] = (two + turned(two))[:, :CHANNELS]
    bias = jnp.concatenate([sums[64:72, :LANES], sums[64:72, LANES:]], axis=0)
    bias = bias + turned(bias)
    bias_one_ref[...] = bias[0:1, :CHANNELS]
    bias_two_ref[...] = bias[8:9, :CHANNELS]
    outer_products(rows_of(early_all, 96, 0), rows_of(late_all, 112, 0), out_ref)


def weight_call(kernel, outs, index, early, late, token):
    parts = [afar(part) for part in early + late[:1]] + [near(part) for part in late[1:]]
    groups = [early, late] if late else [early]
    far = pl.BlockSpec(memory_space=pl.ANY)
    return pl.pallas_call(
        kernel,
        out_shape=outs,
        in_specs=[pl.BlockSpec(memory_space=pltpu.SMEM)] + [far] * len(early + late[:1]) + [VM] * len(late[1:]) + [far],
        out_specs=[VM] * len(outs),
        scratch_shapes=[
            pltpu.VMEM((4 * group[0].shape[0], 4 * CHANNELS), BF16) for group in groups
        ]
        + [pltpu.SemaphoreType.DMA((4,)) for _ in groups],
        cost_estimate=pl.CostEstimate(
            flops=200_000_000, bytes_accessed=3 << 20, transcendentals=0
        ),
        compiler_params=pltpu.CompilerParams(vmem_limit_bytes=VMEM_LIMIT),
    )(index, *parts, afar(token))


TILES = 128
PAIRS = TILES // 2
TILE = 2 * CHANNELS


def unpack_modes(got_ref, second_ref, depth, block=8):
    second = second_ref[...]
    left = side(32)
    for k in range(MZ):
        near = jnp.concatenate(
            [got_ref[d * block : d * block + 8, :] for d in range(k * 4, k * 4 + 4)], axis=0
        ) if block > 8 else got_ref[k * 32 : (k + 1) * 32, :].astype(F32)
        far = turned(near)
        top = jnp.concatenate([jnp.where(left, near, 0.0), jnp.where(left, far, 0.0)], axis=1)
        low = jnp.concatenate([jnp.where(left, 0.0, far), jnp.where(left, 0.0, near)], axis=1)
        out = mm(second, jnp.concatenate([top, low], axis=0).astype(BF16))
        for x in range(2):
            cut = slice(x * LANES, (x + 1) * LANES)
            depth[pl.ds(x * 2048 + k, 64, stride=32), :] = out[:64, cut]
            depth[pl.ds(x * 2048 + MZ + k, 64, stride=32), :] = out[64:, cut]


def pack_modes(spec, second_ref, out_ref, block=8):
    second = second_ref[...]
    left = side(32)
    for k in range(MZ):
        planes = [
            jnp.concatenate(
                [
                    spec[pl.ds(x * 2048 + k, 64, stride=32), :],
                    spec[pl.ds(x * 2048 + MZ + k, 64, stride=32), :],
                ],
                axis=0,
            )
            for x in range(2)
        ]
        out = mm(second, jnp.concatenate(planes, axis=1).astype(BF16))
        near, far = out[:, :LANES], out[:, LANES:]
        packed = jnp.where(left, near[:32] + turned(near[32:]), turned(far[:32]) + far[32:])
        if block == 8:
            out_ref[k * 32 : (k + 1) * 32, :] = packed.astype(out_ref.dtype)
        else:
            for d in range(4):
                at = (k * 4 + d) * block
                out_ref[at : at + 8, :] = packed[d * 8 : (d + 1) * 8]


def branch_of(depth, third, pair):
    at = pl.multiple_of(pair * 64, 64)
    wide = tn(depth[pl.ds(at, 64), :].astype(BF16), third)
    return wide[:, :LANES], wide[:, LANES:]


def store_spectrum(spec, third, pair, first, second):
    done = nt(third, jnp.concatenate([first, second], axis=0))
    at = pl.multiple_of(pair * 64, 64)
    spec[pl.ds(at, 32), :] = done[:, :LANES]
    spec[pl.ds(at + 32, 32), :] = done[:, LANES:]


def tile_at(tile):
    return pl.ds(pl.multiple_of(tile * TILE, TILE), TILE)


def gelu(preact):
    inner = preact * (ROOT + (ROOT * CUBIC) * (preact * preact))
    halved = 0.5 * preact
    return halved + halved * jnp.tanh(inner)


def gelu_slope(preact):
    square = preact * preact
    tangent = jnp.tanh(preact * (ROOT + (ROOT * CUBIC) * square))
    steep = (0.5 * preact) * (ROOT + (3.0 * ROOT * CUBIC) * square)
    return 0.5 + 0.5 * tangent + steep * (1.0 - tangent * tangent)


def hidden_kernel(small, big, outs, kinds, _, scratch, loop):
    got, inv2, inv3, fwd3, fwd2 = small
    (base,) = big
    hidden, preact = kinds
    depth, spec = scratch
    unpack_modes(got, inv2, depth)
    third_back = inv3[...]
    third = fwd3[...]

    def body(pair, carry):
        made = []
        for e, branch in enumerate(branch_of(depth, third_back, pair)):
            at = tile_at(2 * pair + e)
            pre = base[at, :].astype(F32) + branch
            preact[at, :] = pre.astype(BF16)
            value = gelu(pre).astype(BF16)
            hidden[at, :] = value
            made.append(value)
        store_spectrum(spec, third, pair, *made)
        return carry

    loop(body)
    pack_modes(spec, fwd2, outs[0])


def grad_two_kernel(small, big, outs, kinds, _, scratch, loop):
    got, inv2, inv3, fwd3, fwd2 = small
    base, cot = big
    (grad,) = kinds
    depth, spec = scratch
    unpack_modes(got, inv2, depth)
    third_back = inv3[...]
    third = fwd3[...]

    def body(pair, carry):
        made = []
        for e, branch in enumerate(branch_of(depth, third_back, pair)):
            at = tile_at(2 * pair + e)
            slope = gelu_slope(base[at, :].astype(F32) + branch)
            value = (cot[at, :].astype(F32) * slope).astype(BF16)
            grad[at, :] = value
            made.append(value)
        store_spectrum(spec, third, pair, *made)
        return carry

    loop(body)
    pack_modes(spec, fwd2, outs[0])


def grad_one_kernel(small, big, outs, _, __, scratch, loop):
    got, inv2, inv3, fwd3, fwd2 = small
    base, slope, values = big
    (out,) = outs
    depth, spec, wide, sent = scratch
    wide[...] = got[...].astype(F32)
    unpack_modes(wide, inv2, depth, 16)
    third_back = inv3[...]
    third = fwd3[...]
    ones = jnp.ones((16, 4 * LANES), BF16)

    def body(pair, total):
        made = []
        for e, branch in enumerate(branch_of(depth, third_back, pair)):
            at = tile_at(2 * pair + e)
            back = base[at, :].astype(F32) + branch
            made.append((back * slope[at, :].astype(F32)).astype(BF16))
        store_spectrum(spec, third, pair, *made)
        left = jnp.concatenate(
            [wide_tile(values, 2 * pair), wide_tile(values, 2 * pair + 1)], axis=1
        )
        right = jnp.concatenate(
            [part for tile in made for part in (tile[:CHANNELS], tile[CHANNELS:])], axis=1
        )
        return total + nt(jnp.concatenate([left, ones], axis=0), right)

    total = loop(body, jnp.zeros((CHANNELS + 16, CHANNELS), F32))
    pack_modes(spec, fwd2, sent, 48)
    left = side(1)

    def arrived_sum(place):
        row = jnp.sum(wide[pl.ds(place, 64, stride=16), :], axis=0, keepdims=True)
        row = row + turned(row)
        high = row.astype(BF16).astype(F32)
        return jnp.where(left, high, row - high)

    bias = jnp.concatenate([total[64:65], total[64:65]], axis=1)
    terms = jnp.concatenate(
        [
            jnp.concatenate([total[:32], total[32:64]], axis=1),
            bias,
            arrived_sum(8),
            arrived_sum(9),
            jnp.zeros((5, LANES), F32),
        ],
        axis=0,
    )
    for d in range(64):
        sent[d * 48 + 8 : (d + 1) * 48, :] = terms
    for d in range(64):
        out[d * 48 : (d + 1) * 48, :] = sent[d * 48 : (d + 1) * 48, :].astype(BF16)


def planes(kernel, kinds, *operands, big, token):
    scratch = [pltpu.VMEM((4096, LANES), F32), pltpu.VMEM((4096, LANES), F32)]
    return call(
        kernel,
        [CHUNK],
        scratch,
        1_000_000_000,
        20 << 20,
        *operands,
        big=big,
        kinds=kinds,
        token=token,
    )


def wide_tile(ref, tile):
    at = pl.multiple_of(tile * TILE, TILE)
    return jnp.concatenate(
        [ref[pl.ds(at, CHANNELS), :], ref[pl.ds(at + CHANNELS, CHANNELS), :]], axis=1
    )


def store_wide(ref, tile, wide):
    at = pl.multiple_of(tile * TILE, TILE)
    ref[pl.ds(at, CHANNELS), :] = wide[:, :LANES].astype(BF16)
    ref[pl.ds(at + CHANNELS, CHANNELS), :] = wide[:, LANES:].astype(BF16)


def point_kernel(small, big, _, kinds, __, scratch, loop):
    point, bias = small
    weights = point[...]
    shift = jnp.concatenate([bias[...], bias[...]], axis=1)

    def body(pair, carry):
        for tile in (2 * pair, 2 * pair + 1):
            store_wide(kinds[0], tile, mm(weights, wide_tile(big[0], tile)) + shift)
        return carry

    loop(body)


def slope_kernel(small, big, _, kinds, __, scratch, loop):
    def body(pair, carry):
        for tile in (2 * pair, 2 * pair + 1):
            at = tile_at(tile)
            kinds[0][at, :] = gelu_slope(big[0][at, :].astype(F32)).astype(BF16)
        return carry

    loop(body)


def point_back_kernel(small, big, outs, kinds, _, scratch, loop):
    weights = small[0][...]
    hidden, grad = big
    ones = jnp.ones((16, 4 * LANES), BF16)

    def body(pair, total):
        right = [wide_tile(grad, 2 * pair + e) for e in range(2)]
        for e in range(2):
            store_wide(kinds[0], 2 * pair + e, mm(weights, right[e]))
        left = jnp.concatenate(
            [wide_tile(hidden, 2 * pair), wide_tile(hidden, 2 * pair + 1)], axis=1
        )
        return total + nt(
            jnp.concatenate([left, ones], axis=0), jnp.concatenate(right, axis=1)
        )

    outs[0][...] = loop(body, jnp.zeros((CHANNELS + 16, CHANNELS), F32))


def body(field_in, cotangent, spectral_one, spectral_two, point_one, point_two, bias_one, bias_two):
    forward_c, inverse_c = complex_tables(LANES, MY)
    forward_z, inverse_z = real_tables(LANES, MZ)
    shape = spectral_one.shape
    const = lambda table: jnp.asarray(np.ascontiguousarray(table))

    natural_second = const(second_natural(forward_c))
    third_forward = const(forward_z.T)
    third_adjoint = const(inverse_z)
    third_inverse = const(twice_diagonal(inverse_z))
    third_back = const(twice_diagonal(forward_z.T))
    second_fwd = const(second_paired(forward_c))
    second_adj = const(second_paired(flipped(inverse_c)))
    second_inv = const(second_inverse(inverse_c))
    second_back = const(second_inverse(flipped(forward_c)))
    first_fwd = const(first_forward(forward_c))
    first_adj = const(first_forward(flipped(inverse_c)))
    first_inv = const(first_inverse(inverse_c))
    first_back = const(first_inverse(flipped(forward_c)))

    def exchange(chunk):
        return lax.all_to_all(chunk, "space", split_axis=0, concat_axis=0, tiled=True)

    def point_map(values, point, bias, token):
        return call(
            point_kernel,
            [],
            [],
            500_000_000,
            12 << 20,
            point.T,
            spread(bias),
            big=[values],
            kinds=[BF16],
            token=token,
        )[0]

    def samples(spectrum):
        size = 4
        return [spectrum] + [
            lax.ppermute(spectrum, "dp", [(i, i ^ k) for i in range(size)])
            for k in range(1, size)
        ]

    spread = lambda bias: jnp.broadcast_to(bias[:, None], (CHANNELS, LANES))

    chunk = first_partial(field_in, third_forward, natural_second)
    got = exchange(chunk)
    values = relay(field_in, chunk)

    chunk, spec_one = mixing(got, spectral_one, first_fwd, first_inv, token=values)
    got = exchange(chunk)
    base = point_map(values, point_one, bias_one, chunk)

    chunk, hidden, preact = planes(
        hidden_kernel,
        [BF16, BF16],
        got,
        second_inv,
        third_inverse,
        third_forward,
        second_fwd,
        big=[base],
        token=spec_one,
    )
    got = exchange(chunk)
    base = point_map(hidden, point_two, bias_two, chunk)

    chunk, spec_two = mixing(got, spectral_two, first_fwd, first_inv, token=base)
    got = exchange(chunk)
    cot = relay(cotangent, chunk)

    chunk, grad_two = planes(
        grad_two_kernel,
        [BF16],
        got,
        second_inv,
        third_inverse,
        third_adjoint,
        second_adj,
        big=[base, cot],
        token=spec_two,
    )
    got = exchange(chunk)
    term_two, base = call(
        point_back_kernel,
        [((CHANNELS + 16, CHANNELS), F32)],
        [],
        1_000_000_000,
        12 << 20,
        point_two,
        big=[hidden, grad_two],
        kinds=[BF16],
    )

    chunk, early = call(
        unmix_kernel,
        [((1024, LANES), BF16), ((96, 4 * CHANNELS), BF16)],
        [WIDE, pltpu.VMEM((1024, LANES), F32)],
        200_000_000,
        3 << 20,
        got,
        spectral_two,
        first_adj,
        first_back,
        term_two,
        spec_one,
        spec_two,
    )
    got = exchange(chunk)
    early = samples(early)
    slope = call(
        slope_kernel, [], [], 500_000_000, 12 << 20, big=[preact], kinds=[BF16], token=chunk
    )[0]

    chunk = call(
        grad_one_kernel,
        [((3072, LANES), BF16)],
        [
            pltpu.VMEM((4096, LANES), F32),
            pltpu.VMEM((4096, LANES), F32),
            pltpu.VMEM((1024, LANES), F32),
            pltpu.VMEM((3072, LANES), F32),
        ],
        1_500_000_000,
        20 << 20,
        got,
        second_back,
        third_back,
        third_adjoint,
        second_adj,
        big=[base, slope, values],
        token=early[1:],
    )[0]
    got = exchange(chunk)
    late = call(
        last_kernel,
        [((112, 4 * CHANNELS), BF16)],
        [pltpu.VMEM((3072, LANES), F32)],
        50_000_000,
        1 << 20,
        got,
        first_adj,
    )[0]
    index = lax.axis_index("dp").astype(jnp.int32).reshape(1)
    weights = jax.ShapeDtypeStruct(shape, BF16)
    spectral_grad_two = weight_call(weight_two_kernel, [weights], index, early, [], late)[0]
    late = samples(late)
    cells = lax.axis_size("dp") * lax.axis_size("space") * 2 * LANES * LANES
    square = jax.ShapeDtypeStruct((CHANNELS, CHANNELS), F32)
    line = jax.ShapeDtypeStruct((1, CHANNELS), F32)
    spectral_grad_one, point_grad_one, point_grad_two, bias_grad_one, bias_grad_two = weight_call(
        functools.partial(weight_one_kernel, 1.0 / math.sqrt(cells)),
        [weights, square, square, line, line],
        index,
        early,
        late,
        spectral_grad_two,
    )
    return (
        spectral_grad_one,
        spectral_grad_two,
        point_grad_one,
        point_grad_two,
        bias_grad_one.reshape(CHANNELS),
        bias_grad_two.reshape(CHANNELS),
    )


def solution(mesh):
    field = P("dp", None, "space", None, None)
    modes = P(None, None, "space", None, None)
    return jax.shard_map(
        body,
        mesh=mesh,
        in_specs=(field, field, modes, modes, P(), P(), P(), P()),
        out_specs=(modes, modes, P(), P(), P(), P()),
        check_vma=False,
    )
```

```python
import functools
import math

import jax
import jax.numpy as jnp
import numpy as np
from jax import lax
from jax.experimental import pallas as pl
from jax.experimental.pallas import tpu as pltpu
from jax.sharding import PartitionSpec as P

MY = 16
MZ = 16
CHANNELS = 64
LANES = 128
ROOT = math.sqrt(2.0 / math.pi)
CUBIC = 0.044715
F32 = jnp.float32
BF16 = jnp.bfloat16
VMEM_LIMIT = 44 * 1024 * 1024


def angles(length, modes, two_sided):
    places = np.arange(length, dtype=np.int64)[:, None]
    orders = np.arange(modes, dtype=np.int64)[None, :]
    if two_sided:
        orders = np.where(orders < modes // 2, orders, orders - modes + length)
    phases = places * orders % length
    return np.float32(2.0 * math.pi / length) * phases.astype(np.float32)


def complex_tables(length, modes):
    radians = angles(length, modes, True)
    factor = np.float32(1.0 / math.sqrt(length))
    cosines = np.cos(radians) * factor
    sines = np.sin(radians) * factor
    forward = np.stack(
        [np.stack([cosines, -sines], axis=1), np.stack([sines, cosines], axis=1)], axis=0
    )
    inverse = np.stack(
        [np.stack([cosines.T, sines.T], axis=1), np.stack([-sines.T, cosines.T], axis=1)], axis=0
    )
    return forward.astype(BF16), inverse.astype(BF16)


def real_tables(length, modes):
    radians = angles(length, modes, False)
    factor = np.float32(1.0 / math.sqrt(length))
    cosines = np.cos(radians) * factor
    sines = np.sin(radians) * factor
    forward = np.concatenate([cosines, -sines], axis=1)
    doubled = np.where(np.arange(modes) == 0, 1.0, 2.0).astype(np.float32)[None, :]
    inverse = np.concatenate([(cosines * doubled).T, (-sines * doubled).T], axis=0)
    return forward.astype(BF16), inverse.astype(BF16)


def flipped(table):
    return np.transpose(table, (2, 3, 0, 1))


def second_natural(table):
    length = table.shape[1]
    split = table.reshape(2, length, 2, MY // 4, 4)
    return split.transpose(3, 2, 4, 0, 1).reshape(2 * MY, 2 * length)


def second_paired(table):
    length = table.shape[1]
    split = table.reshape(2, length // 2, 2, 2, MY // 4, 4)
    return split.transpose(2, 4, 3, 5, 0, 1).reshape(4 * MY, length)


def second_inverse(table):
    length = table.shape[3]
    split = table.reshape(2, MY // 4, 4, 2, length // 2, 2)
    return split.transpose(3, 4, 5, 1, 0, 2).reshape(length, 4 * MY)


def first_forward(table):
    length, modes = table.shape[1], table.shape[3]
    split = table.reshape(2, length // 2, 2, 2, modes)
    return split.transpose(2, 3, 4, 0, 1).reshape(4 * modes, length)


def first_inverse(table):
    modes, length = table.shape[1], table.shape[3]
    split = table.reshape(2, modes, 2, length // 2, 2)
    return split.transpose(2, 3, 4, 0, 1).reshape(length, 4 * modes)


def twice_diagonal(table):
    zero = np.zeros_like(table)
    return np.block([[table, zero], [zero, table]])


def mm(left, right):
    return lax.dot_general(left, right, (((1,), (0,)), ((), ())), preferred_element_type=F32)


def nt(left, right):
    return lax.dot_general(left, right, (((1,), (1,)), ((), ())), preferred_element_type=F32)


def tn(left, right):
    return lax.dot_general(left, right, (((0,), (0,)), ((), ())), preferred_element_type=F32)


def side(rows):
    return lax.broadcasted_iota(jnp.int32, (rows, LANES), 1) < LANES // 2


def turned(values):
    return pltpu.roll(values, LANES // 2, 1)


def whole(shape):
    return pl.BlockSpec(shape, lambda *_: (0,) * len(shape))


VM = pl.BlockSpec(memory_space=pltpu.VMEM)


GROUPS = 4
ROWS = 2 * LANES * CHANNELS


def near(value):
    return pltpu.with_memory_space_constraint(value, pltpu.VMEM)


def afar(value):
    return pltpu.with_memory_space_constraint(value, pltpu.HBM)


def call(
    kernel, outs, scratch, flops, moved, *operands, big=(), kinds=(), plain=(), token=None, reach=False
):
    cut = ROWS // GROUPS
    extra = [] if token is None else list(token) if isinstance(token, list) else [token]
    counts = [
        len(operands),
        len(big),
        len(extra),
        len(outs),
        len(kinds),
        len(plain),
        len(scratch),
        len(outs),
        len(big),
        len(kinds),
        3,
    ]

    def whole_kernel(*refs):
        parts = []
        at = 0
        for count in counts:
            parts.append(refs[at : at + count])
            at += count
        small, big_far, tokens, outs_far, kinds_far, plains, own, outs_near, big_near, kinds_near, sems = parts
        in_sem, out_sem, end_sem = sems

        def group_of(far, close, sem, index, group, out):
            rows = pl.ds(pl.multiple_of(group * cut, cut), cut)
            pair = (close.at[rows], far.at[rows]) if out else (far.at[rows], close.at[rows])
            return pltpu.make_async_copy(*pair, sem.at[index, group])

        def coming(index, group):
            return group_of(big_far[index], big_near[index], in_sem, index, group, False)

        def going(index, group):
            return group_of(kinds_far[index], kinds_near[index], out_sem, index, group, True)

        for group in range(GROUPS):
            for index in range(len(big)):
                coming(index, group).start()

        def loop(body, carry=0, unroll=PAIRS // GROUPS):
            per = PAIRS // GROUPS

            def some(i, carry):
                for j in range(unroll):
                    carry = body(i * unroll + j, carry)
                return carry

            def each(group, carry):
                for index in range(len(big)):
                    coming(index, group).wait()
                first = group * (per // unroll)
                carry = lax.fori_loop(first, first + per // unroll, some, carry)
                for index in range(len(kinds)):
                    going(index, group).start()
                return carry

            return lax.fori_loop(0, GROUPS, each, carry)

        kernel(small + tokens if reach else small, big_near, outs_near, kinds_near, plains, own, loop)
        last = [
            pltpu.make_async_copy(close, far, end_sem.at[index])
            for index, (close, far) in enumerate(zip(outs_near, outs_far))
        ]
        for copy in last:
            copy.start()
        for index in range(len(kinds)):
            for group in range(GROUPS):
                going(index, group).wait()
        for copy in last:
            copy.wait()

    operands = [near(operand) for operand in operands]
    far = pl.BlockSpec(memory_space=pl.ANY)
    shapes = [pltpu.HBM(shape, kind) for shape, kind in outs]
    shapes += [pltpu.HBM((ROWS, LANES), kind) for kind in kinds]
    return pl.pallas_call(
        whole_kernel,
        out_shape=shapes + list(plain),
        in_specs=[VM] * len(operands) + [far] * (len(big) + len(extra)),
        out_specs=[far] * len(shapes) + [VM] * len(plain),
        scratch_shapes=list(scratch)
        + [pltpu.VMEM(shape, kind) for shape, kind in outs]
        + [pltpu.VMEM((ROWS, LANES), array.dtype) for array in big]
        + [pltpu.VMEM((ROWS, LANES), kind) for kind in kinds]
        + [
            pltpu.SemaphoreType.DMA((max(len(big), 1), GROUPS)),
            pltpu.SemaphoreType.DMA((max(len(kinds), 1), GROUPS)),
            pltpu.SemaphoreType.DMA((max(len(outs), 1),)),
        ],
        cost_estimate=pl.CostEstimate(flops=flops, bytes_accessed=moved, transcendentals=0),
        compiler_params=pltpu.CompilerParams(vmem_limit_bytes=VMEM_LIMIT),
    )(*operands, *[afar(array) for array in (*big, *extra)])


C_STEP = 8


def spectrum_kernel(field, third_far, second_far, out_far, near_field, third_ref, second_ref, chunk, spec, sems, extra):
    def coming(step):
        cut = pl.ds(step * C_STEP, C_STEP)
        return pltpu.make_async_copy(field.at[0, cut], near_field.at[cut], sems.at[step])

    tables = [
        pltpu.make_async_copy(third_far, third_ref, extra.at[0]),
        pltpu.make_async_copy(second_far, second_ref, extra.at[1]),
    ]
    for copy in tables:
        copy.start()
    for step in range(CHANNELS // C_STEP):
        coming(step).start()
    for copy in tables:
        copy.wait()
    third = third_ref[...]

    def some(step, carry):
        coming(step).wait()
        for x in range(2):
            rows = near_field[pl.ds(step * C_STEP, C_STEP), x].reshape(C_STEP * LANES, LANES)
            done = nt(third, rows)
            for c in range(C_STEP):
                place = pl.multiple_of((x * CHANNELS + step * C_STEP + c) * 2 * MZ, 2 * MZ)
                spec[pl.ds(place, 2 * MZ), :] = done[:, c * LANES : (c + 1) * LANES]
        return carry

    lax.fori_loop(0, CHANNELS // C_STEP, some, 0)
    second = second_ref[...]
    for k in range(MZ):
        real = spec[pl.ds(k, LANES, stride=2 * MZ), :]
        imag = spec[pl.ds(MZ + k, LANES, stride=2 * MZ), :]
        both = jnp.concatenate([real, imag], axis=1).astype(BF16)
        chunk[k * 32 : (k + 1) * 32, :] = nt(second, both).astype(BF16)
    out = pltpu.make_async_copy(chunk, out_far, extra.at[2])
    out.start()
    out.wait()


def first_partial(field, third, second):
    far = pl.BlockSpec(memory_space=pl.ANY)
    return pl.pallas_call(
        spectrum_kernel,
        out_shape=pltpu.HBM((512, LANES), BF16),
        in_specs=[far] * 3,
        out_specs=far,
        scratch_shapes=[
            pltpu.VMEM(field.shape[1:], BF16),
            pltpu.VMEM(third.shape, BF16),
            pltpu.VMEM(second.shape, BF16),
            pltpu.VMEM((512, LANES), BF16),
            pltpu.VMEM((4096, LANES), F32),
            pltpu.SemaphoreType.DMA((CHANNELS // C_STEP,)),
            pltpu.SemaphoreType.DMA((3,)),
        ],
        cost_estimate=pl.CostEstimate(
            flops=600_000_000, bytes_accessed=6 << 20, transcendentals=0
        ),
        compiler_params=pltpu.CompilerParams(vmem_limit_bytes=VMEM_LIMIT),
    )(afar(field), afar(third), afar(second))


Y_STEP = 16
Y_STEPS = LANES // Y_STEP
Y_ROWS = Y_STEP * CHANNELS


def relay_kernel(field, _, out_far, near_field, out_near, rows_ref, in_sem, out_sem):
    def coming(step):
        x = step // Y_STEPS
        cut = pl.ds(pl.multiple_of((step % Y_STEPS) * Y_STEP, Y_STEP), Y_STEP)
        return pltpu.make_async_copy(
            field.at[0, :, x, cut], near_field.at[:, x, cut], in_sem.at[step]
        )

    def going(step):
        cut = pl.ds(pl.multiple_of(step * Y_ROWS, Y_ROWS), Y_ROWS)
        return pltpu.make_async_copy(out_near.at[cut], out_far.at[cut], out_sem.at[step])

    for step in range(2 * Y_STEPS):
        coming(step).start()

    def some(step, carry):
        coming(step).wait()
        at = pl.multiple_of((step % Y_STEPS) * Y_STEP, Y_STEP)
        rows_ref[...] = (
            near_field[:, step // Y_STEPS, pl.ds(at, Y_STEP), :].astype(F32).reshape(Y_ROWS, LANES)
        )
        for y in range(0, Y_STEP, 2):
            pair = [rows_ref[pl.ds(y + e, CHANNELS, stride=Y_STEP), :] for e in range(2)]
            tile = step * (Y_STEP // 2) + y // 2
            out_near[tile_at(tile), :] = jnp.concatenate(pair, axis=0).astype(BF16)
        going(step).start()
        return carry

    lax.fori_loop(0, 2 * Y_STEPS, some, 0)
    for step in range(2 * Y_STEPS):
        going(step).wait()


def relay(field, token):
    far = pl.BlockSpec(memory_space=pl.ANY)
    return pl.pallas_call(
        relay_kernel,
        out_shape=pltpu.HBM((ROWS, LANES), BF16),
        in_specs=[far] * 2,
        out_specs=far,
        scratch_shapes=[
            pltpu.VMEM(field.shape[1:], BF16),
            pltpu.VMEM((ROWS, LANES), BF16),
            pltpu.VMEM((Y_ROWS, LANES), F32),
            pltpu.SemaphoreType.DMA((2 * Y_STEPS,)),
            pltpu.SemaphoreType.DMA((2 * Y_STEPS,)),
        ],
        cost_estimate=pl.CostEstimate(
            flops=600_000_000, bytes_accessed=12 << 20, transcendentals=0
        ),
        compiler_params=pltpu.CompilerParams(vmem_limit_bytes=VMEM_LIMIT),
    )(afar(field), afar(token))


def own_spectrum(wide, table, place, block=8):
    real = wide[pl.ds(place, 64, stride=block), :]
    imag = wide[pl.ds(4 + place, 64, stride=block), :]
    both = mm(table, jnp.concatenate([real, imag], axis=0).astype(BF16))
    return both[:32, :CHANNELS] + both[32:, CHANNELS:]


def send_field(mixed, table, place, sent, block=8):
    twin = jnp.concatenate([mixed, mixed], axis=1)
    left = side(32)
    both = jnp.concatenate([jnp.where(left, twin, 0.0), jnp.where(left, 0.0, twin)], axis=0)
    out = mm(table, both.astype(BF16))
    sent[pl.ds(place, 64, stride=block), :] = out[:64]
    sent[pl.ds(4 + place, 64, stride=block), :] = out[64:]


def mode_lanes(modes):
    row = lax.broadcasted_iota(jnp.int32, (32, LANES), 0) % modes
    half = lax.broadcasted_iota(jnp.int32, (32, LANES), 1) // CHANNELS
    return row, half


def mix_kernel(small, _, outs, __, ___, scratch, loop):
    got_ref, weight_ref, forward_ref, inverse_ref = small
    out_ref, spec_ref = outs
    wide, sent = scratch
    wide[...] = got_ref[...].astype(F32)
    forward = forward_ref[...]
    inverse = inverse_ref[...]
    modes = weight_ref.shape[1]
    row, half = mode_lanes(modes)
    for p in range(4):
        spec = own_spectrum(wide, forward, p).astype(BF16)
        spec_ref[:, p * CHANNELS : (p + 1) * CHANNELS] = spec
        spec = spec.astype(F32)
        other = jnp.concatenate([-spec[modes:], spec[:modes]], axis=0)
        pieces = []
        for part in (spec, other):
            twin = jnp.concatenate([part, part], axis=1)
            for pair in range(modes // 2):
                pieces.append(jnp.where(row == 2 * pair + half, twin, 0.0).astype(BF16))
        spread = jnp.concatenate(pieces, axis=1)
        weights = weight_ref[:, :, p].reshape(2 * modes * CHANNELS, CHANNELS)
        mixed = mm(spread, weights).astype(BF16).astype(F32)
        send_field(mixed, inverse, p, sent)
    out_ref[...] = sent[...].astype(BF16)


def high_low(values):
    high = values.astype(BF16).astype(F32)
    return jnp.concatenate([high, values - high], axis=1)


def unmix_kernel(small, _, outs, __, ___, scratch, loop):
    got_ref, weight_ref, forward_ref, inverse_ref, one_ref, two_ref, term_far = small
    out_ref, spec_ref = outs
    wide, sent, term_ref, term_sem = scratch
    fetch = pltpu.make_async_copy(term_far, term_ref, term_sem.at[0])
    fetch.start()
    wide[...] = got_ref[...].astype(F32)
    forward = forward_ref[...]
    inverse = inverse_ref[...]
    modes = weight_ref.shape[1]
    row, half = mode_lanes(modes)
    spec_ref[0:32, :] = one_ref[...]
    spec_ref[32:64, :] = two_ref[...]
    sent[...] = jnp.zeros_like(sent)
    for p in range(4):
        spec = own_spectrum(wide, forward, p).astype(BF16)
        spec_ref[64:96, p * CHANNELS : (p + 1) * CHANNELS] = spec
        other = jnp.concatenate([spec[modes:].astype(F32), -spec[:modes].astype(F32)], axis=0)
        products = nt(spec, weight_ref[0, :, p].reshape(modes * CHANNELS, CHANNELS)) + nt(
            other.astype(BF16), weight_ref[1, :, p].reshape(modes * CHANNELS, CHANNELS)
        )
        total = jnp.zeros((32, LANES), F32)
        for pair in range(modes // 2):
            piece = products[:, pair * LANES : (pair + 1) * LANES]
            total = total + jnp.where(row == 2 * pair + half, piece, 0.0)
        mixed = (total + turned(total))[:, :CHANNELS].astype(BF16).astype(F32)
        send_field(mixed, inverse, p, sent, 16)
    fetch.wait()
    terms = high_low(term_ref[...])
    sent[pl.ds(8, 64, stride=16), :] = terms[:CHANNELS]
    sent[pl.ds(9, 64, stride=16), :] = jnp.broadcast_to(
        terms[CHANNELS : CHANNELS + 1], (CHANNELS, LANES)
    )
    out_ref[...] = sent[...].astype(BF16)


def last_kernel(small, _, outs, __, ___, scratch, loop):
    got_ref, forward_ref = small
    (out_ref,) = outs
    (wide,) = scratch
    for d in range(64):
        wide[d * 48 : (d + 1) * 48, :] = got_ref[d * 48 : (d + 1) * 48, :].astype(F32)
    forward = forward_ref[...]
    for p in range(4):
        out_ref[0:32, p * CHANNELS : (p + 1) * CHANNELS] = own_spectrum(
            wide, forward, p, 48
        ).astype(BF16)
    total = jnp.zeros((40, LANES), F32)
    for d in range(64):
        total = total + wide[d * 48 + 8 : (d + 1) * 48, :]
    high = total.astype(BF16)
    low = (total - high.astype(F32)).astype(BF16)
    out_ref[32:64, :] = jnp.concatenate([high[:32], low[:32]], axis=1)
    rows = wide[pl.ds(41, 64, stride=48), :]
    out_ref[64:96, :] = jnp.concatenate([rows[:32], rows[32:]], axis=1).astype(BF16)
    biases = jnp.concatenate(
        [
            high_low(total[32:40, :CHANNELS]),
            jnp.broadcast_to(wide[42:43, :], (8, LANES)),
        ],
        axis=1,
    )
    out_ref[96:112, :] = jnp.concatenate([biases, biases], axis=0).astype(BF16)


CHUNK = ((512, LANES), BF16)
SPECTRUM = ((32, 4 * CHANNELS), BF16)
WIDE = pltpu.VMEM((512, LANES), F32)


def mixing(got, weights, forward, inverse, token):
    return call(
        mix_kernel,
        [CHUNK, SPECTRUM],
        [WIDE, WIDE],
        200_000_000,
        3 << 20,
        got,
        weights,
        forward,
        inverse,
        token=token,
    )


def outer_products(spec, grad, out_ref):
    modes = out_ref.shape[1]
    depth = spec.shape[0]
    lane = lax.broadcasted_iota(jnp.int32, (CHANNELS, depth), 1) % modes
    other = []
    for n in range(depth // (2 * modes)):
        at = n * 2 * modes
        other += [grad[at + modes : at + 2 * modes], -grad[at : at + modes]]
    other = jnp.concatenate(other, axis=0)
    for p in range(4):
        cut = slice(p * CHANNELS, (p + 1) * CHANNELS)
        both = jnp.concatenate([grad[:, cut], other[:, cut]], axis=1).astype(BF16)
        tall = spec[:, cut].T
        for m in range(modes):
            out = mm(jnp.where(lane == m, tall, 0.0).astype(BF16), both).astype(BF16)
            out_ref[0, m, p] = out[:, :CHANNELS]
            out_ref[1, m, p] = out[:, CHANNELS:]


def rows_of(ref, step, at):
    count = ref.shape[0] // step
    return jnp.concatenate(
        [ref[n * step + at : n * step + at + 32, :] for n in range(count)], axis=0
    ).astype(F32)


def in_order(index, parts, ordered, sems):
    rows = parts[0].shape[0]
    copies = []
    for k, part in enumerate(parts):
        at = pl.multiple_of((index ^ k) * rows, 16)
        copies.append(pltpu.make_async_copy(part, ordered.at[pl.ds(at, rows)], sems.at[k]))
    for copy in copies:
        copy.start()
    return copies


def weight_two_kernel(index_ref, *refs):
    early, _, out_ref, ordered, sems = refs[:4], refs[4], refs[5], refs[6], refs[7]
    for copy in in_order(index_ref[0], early, ordered, sems):
        copy.wait()
    outer_products(rows_of(ordered, 96, 32), rows_of(ordered, 96, 64), out_ref)


def weight_one_kernel(factor, index_ref, *refs):
    early, late = refs[:4], refs[4:8]
    out_ref, one_ref, two_ref, bias_one_ref, bias_two_ref = refs[9:14]
    early_all, late_all, early_sems, late_sems = refs[14:]
    copies = in_order(index_ref[0], early, early_all, early_sems)
    copies += in_order(index_ref[0], late, late_all, late_sems)
    for copy in copies:
        copy.wait()
    sums = late_all[32:112, :].astype(F32)
    for n in range(1, 4):
        sums = sums + late_all[n * 112 + 32 : (n + 1) * 112, :].astype(F32)
    sums = sums * factor
    one = sums[:32, :LANES] + sums[:32, LANES:]
    one_ref[0:32, :] = one[:, :CHANNELS]
    one_ref[32:64, :] = one[:, CHANNELS:]
    two = jnp.concatenate([sums[32:64, :LANES], sums[32:64, LANES:]], axis=0)
    two_ref[...] = (two + turned(two))[:, :CHANNELS]
    bias = jnp.concatenate([sums[64:72, :LANES], sums[64:72, LANES:]], axis=0)
    bias = bias + turned(bias)
    bias_one_ref[...] = bias[0:1, :CHANNELS]
    bias_two_ref[...] = bias[8:9, :CHANNELS]
    outer_products(rows_of(early_all, 96, 0), rows_of(late_all, 112, 0), out_ref)


def weight_call(kernel, outs, index, early, late, token):
    parts = [afar(part) for part in early + late[:1]] + [near(part) for part in late[1:]]
    groups = [early, late] if late else [early]
    far = pl.BlockSpec(memory_space=pl.ANY)
    return pl.pallas_call(
        kernel,
        out_shape=outs,
        in_specs=[pl.BlockSpec(memory_space=pltpu.SMEM)] + [far] * len(early + late[:1]) + [VM] * len(late[1:]) + [far],
        out_specs=[VM] * len(outs),
        scratch_shapes=[
            pltpu.VMEM((4 * group[0].shape[0], 4 * CHANNELS), BF16) for group in groups
        ]
        + [pltpu.SemaphoreType.DMA((4,)) for _ in groups],
        cost_estimate=pl.CostEstimate(
            flops=200_000_000, bytes_accessed=3 << 20, transcendentals=0
        ),
        compiler_params=pltpu.CompilerParams(vmem_limit_bytes=VMEM_LIMIT),
    )(index, *parts, afar(token))


TILES = 128
PAIRS = TILES // 2
TILE = 2 * CHANNELS


def unpack_modes(got_ref, second_ref, depth, block=8):
    second = second_ref[...]
    left = side(32)
    for k in range(MZ):
        near = jnp.concatenate(
            [got_ref[d * block : d * block + 8, :] for d in range(k * 4, k * 4 + 4)], axis=0
        ) if block > 8 else got_ref[k * 32 : (k + 1) * 32, :].astype(F32)
        far = turned(near)
        top = jnp.concatenate([jnp.where(left, near, 0.0), jnp.where(left, far, 0.0)], axis=1)
        low = jnp.concatenate([jnp.where(left, 0.0, far), jnp.where(left, 0.0, near)], axis=1)
        out = mm(second, jnp.concatenate([top, low], axis=0).astype(BF16))
        for x in range(2):
            cut = slice(x * LANES, (x + 1) * LANES)
            depth[pl.ds(x * 2048 + k, 64, stride=32), :] = out[:64, cut]
            depth[pl.ds(x * 2048 + MZ + k, 64, stride=32), :] = out[64:, cut]


def pack_modes(spec, second_ref, out_ref, block=8):
    second = second_ref[...]
    left = side(32)
    for k in range(MZ):
        planes = [
            jnp.concatenate(
                [
                    spec[pl.ds(x * 2048 + k, 64, stride=32), :],
                    spec[pl.ds(x * 2048 + MZ + k, 64, stride=32), :],
                ],
                axis=0,
            )
            for x in range(2)
        ]
        out = mm(second, jnp.concatenate(planes, axis=1).astype(BF16))
        near, far = out[:, :LANES], out[:, LANES:]
        packed = jnp.where(left, near[:32] + turned(near[32:]), turned(far[:32]) + far[32:])
        if block == 8:
            out_ref[k * 32 : (k + 1) * 32, :] = packed.astype(out_ref.dtype)
        else:
            for d in range(4):
                at = (k * 4 + d) * block
                out_ref[at : at + 8, :] = packed[d * 8 : (d + 1) * 8]


def branch_of(depth, third, pair):
    at = pl.multiple_of(pair * 64, 64)
    wide = tn(depth[pl.ds(at, 64), :].astype(BF16), third)
    return wide[:, :LANES], wide[:, LANES:]


def store_spectrum(spec, third, pair, first, second):
    done = nt(third, jnp.concatenate([first, second], axis=0))
    at = pl.multiple_of(pair * 64, 64)
    spec[pl.ds(at, 32), :] = done[:, :LANES]
    spec[pl.ds(at + 32, 32), :] = done[:, LANES:]


def tile_at(tile):
    return pl.ds(pl.multiple_of(tile * TILE, TILE), TILE)


def gelu(preact):
    inner = preact * (ROOT + (ROOT * CUBIC) * (preact * preact))
    halved = 0.5 * preact
    return halved + halved * jnp.tanh(inner)


def gelu_slope(preact):
    square = preact * preact
    tangent = jnp.tanh(preact * (ROOT + (ROOT * CUBIC) * square))
    steep = (0.5 * preact) * (ROOT + (3.0 * ROOT * CUBIC) * square)
    return 0.5 + 0.5 * tangent + steep * (1.0 - tangent * tangent)


def hidden_kernel(small, big, outs, kinds, _, scratch, loop):
    got, inv2, inv3, fwd3, fwd2 = small
    (base,) = big
    hidden, preact = kinds
    depth, spec = scratch
    unpack_modes(got, inv2, depth)
    third_back = inv3[...]
    third = fwd3[...]

    def body(pair, carry):
        made = []
        for e, branch in enumerate(branch_of(depth, third_back, pair)):
            at = tile_at(2 * pair + e)
            pre = base[at, :].astype(F32) + branch
            preact[at, :] = pre.astype(BF16)
            value = gelu(pre).astype(BF16)
            hidden[at, :] = value
            made.append(value)
        store_spectrum(spec, third, pair, *made)
        return carry

    loop(body)
    pack_modes(spec, fwd2, outs[0])


def grad_two_kernel(small, big, outs, kinds, _, scratch, loop):
    got, inv2, inv3, fwd3, fwd2 = small
    base, cot = big
    (grad,) = kinds
    depth, spec = scratch
    unpack_modes(got, inv2, depth)
    third_back = inv3[...]
    third = fwd3[...]

    def body(pair, carry):
        made = []
        for e, branch in enumerate(branch_of(depth, third_back, pair)):
            at = tile_at(2 * pair + e)
            slope = gelu_slope(base[at, :].astype(F32) + branch)
            value = (cot[at, :].astype(F32) * slope).astype(BF16)
            grad[at, :] = value
            made.append(value)
        store_spectrum(spec, third, pair, *made)
        return carry

    loop(body)
    pack_modes(spec, fwd2, outs[0])


def grad_one_kernel(small, big, outs, _, __, scratch, loop):
    got, inv2, inv3, fwd3, fwd2 = small
    base, slope, values = big
    (out,) = outs
    depth, spec, wide, sent = scratch
    wide[...] = got[...].astype(F32)
    unpack_modes(wide, inv2, depth, 16)
    third_back = inv3[...]
    third = fwd3[...]
    ones = jnp.ones((16, 4 * LANES), BF16)

    def body(pair, total):
        made = []
        for e, branch in enumerate(branch_of(depth, third_back, pair)):
            at = tile_at(2 * pair + e)
            back = base[at, :].astype(F32) + branch
            made.append((back * slope[at, :].astype(F32)).astype(BF16))
        store_spectrum(spec, third, pair, *made)
        left = jnp.concatenate(
            [wide_tile(values, 2 * pair), wide_tile(values, 2 * pair + 1)], axis=1
        )
        right = jnp.concatenate(
            [part for tile in made for part in (tile[:CHANNELS], tile[CHANNELS:])], axis=1
        )
        return total + nt(jnp.concatenate([left, ones], axis=0), right)

    total = loop(body, jnp.zeros((CHANNELS + 16, CHANNELS), F32))
    pack_modes(spec, fwd2, sent, 48)
    left = side(1)

    def arrived_sum(place):
        row = jnp.sum(wide[pl.ds(place, 64, stride=16), :], axis=0, keepdims=True)
        row = row + turned(row)
        high = row.astype(BF16).astype(F32)
        return jnp.where(left, high, row - high)

    bias = jnp.concatenate([total[64:65], total[64:65]], axis=1)
    terms = jnp.concatenate(
        [
            jnp.concatenate([total[:32], total[32:64]], axis=1),
            bias,
            arrived_sum(8),
            arrived_sum(9),
            jnp.zeros((5, LANES), F32),
        ],
        axis=0,
    )
    for d in range(64):
        block = jnp.concatenate([sent[d * 48 : d * 48 + 8, :], terms], axis=0)
        out[d * 48 : (d + 1) * 48, :] = block.astype(BF16)


def planes(kernel, kinds, *operands, big, token):
    scratch = [pltpu.VMEM((4096, LANES), F32), pltpu.VMEM((4096, LANES), F32)]
    return call(
        kernel,
        [CHUNK],
        scratch,
        1_000_000_000,
        20 << 20,
        *operands,
        big=big,
        kinds=kinds,
        token=token,
    )


def wide_tile(ref, tile):
    at = pl.multiple_of(tile * TILE, TILE)
    return jnp.concatenate(
        [ref[pl.ds(at, CHANNELS), :], ref[pl.ds(at + CHANNELS, CHANNELS), :]], axis=1
    )


def store_wide(ref, tile, wide):
    at = pl.multiple_of(tile * TILE, TILE)
    ref[pl.ds(at, CHANNELS), :] = wide[:, :LANES].astype(BF16)
    ref[pl.ds(at + CHANNELS, CHANNELS), :] = wide[:, LANES:].astype(BF16)


def point_kernel(small, big, _, kinds, __, scratch, loop):
    point, bias = small
    weights = point[...]
    shift = jnp.concatenate([bias[...], bias[...]], axis=1)

    def body(pair, carry):
        for tile in (2 * pair, 2 * pair + 1):
            store_wide(kinds[0], tile, mm(weights, wide_tile(big[0], tile)) + shift)
        return carry

    loop(body)


def slope_kernel(small, big, _, kinds, __, scratch, loop):
    def body(pair, carry):
        for tile in (2 * pair, 2 * pair + 1):
            at = tile_at(tile)
            kinds[0][at, :] = gelu_slope(big[0][at, :].astype(F32)).astype(BF16)
        return carry

    loop(body)


def point_back_kernel(small, big, outs, kinds, _, scratch, loop):
    weights = small[0][...]
    hidden, grad = big
    ones = jnp.ones((16, 4 * LANES), BF16)

    def body(pair, total):
        right = [wide_tile(grad, 2 * pair + e) for e in range(2)]
        for e in range(2):
            store_wide(kinds[0], 2 * pair + e, mm(weights, right[e]))
        left = jnp.concatenate(
            [wide_tile(hidden, 2 * pair), wide_tile(hidden, 2 * pair + 1)], axis=1
        )
        return total + nt(
            jnp.concatenate([left, ones], axis=0), jnp.concatenate(right, axis=1)
        )

    outs[0][...] = loop(body, jnp.zeros((CHANNELS + 16, CHANNELS), F32))


def body(field_in, cotangent, spectral_one, spectral_two, point_one, point_two, bias_one, bias_two):
    forward_c, inverse_c = complex_tables(LANES, MY)
    forward_z, inverse_z = real_tables(LANES, MZ)
    shape = spectral_one.shape
    const = lambda table: jnp.asarray(np.ascontiguousarray(table))

    natural_second = const(second_natural(forward_c))
    third_forward = const(forward_z.T)
    third_adjoint = const(inverse_z)
    third_inverse = const(twice_diagonal(inverse_z))
    third_back = const(twice_diagonal(forward_z.T))
    second_fwd = const(second_paired(forward_c))
    second_adj = const(second_paired(flipped(inverse_c)))
    second_inv = const(second_inverse(inverse_c))
    second_back = const(second_inverse(flipped(forward_c)))
    first_fwd = const(first_forward(forward_c))
    first_adj = const(first_forward(flipped(inverse_c)))
    first_inv = const(first_inverse(inverse_c))
    first_back = const(first_inverse(flipped(forward_c)))

    def exchange(chunk):
        return lax.all_to_all(chunk, "space", split_axis=0, concat_axis=0, tiled=True)

    def point_map(values, point, bias, token):
        return call(
            point_kernel,
            [],
            [],
            500_000_000,
            12 << 20,
            point.T,
            spread(bias),
            big=[values],
            kinds=[BF16],
            token=token,
        )[0]

    def samples(spectrum):
        size = 4
        return [spectrum] + [
            lax.ppermute(spectrum, "dp", [(i, i ^ k) for i in range(size)])
            for k in range(1, size)
        ]

    spread = lambda bias: jnp.broadcast_to(bias[:, None], (CHANNELS, LANES))

    chunk = first_partial(field_in, third_forward, natural_second)
    got = exchange(chunk)
    values = relay(field_in, chunk)

    chunk, spec_one = mixing(got, spectral_one, first_fwd, first_inv, token=values)
    got = exchange(chunk)
    base = point_map(values, point_one, bias_one, chunk)

    chunk, hidden, preact = planes(
        hidden_kernel,
        [BF16, BF16],
        got,
        second_inv,
        third_inverse,
        third_forward,
        second_fwd,
        big=[base],
        token=spec_one,
    )
    got = exchange(chunk)
    base = point_map(hidden, point_two, bias_two, chunk)

    chunk, spec_two = mixing(got, spectral_two, first_fwd, first_inv, token=base)
    got = exchange(chunk)
    cot = relay(cotangent, chunk)

    chunk, grad_two = planes(
        grad_two_kernel,
        [BF16],
        got,
        second_inv,
        third_inverse,
        third_adjoint,
        second_adj,
        big=[base, cot],
        token=spec_two,
    )
    got = exchange(chunk)
    term_two, base = call(
        point_back_kernel,
        [((CHANNELS + 16, CHANNELS), F32)],
        [],
        1_000_000_000,
        12 << 20,
        point_two,
        big=[hidden, grad_two],
        kinds=[BF16],
    )

    chunk, early = call(
        unmix_kernel,
        [((1024, LANES), BF16), ((96, 4 * CHANNELS), BF16)],
        [
            WIDE,
            pltpu.VMEM((1024, LANES), F32),
            pltpu.VMEM((CHANNELS + 16, CHANNELS), F32),
            pltpu.SemaphoreType.DMA((1,)),
        ],
        200_000_000,
        3 << 20,
        got,
        spectral_two,
        first_adj,
        first_back,
        spec_one,
        spec_two,
        token=term_two,
        reach=True,
    )
    got = exchange(chunk)
    early = samples(early)
    slope = call(
        slope_kernel, [], [], 500_000_000, 12 << 20, big=[preact], kinds=[BF16], token=chunk
    )[0]

    chunk = call(
        grad_one_kernel,
        [((3072, LANES), BF16)],
        [
            pltpu.VMEM((4096, LANES), F32),
            pltpu.VMEM((4096, LANES), F32),
            pltpu.VMEM((1024, LANES), F32),
            pltpu.VMEM((3072, LANES), F32),
        ],
        1_500_000_000,
        20 << 20,
        got,
        second_back,
        third_back,
        third_adjoint,
        second_adj,
        big=[base, slope, values],
        token=early[1:],
    )[0]
    got = exchange(chunk)
    late = call(
        last_kernel,
        [((112, 4 * CHANNELS), BF16)],
        [pltpu.VMEM((3072, LANES), F32)],
        50_000_000,
        1 << 20,
        got,
        first_adj,
    )[0]
    index = lax.axis_index("dp").astype(jnp.int32).reshape(1)
    weights = jax.ShapeDtypeStruct(shape, BF16)
    spectral_grad_two = weight_call(weight_two_kernel, [weights], index, early, [], late)[0]
    late = samples(late)
    cells = lax.axis_size("dp") * lax.axis_size("space") * 2 * LANES * LANES
    square = jax.ShapeDtypeStruct((CHANNELS, CHANNELS), F32)
    line = jax.ShapeDtypeStruct((1, CHANNELS), F32)
    spectral_grad_one, point_grad_one, point_grad_two, bias_grad_one, bias_grad_two = weight_call(
        functools.partial(weight_one_kernel, 1.0 / math.sqrt(cells)),
        [weights, square, square, line, line],
        index,
        early,
        late,
        spectral_grad_two,
    )
    return (
        spectral_grad_one,
        spectral_grad_two,
        point_grad_one,
        point_grad_two,
        bias_grad_one.reshape(CHANNELS),
        bias_grad_two.reshape(CHANNELS),
    )


def solution(mesh):
    field = P("dp", None, "space", None, None)
    modes = P(None, None, "space", None, None)
    return jax.shard_map(
        body,
        mesh=mesh,
        in_specs=(field, field, modes, modes, P(), P(), P(), P()),
        out_specs=(modes, modes, P(), P(), P(), P()),
        check_vma=False,
    )
```
